32 devices in a mesh: section: 2 (over x), dec: 4 (over z), row: 4 (over y, core).
Axes of the slice: x: 2, y: 2, z: 4, core: 2. Of those that a mesh axis runs over, the one named last changes fastest.
Arguments:
- hidden: bfloat16 [8, 4, 16, 8, 5120], P('dec', None, 'row', None, 'section'), may hold values from -12 to 12
- head_weight: bfloat16 [5120, 64], P('section'), may hold values from -0.078125 to 0.078125
- head_bias: float32 [64], replicated, may hold values from -3 to 3
- lat_cache: bfloat16 [8, 2, 32, 16, 16], P('dec', None, 'row'), may hold values from -6 to 6
- mid_cache: bfloat16 [8, 2, 32, 16, 512], P('dec', None, 'row', None, 'section'), may hold values from -6 to 6
- moves: int32 [8], replicated, may hold values from 0 to 7, each once
- span_index: int32 [8], P('dec'), may hold values from 0 to 3
- conv_in_weight: bfloat16 [3, 3, 3, 16, 512], P(None, None, None, None, 'section'), may hold values from -0.3125 to 0.3125
- conv_in_bias: float32 [512], P('section'), may hold values from -3 to 3
- gn_gain: float32 [512], P('section'), may hold values from 0.25 to 1.75
- gn_bias: float32 [512], P('section'), may hold values from -3 to 3
- mid_weight: bfloat16 [3, 3, 3, 512, 512], P(None, None, None, None, 'section'), may hold values from -0.0546875 to 0.0546875
- mid_bias: float32 [512], P('section'), may hold values from -3 to 3
Outputs:
- decoded: bfloat16 [8, 4, 32, 16, 512], P('dec', None, 'row', None, 'section')
- new_lat_cache: bfloat16 [8, 2, 32, 16, 16], P('dec', None, 'row')
- new_mid_cache: bfloat16 [8, 2, 32, 16, 512], P('dec', None, 'row', None, 'section')
The draws below stay inside these ranges and needn't reach their ends.
Inputs may be any that keep to these rules, and one draw needn't show every extreme that they name: moves holds each of the 8 slots once.
All inputs are finite; a program needn't handle non-finite values.
Results may differ from the reference program's by a relative error of at most 0.012.
Values may be sent and summed in bfloat16 or wider, within the bound.
A program may use at most 128 MiB of HBM per device.

```python
import jax
import jax.numpy as jnp
from jax import lax

D = 5120
CZ = 16
C = 512
GROUPS = 32
F = 4
CACHE = 2
W = 16
STREAMS = 8
H = 32
HP = 16
WP = 8
PO = 64


def draw_hidden(key, part):
    shape = (STREAMS, F, HP, WP, D)
    position = jnp.arange(HP, dtype=jnp.float32) / (HP - 1)
    base = jax.random.truncated_normal(key, -6.0, 6.0, shape, jnp.float32)
    scale = jnp.exp(jnp.log(0.5) + position * jnp.log(4.0))
    return (base * scale[None, None, :, None, None]).astype(jnp.bfloat16)


def plant(drawn, key, least, largest):
    spot = [jax.random.randint(jax.random.fold_in(key, axis), (), 0, length) for axis, length in enumerate(drawn.shape)]
    main_axis = drawn.shape.index(max(drawn.shape))
    beside = spot[:main_axis] + [(spot[main_axis] + 1) % drawn.shape[main_axis]] + spot[main_axis + 1:]
    return drawn.at[tuple(spot)].set(least).at[tuple(beside)].set(largest)


def level_of(key, shape, shards, smallest, largest):
    level = 1.0
    for dim, shards_of in shards:
        heights = jax.random.uniform(jax.random.fold_in(jax.random.fold_in(key, 6), dim), (shards_of,), jnp.float32, smallest / len(shards), largest / len(shards))
        level = level * jnp.repeat(jnp.exp(heights), shape[dim] // shards_of).reshape((-1,) + (1,) * (len(shape) - 1 - dim))
    return level


def noise(rng, extent, spread, bound, split=(), kind=jnp.bfloat16):
    factor_of = level_of(rng, extent, split, -0.22, 0.18) if split else 1.0
    result = jax.random.normal(rng, extent, jnp.float32) * spread * factor_of
    return jnp.minimum(jnp.maximum(result, -bound), bound).astype(kind)


def setup_inputs(seed: int = 0) -> dict:
    arg_keys = jax.random.split(jax.random.key(seed), 14)
    hidden = draw_hidden(jax.random.fold_in(arg_keys[13], 71), 0)
    head_weight = noise(arg_keys[1], (D, PO), D ** -0.5, 0.078125, ((0, 2),))
    head_bias = noise(arg_keys[2], (PO,), 0.5, 3.0, (), jnp.float32)
    lat_cache = noise(arg_keys[3], (STREAMS, CACHE, H, W, CZ), 1.0, 6.0, ((0, 4), (2, 4)))
    mid_cache = noise(arg_keys[4], (STREAMS, CACHE, H, W, C), 1.0, 6.0, ((0, 4), (2, 4), (4, 2)))
    moves = jax.random.permutation(arg_keys[5], STREAMS).astype(jnp.int32)
    span_index = plant(jax.random.randint(arg_keys[6], (STREAMS,), 0, 4), jax.random.fold_in(arg_keys[6], 1), 0, 3).astype(jnp.int32)
    conv_in_weight = noise(arg_keys[7], (3, 3, 3, CZ, C), (27 * CZ) ** -0.5, 0.3125, ((4, 2),))
    conv_in_bias = noise(arg_keys[8], (C,), 0.5, 3.0, ((0, 2),), jnp.float32)
    gn_gain = jnp.clip(1.0 + 0.15 * jax.random.normal(arg_keys[9], (C,), jnp.float32), 0.25, 1.75)
    gn_bias = noise(arg_keys[10], (C,), 0.5, 3.0, ((0, 2),), jnp.float32)
    mid_weight = noise(arg_keys[11], (3, 3, 3, C, C), (27 * C) ** -0.5, 0.0546875, ((4, 2),))
    mid_bias = noise(arg_keys[12], (C,), 0.5, 3.0, ((0, 2),), jnp.float32)
    return dict(hidden=hidden, head_weight=head_weight, head_bias=head_bias, lat_cache=lat_cache, mid_cache=mid_cache, moves=moves, span_index=span_index, conv_in_weight=conv_in_weight, conv_in_bias=conv_in_bias, gn_gain=gn_gain, gn_bias=gn_bias, mid_weight=mid_weight, mid_bias=mid_bias)


def conv_taps(padded, weight, frames, rows, cols):
    cin = padded.shape[-1]
    total = jnp.zeros((frames * rows * cols, weight.shape[-1]), jnp.float32)
    for a in range(3):
        for b in range(3):
            for e in range(3):
                tap = padded[a:a + frames, b:b + rows, e:e + cols].reshape(-1, cin)
                total = total + jnp.dot(tap, weight[a, b, e], preferred_element_type=jnp.float32)
    return total.reshape(frames, rows, cols, -1)

def reference(hidden, head_weight, head_bias, lat_cache, mid_cache, moves, span_index, conv_in_weight, conv_in_bias, gn_gain, gn_bias, mid_weight, mid_bias):
    streams, frames, half_rows, half_cols, width = hidden.shape
    patches = jnp.dot(hidden.reshape(-1, width), head_weight, preferred_element_type=jnp.float32) + head_bias
    latent = patches.reshape(streams, frames, half_rows, half_cols, 2, 2, CZ)
    latent = latent.transpose(0, 1, 2, 4, 3, 5, 6).reshape(streams, frames, 2 * half_rows, 2 * half_cols, CZ).astype(jnp.bfloat16)
    live = (span_index > 0).astype(jnp.bfloat16)[:, None, None, None, None]
    prev_lat = jnp.take(lat_cache, moves.astype(jnp.int32), axis=0) * live
    prev_mid = jnp.take(mid_cache, moves.astype(jnp.int32), axis=0) * live

    def decode_one(items):
        lat_prev, lat_now, mid_prev = items
        x_in = jnp.concatenate([lat_prev, lat_now], 0)
        x_pad = jnp.pad(x_in, ((0, 0), (1, 1), (1, 1), (0, 0)))
        first = (conv_taps(x_pad, conv_in_weight, F, H, W) + conv_in_bias).astype(jnp.bfloat16)
        grouped = first.astype(jnp.float32).reshape(F, H, W, GROUPS, C // GROUPS)
        gmean = lax.optimization_barrier(jnp.mean(grouped, axis=(0, 1, 2, 4), keepdims=True))
        gvar = lax.optimization_barrier(jnp.mean(grouped * grouped, axis=(0, 1, 2, 4), keepdims=True)) - gmean * gmean
        scaled = ((grouped - gmean) * lax.rsqrt(gvar + 1e-05)).reshape(F, H, W, C) * gn_gain + gn_bias
        act = jax.nn.silu(scaled).astype(jnp.bfloat16)
        m_in = jnp.concatenate([mid_prev, act], 0)
        m_pad = jnp.pad(m_in, ((0, 0), (1, 1), (1, 1), (0, 0)))
        conv = conv_taps(m_pad, mid_weight, F, H, W) + mid_bias
        out = (first.astype(jnp.float32) + conv).astype(jnp.bfloat16)
        return (out, act[F - CACHE:])
    decoded, new_mid = lax.map(decode_one, (prev_lat, latent, prev_mid))
    return (decoded, latent[:, F - CACHE:], new_mid)
```

```python
import functools

import jax
import jax.numpy as jnp
from jax import lax
from jax.experimental import pallas as pl
from jax.experimental.pallas import tpu as pltpu
from jax.sharding import PartitionSpec as P

CZ = 16
GROUP = 16
MESH = pl.DeviceIdType.MESH
F32 = jnp.float32
BF16 = jnp.bfloat16


def shifted(flat, step):
    n = flat.shape[0]
    j = lax.broadcasted_iota(jnp.int32, flat.shape, 0) % 8
    if step < 0:
        return jnp.where(j == 0, 0.0, pltpu.roll(flat, 1, 0))
    return jnp.where(j == 7, 0.0, pltpu.roll(flat, n - 1, 0))


def kernel(
    n_dec,
    n_row,
    hidden,
    head_t,
    head_bias,
    lat,
    mid,
    moves,
    span,
    cw,
    cb,
    gain,
    gbias,
    midw,
    midb,
    decoded,
    new_lat,
    new_mid,
    hid_v,
    midw_v,
    part,
    part_x,
    part_h,
    lat_all,
    lat_own,
    lat_h,
    cw_all,
    par_all,
    wide,
    z,
    h1,
    stats,
    stats_in,
    gm,
    pm,
    mb,
    acc,
    local_sem,
    lat_s,
    lat_r,
    mid_s,
    mid_r,
    w_s,
    w_r,
    part_s,
    part_r,
    lh_s,
    lh_r,
    st_s,
    st_r,
    pm_s,
    pm_r,
):
    s = lax.axis_index("section")
    d = lax.axis_index("dec")
    r = lax.axis_index("row")
    o = 1 - s
    lanes = pl.ds(pl.multiple_of(s * 256, 256), 256)
    olanes = pl.ds(pl.multiple_of(o * 256, 256), 256)
    has_up = r > 0
    has_down = r < n_row - 1

    barrier = pltpu.get_barrier_semaphore()

    def greet(dev):
        pl.semaphore_signal(barrier, inc=1, device_id=dev, device_id_type=MESH)

    greet((o, d, r))
    for k in range(1, n_dec):
        greet((s, lax.rem(d + k, n_dec), r))
    for k in range(1, n_row):
        greet((s, d, lax.rem(r + k, n_row)))
        greet((o, d, lax.rem(r + k, n_row)))

    load_hidden = pltpu.make_async_copy(hidden, hid_v, local_sem.at[0])
    load_hidden.start()
    own_mid = pltpu.make_async_copy(mid, gm.at[pl.ds(2 * d, 2)], local_sem.at[1])
    own_mid.start()
    load_w = pltpu.make_async_copy(midw, midw_v, local_sem.at[2])
    load_w.start()

    pl.semaphore_wait(barrier, 1 + (n_dec - 1) + 2 * (n_row - 1))

    def remote(src, dst, ssem, rsem, dev):
        return pltpu.make_async_remote_copy(
            src_ref=src, dst_ref=dst, send_sem=ssem, recv_sem=rsem, device_id=dev, device_id_type=MESH
        )

    def lat_copy(k, origin):
        return remote(
            lat, lat_all.at[pl.ds(2 * origin, 2)], lat_s.at[k - 1], lat_r.at[k - 1],
            (s, lax.rem(d + k, n_dec), r),
        )

    def mid_copy(k, origin):
        return remote(
            mid, gm.at[pl.ds(2 * origin, 2)], mid_s.at[k - 1], mid_r.at[k - 1],
            (s, lax.rem(d + k, n_dec), r),
        )

    for k in range(1, n_dec):
        lat_copy(k, d).start()

    cw_copy = remote(cw, cw_all.at[:, :, lanes], w_s.at[0], w_r.at[0], (o, d, r))
    cw_copy.start()
    par_copies = [
        remote(ref, par_all.at[n, :, lanes], w_s.at[n + 1], w_r.at[n + 1], (o, d, r))
        for n, ref in enumerate((cb, gain, gbias))
    ]
    for c in par_copies:
        c.start()
    for k in range(1, n_dec):
        mid_copy(k, d).start()

    load_hidden.wait()
    head = lax.dot_general(
        hid_v[...], head_t[...], (((1,), (1,)), ((), ())), preferred_element_type=F32
    )
    head = head.reshape(2, 4, 4, 8, 128)
    lane = lax.broadcasted_iota(jnp.int32, (4, 8, 128), 2)
    for t in range(2):
        for st in range(2):
            high = pltpu.roll(head[st, t + 2].reshape(32, 128), 64, 1).reshape(4, 8, 128)
            part[t, :, pl.ds(8 * st, 8), :] = jnp.where(lane < 64, head[st, t], high)

    def part_copies():
        full = remote(part, part_x, part_s.at[0], part_r.at[0], (o, d, r))
        up = [
            remote(part.at[:, 0], part_h.at[1, n], part_s.at[1 + n], part_r.at[1 + n], (dev, d, r - 1))
            for n, dev in enumerate((s, o))
        ]
        down = [
            remote(part.at[:, 3], part_h.at[0, n], part_s.at[3 + n], part_r.at[3 + n], (dev, d, r + 1))
            for n, dev in enumerate((s, o))
        ]
        return full, up, down

    full, up, down = part_copies()

    @pl.when(has_up)
    def _():
        for c in up:
            c.start()

    @pl.when(has_down)
    def _():
        for c in down:
            c.start()

    full.start()

    lat_all[pl.ds(2 * d, 2)] = lat[...]
    cw_all[:, :, lanes] = cw[...]
    for n, ref in enumerate((cb, gain, gbias)):
        par_all[n, :, lanes] = ref[...]

    for k in range(1, n_dec):
        lat_copy(k, lax.rem(d + n_dec - k, n_dec)).wait_recv()
    for st in range(2):
        live = (span[st] > 0).astype(F32)
        x = lat_all[moves[2 * d + st]].astype(F32) * live
        lat_own[:, pl.ds(8 * st, 8), :] = x.reshape(4, 8, 128)
    lat_edge_up = remote(lat_own.at[0], lat_h.at[1], lh_s.at[0], lh_r.at[0], (s, d, r - 1))
    lat_edge_down = remote(lat_own.at[3], lat_h.at[0], lh_s.at[1], lh_r.at[1], (s, d, r + 1))

    @pl.when(has_up)
    def _():
        lat_edge_up.start()

    @pl.when(has_down)
    def _():
        lat_edge_down.start()

    remote(cw, cw_all.at[:, :, olanes], w_s.at[0], w_r.at[0], (o, d, r)).wait_recv()
    for n, ref in enumerate((cb, gain, gbias)):
        remote(ref, par_all.at[n, :, olanes], w_s.at[n + 1], w_r.at[n + 1], (o, d, r)).wait_recv()
    zero_slab = jnp.zeros((CZ, 512), BF16)

    def build(a, carry):
        for pp in range(2):
            for qq in range(2):
                for di in range(2):
                    for dj in range(2):
                        for p in range(2):
                            for q in range(2):
                                b = 2 * di + p - 1 + pp
                                e = 2 * dj + q - 1 + qq
                                row = di * 128 + dj * 64 + p * 32 + q * 16
                                if 0 <= b < 3 and 0 <= e < 3:
                                    slab = cw_all[a * 9 + b * 3 + e]
                                else:
                                    slab = zero_slab
                                wide[pp * 2 + qq, a, pl.ds(row, 16), :] = slab
        return carry

    lax.fori_loop(0, 3, build, 0)

    full.wait_recv()

    @pl.when(has_up)
    def _():
        for c in down:
            c.wait_recv()
        lat_edge_down.wait_recv()

    @pl.when(has_down)
    def _():
        for c in up:
            c.wait_recv()
        lat_edge_up.wait_recv()

    bias = head_bias[...]

    def place(low, base, step, packed):
        count = packed.shape[0]
        flat = packed.astype(BF16).astype(F32).reshape(count * 16, 128)
        lane = lax.broadcasted_iota(jnp.int32, flat.shape, 1) < 64
        turn = pltpu.roll(flat, 64, 1)
        before = shifted(flat, -1)
        after = shifted(flat, 1)
        turn_before = pltpu.roll(before, 64, 1)
        turn_after = pltpu.roll(after, 64, 1)
        for q, frame, left, right in (
            (0, base, before, turn),
            (0, base + step, turn_before, flat),
            (1, base, flat, turn_after),
            (1, base + step, turn, after),
        ):
            z[q, frame, pl.ds(low, count)] = (
                jnp.where(lane, left, right).astype(BF16).reshape(count, 16, 128)
            )

    up_live = has_up.astype(F32)
    down_live = has_down.astype(F32)

    @pl.when(jnp.logical_not(has_up))
    def _():
        part_h[0] = jnp.zeros((2, 2, 16, 128), F32)
        lat_h[0] = jnp.zeros((16, 128), F32)

    @pl.when(jnp.logical_not(has_down))
    def _():
        part_h[1] = jnp.zeros((2, 2, 16, 128), F32)
        lat_h[1] = jnp.zeros((16, 128), F32)

    for t in range(2):
        own = part[t] + part_x[t] + bias
        new_lat[t] = own.astype(BF16)
        place(1, 2 + t, 2, own)
        place(0, 2 + t, 2, ((part_h[0, 0, t] + part_h[0, 1, t] + bias) * up_live)[None])
        place(5, 2 + t, 2, ((part_h[1, 0, t] + part_h[1, 1, t] + bias) * down_live)[None])
    place(1, 0, 1, lat_own[...])
    place(0, 0, 1, lat_h[0][None])
    place(5, 0, 1, lat_h[1][None])

    total = jnp.zeros((16, 512), F32)
    square = jnp.zeros((16, 512), F32)
    conv_bias = par_all[0]
    for pp in range(2):
        for qq in range(2):
            out = jnp.zeros((320, 512), F32)
            for a in range(3):
                lhs = jnp.concatenate(
                    [z[qq, a : a + 4, di : di + 5].reshape(320, 128) for di in range(2)], axis=1
                )
                out = out + jnp.dot(lhs, wide[pp * 2 + qq, a], preferred_element_type=F32)
            first = (out + conv_bias).astype(BF16)
            h1[pp * 2 + qq] = first.reshape(4, 5, 16, 512)
            mine = first.astype(F32).reshape(4, 5, 16, 512)[:, pp : pp + 4].reshape(16, 16, 512)
            total = total + jnp.sum(mine, axis=0)
            square = square + jnp.sum(mine * mine, axis=0)
    stats[...] = jnp.concatenate(
        [
            jnp.sum(total[0:8], axis=0, keepdims=True),
            jnp.sum(total[8:16], axis=0, keepdims=True),
            jnp.sum(square[0:8], axis=0, keepdims=True),
            jnp.sum(square[8:16], axis=0, keepdims=True),
            jnp.zeros((4, 512), F32),
        ],
        axis=0,
    )
    stat_copies = [
        remote(stats, stats_in.at[k - 1], st_s.at[k - 1], st_r.at[k - 1], (s, d, lax.rem(r + k, n_row)))
        for k in range(1, n_row)
    ]
    for c in stat_copies:
        c.start()
    for c in stat_copies:
        c.wait_recv()
    sums = stats[...]
    for k in range(1, n_row):
        sums = sums + stats_in[k - 1]
    lane8 = lax.broadcasted_iota(jnp.int32, (8, 512), 1)
    for k in (1, 2, 4, 8):
        other = jnp.where((lane8 & k) > 0, pltpu.roll(sums, k, 1), pltpu.roll(sums, 512 - k, 1))
        sums = sums + other
    sums = sums / (4 * 8 * 16 * GROUP * n_row)
    gv = sums[2:4] - sums[0:2] * sums[0:2]
    scale = lax.rsqrt(gv + 1e-5) * par_all[1]
    shift = par_all[2]

    def spread(v):
        return jnp.concatenate(
            [jnp.broadcast_to(v[0:1], (8, 512)), jnp.broadcast_to(v[1:2], (8, 512))], axis=0
        )

    mean16 = spread(sums[0:2])
    scale16 = spread(scale)

    def activate(t, carry):
        for pp in range(2):
            for qq in range(2):
                v = (h1[pp * 2 + qq, t].astype(F32) - mean16) * scale16 + shift
                v = v * (0.5 * jnp.tanh(0.5 * v) + 0.5)
                edge = lax.broadcasted_iota(jnp.int32, (5, 16, 512), 0)
                if pp == 1:
                    v = jnp.where((edge == 0) & jnp.logical_not(has_up), 0.0, v)
                else:
                    v = jnp.where((edge == 4) & jnp.logical_not(has_down), 0.0, v)
                v = v.astype(BF16)
                mb[pp, qq, t + 2] = v
                moved = shifted(v.astype(F32).reshape(80, 512), -1 if qq == 1 else 1)
                mb[pp, 2 if qq == 1 else 3, t + 2] = moved.astype(BF16).reshape(5, 16, 512)
        return carry

    lax.fori_loop(0, 4, activate, 0)

    acc[...] = jnp.zeros_like(acc)

    def conv(k, pairs):
        b = k // 3
        e = k % 3
        for a, t0, nt in pairs:
            pieces = []
            for pp in range(2):
                src = (b + 1) % 2 if pp == 0 else b % 2
                off = b // 2 if pp == 0 else (b + 1) // 2
                for qq in range(2):
                    var = (e + 2) % 3 if qq == 0 else e + e // 2
                    pieces.append(
                        mb[src, var, t0 + a : t0 + a + nt, pl.ds(off, 4)].reshape(nt * 64, 512)
                    )
            lhs = jnp.concatenate(pieces, axis=0)
            got = jnp.dot(lhs, midw_v[a * 9 + k], preferred_element_type=F32)
            acc[:, t0 : t0 + nt] += got.reshape(4, nt, 64, 256)

    load_w.wait()

    def tap_late(k, carry):
        conv(k, ((2, 0, 4),))
        return carry

    lax.fori_loop(0, 9, tap_late, 0)

    own_mid.wait()
    for k in range(1, n_dec):
        mid_copy(k, lax.rem(d + n_dec - k, n_dec)).wait_recv()
    zero_row = jnp.zeros((2, 32, 512), BF16)

    @pl.when(jnp.logical_not(has_up))
    def _():
        pm[:, 0] = zero_row

    @pl.when(jnp.logical_not(has_down))
    def _():
        pm[:, 9] = zero_row

    for st in range(2):
        live = (span[st] > 0).astype(BF16)
        pm[:, 1:9, pl.ds(16 * st, 16), lanes] = gm[moves[2 * d + st]] * live

    pm_full = remote(
        pm.at[:, 1:9, :, lanes], pm.at[:, 1:9, :, lanes], pm_s.at[0], pm_r.at[0], (o, d, r)
    )
    pm_up = [
        remote(pm.at[:, 1, :, lanes], pm.at[:, 9, :, lanes], pm_s.at[1 + n], pm_r.at[1 + n], (dev, d, r - 1))
        for n, dev in enumerate((s, o))
    ]
    pm_down = [
        remote(pm.at[:, 8, :, lanes], pm.at[:, 0, :, lanes], pm_s.at[3 + n], pm_r.at[3 + n], (dev, d, r + 1))
        for n, dev in enumerate((s, o))
    ]
    pm_full.start()

    @pl.when(has_up)
    def _():
        for c in pm_up:
            c.start()

    @pl.when(has_down)
    def _():
        for c in pm_down:
            c.start()

    def tap_mid(k, carry):
        conv(k, ((1, 1, 3), (0, 2, 2)))
        return carry

    lax.fori_loop(0, 9, tap_mid, 0)

    def blend(rows, cols, offs):
        return offs

    ro = lax.broadcasted_iota(jnp.int32, (64, 32), 0)
    co = lax.broadcasted_iota(jnp.int32, (64, 32), 1)
    v4 = ro // 16
    j2 = 2 * (ro % 8)
    col = jnp.where(v4 == 0, j2, jnp.where(v4 == 1, j2 + 1, jnp.where(v4 == 2, j2 - 1, j2 + 2)))
    fits = (col >= 0) & (col < 16) & (co == (ro // 8) % 2 * 16 + col)
    deal = jnp.where(fits, 1.0, 0.0).astype(BF16)

    ro = lax.broadcasted_iota(jnp.int32, (32, 32), 0)
    co = lax.broadcasted_iota(jnp.int32, (32, 32), 1)
    weave = jnp.where(co == (ro % 2) * 16 + (ro // 16) * 8 + (ro % 16) // 2, 1.0, 0.0).astype(BF16)

    def keep_mid(t, carry):
        for pp in range(2):
            for i in range(4):
                y = jnp.concatenate(
                    [mb[pp, 0, t + 4, i + pp, :, lanes], mb[pp, 1, t + 4, i + pp, :, lanes]], axis=0
                )
                y = jnp.dot(weave, y, preferred_element_type=F32).astype(BF16)
                new_mid[0, t, 2 * i + pp] = y[0:16]
                new_mid[1, t, 2 * i + pp] = y[16:32]
        return carry

    lax.fori_loop(0, 2, keep_mid, 0)

    pm_full_in = remote(
        pm.at[:, 1:9, :, olanes], pm.at[:, 1:9, :, olanes], pm_s.at[0], pm_r.at[0], (o, d, r)
    )
    pm_full_in.wait_recv()

    @pl.when(has_up)
    def _():
        for n, c in enumerate((lanes, olanes)):
            remote(
                pm.at[:, 8, :, c], pm.at[:, 0, :, c], pm_s.at[3 + n], pm_r.at[3 + n], (s, d, r - 1)
            ).wait_recv()

    @pl.when(has_down)
    def _():
        for n, c in enumerate((lanes, olanes)):
            remote(
                pm.at[:, 1, :, c], pm.at[:, 9, :, c], pm_s.at[1 + n], pm_r.at[1 + n], (s, d, r + 1)
            ).wait_recv()

    def unfold(f, carry):
        for row in range(10):
            y = jnp.dot(deal, pm[f, row], preferred_element_type=F32).astype(BF16)
            for v in range(4):
                mb[(row + 1) % 2, v, f, row // 2] = y[16 * v : 16 * v + 16]
        return carry

    lax.fori_loop(0, 2, unfold, 0)

    def tap_early(k, carry):
        conv(k, ((1, 0, 1), (0, 0, 2)))
        return carry

    lax.fori_loop(0, 9, tap_early, 0)

    def finish(t, carry):
        for pp in range(2):
            for i in range(4):
                y = jnp.concatenate(
                    [
                        h1[pp * 2 + qq, t, i + pp, :, lanes].astype(F32)
                        + acc[pp * 2 + qq, t, pl.ds(16 * i, 16)]
                        + midb[...]
                        for qq in range(2)
                    ],
                    axis=0,
                ).astype(BF16)
                y = jnp.dot(weave, y, preferred_element_type=F32).astype(BF16)
                decoded[0, t, 2 * i + pp] = y[0:16]
                decoded[1, t, 2 * i + pp] = y[16:32]
        return carry

    lax.fori_loop(0, 4, finish, 0)

    for k in range(1, n_dec):
        lat_copy(k, d).wait_send()
        mid_copy(k, d).wait_send()
    cw_copy.wait_send()
    for c in par_copies + stat_copies + [full, pm_full]:
        c.wait_send()

    @pl.when(has_up)
    def _():
        for c in up + pm_up + [lat_edge_up]:
            c.wait_send()

    @pl.when(has_down)
    def _():
        for c in down + pm_down + [lat_edge_down]:
            c.wait_send()


def shards(
    n_dec,
    n_row,
    hidden,
    head_weight,
    head_bias,
    lat_cache,
    mid_cache,
    moves,
    span_index,
    conv_in_weight,
    conv_in_bias,
    gn_gain,
    gn_bias,
    mid_weight,
    mid_bias,
):
    slots = n_dec * 2
    depth = hidden.shape[-1]
    head_t = jnp.pad(head_weight.T, ((0, 64), (0, 0)))
    bias = jnp.concatenate([head_bias, head_bias]).reshape(1, 128)
    lat = lat_cache.reshape(2, 2, 4, 2, 8, 2, CZ).transpose(0, 2, 4, 1, 3, 5, 6).reshape(2, 32, 128)
    vm = pl.BlockSpec(memory_space=pltpu.VMEM)
    sm = pl.BlockSpec(memory_space=pltpu.SMEM)
    hbm = pl.BlockSpec(memory_space=pl.ANY)
    dma = pltpu.SemaphoreType.DMA
    decoded, latent, new_mid = pl.pallas_call(
        functools.partial(kernel, n_dec, n_row),
        out_shape=(
            jax.ShapeDtypeStruct((2, 4, 8, 16, 256), BF16),
            jax.ShapeDtypeStruct((2, 4, 16, 128), BF16),
            jax.ShapeDtypeStruct((2, 2, 8, 16, 256), BF16),
        ),
        in_specs=[hbm, vm, vm, vm, hbm, sm, sm, vm, vm, vm, vm, hbm, vm],
        out_specs=(vm, vm, vm),
        scratch_shapes=[
            pltpu.VMEM((256, depth), BF16),
            pltpu.VMEM((27, 512, 256), BF16),
            pltpu.VMEM((2, 4, 16, 128), F32),
            pltpu.VMEM((2, 4, 16, 128), F32),
            pltpu.VMEM((2, 2, 2, 16, 128), F32),
            pltpu.VMEM((slots, 32, 128), BF16),
            pltpu.VMEM((4, 16, 128), F32),
            pltpu.VMEM((2, 16, 128), F32),
            pltpu.VMEM((27, CZ, 512), BF16),
            pltpu.VMEM((3, 1, 512), F32),
            pltpu.VMEM((4, 3, 256, 512), BF16),
            pltpu.VMEM((2, 6, 6, 16, 128), BF16),
            pltpu.VMEM((4, 4, 5, 16, 512), BF16),
            pltpu.VMEM((8, 512), F32),
            pltpu.VMEM((n_row - 1, 8, 512), F32),
            pltpu.VMEM((slots, 2, 8, 16, 256), BF16),
            pltpu.VMEM((2, 10, 32, 512), BF16),
            pltpu.VMEM((2, 4, 6, 5, 16, 512), BF16),
            pltpu.VMEM((4, 4, 64, 256), F32),
            dma((3,)),
            dma((n_dec - 1,)),
            dma((n_dec - 1,)),
            dma((n_dec - 1,)),
            dma((n_dec - 1,)),
            dma((4,)),
            dma((4,)),
            dma((5,)),
            dma((5,)),
            dma((2,)),
            dma((2,)),
            dma((n_row - 1,)),
            dma((n_row - 1,)),
            dma((5,)),
            dma((5,)),
        ],
        compiler_params=pltpu.CompilerParams(
            collective_id=0, has_side_effects=True, vmem_limit_bytes=56 * 1024 * 1024
        ),
        cost_estimate=pl.CostEstimate(
            flops=9_000_000_000, bytes_accessed=12_000_000, transcendentals=700_000
        ),
    )(
        hidden.reshape(256, depth),
        head_t,
        bias,
        lat,
        mid_cache,
        moves,
        span_index,
        conv_in_weight.reshape(27, CZ, 256),
        conv_in_bias.reshape(1, 256),
        gn_gain.reshape(1, 256),
        gn_bias.reshape(1, 256),
        mid_weight.reshape(27, 512, 256),
        mid_bias.reshape(1, 256),
    )
    kept = latent[..., 64:].reshape(2, 4, 2, 8, 2, 2, CZ)
    kept = kept.transpose(2, 0, 1, 4, 3, 5, 6).reshape(2, 2, 8, 16, CZ)
    return decoded, kept, new_mid


def solution(mesh):
    placed = (
        P("dec", None, "row", None, "section"),
        P("section", None),
        P(),
        P("dec", None, "row", None, None),
        P("dec", None, "row", None, "section"),
        P(),
        P("dec"),
        P(None, None, None, None, "section"),
        P("section"),
        P("section"),
        P("section"),
        P(None, None, None, None, "section"),
        P("section"),
    )
    return jax.shard_map(
        functools.partial(shards, mesh.shape["dec"], mesh.shape["row"]),
        mesh=mesh,
        in_specs=placed,
        out_specs=(
            P("dec", None, "row", None, "section"),
            P("dec", None, "row", None, None),
            P("dec", None, "row", None, "section"),
        ),
        check_vma=False,
    )
```

```python
import functools

import jax
import jax.numpy as jnp
from jax import lax
from jax.experimental import pallas as pl
from jax.experimental.pallas import tpu as pltpu
from jax.sharding import PartitionSpec as P

CZ = 16
GROUP = 16
MESH = pl.DeviceIdType.MESH
F32 = jnp.float32
BF16 = jnp.bfloat16


def shifted(flat, step):
    n = flat.shape[0]
    j = lax.broadcasted_iota(jnp.int32, flat.shape, 0) % 8
    if step < 0:
        return jnp.where(j == 0, 0.0, pltpu.roll(flat, 1, 0))
    return jnp.where(j == 7, 0.0, pltpu.roll(flat, n - 1, 0))


def kernel(
    n_dec,
    n_row,
    hidden,
    head_t,
    head_bias,
    lat,
    mid,
    moves,
    span,
    cw,
    cb,
    gain,
    gbias,
    midw,
    midb,
    decoded,
    new_lat,
    new_mid,
    lat_pk,
    hid_v,
    midw_v,
    part,
    part_x,
    part_h,
    lat_all,
    lat_own,
    lat_h,
    cw_all,
    par_all,
    wide,
    z,
    h1,
    stats,
    stats_in,
    gm0,
    gm1,
    sel,
    pm,
    mb,
    acc,
    local_sem,
    lat_s,
    lat_r,
    mid_s,
    mid_r,
    hop_s,
    hop_r,
    w_s,
    w_r,
    part_s,
    part_r,
    lh_s,
    lh_r,
    st_s,
    st_r,
    pm_s,
    pm_r,
):
    s = lax.axis_index("section")
    d = lax.axis_index("dec")
    r = lax.axis_index("row")
    o = 1 - s
    lanes = pl.ds(pl.multiple_of(s * 256, 256), 256)
    olanes = pl.ds(pl.multiple_of(o * 256, 256), 256)
    has_up = r > 0
    has_down = r < n_row - 1

    barrier = pltpu.get_barrier_semaphore()

    def greet(dev):
        pl.semaphore_signal(barrier, inc=1, device_id=dev, device_id_type=MESH)

    greet((o, d, r))
    for k in range(1, n_dec):
        greet((s, lax.rem(d + k, n_dec), r))
    for k in range(1, n_row):
        greet((s, d, lax.rem(r + k, n_row)))
        greet((o, d, lax.rem(r + k, n_row)))

    load_hidden = pltpu.make_async_copy(hidden, hid_v, local_sem.at[0])
    load_hidden.start()
    gm = (gm0, gm1)
    own_mid = [
        pltpu.make_async_copy(mid.at[:, f], gm[f].at[pl.ds(2 * d, 2)], local_sem.at[1 + f])
        for f in range(2)
    ]
    for c in own_mid:
        c.start()
    load_w = pltpu.make_async_copy(midw, midw_v, local_sem.at[3])
    load_w.start()

    ri = lax.broadcasted_iota(jnp.int32, (CZ, 128), 0)
    ci = lax.broadcasted_iota(jnp.int32, (CZ, 128), 1)
    tile = jnp.where(ci % CZ == ri, 1.0, 0.0).astype(BF16)
    wide_lat = jnp.dot(lat[...].reshape(512, CZ), tile, preferred_element_type=F32)
    wide_lat = wide_lat.reshape(2, 2, 4, 2, 16, 128)
    lane6 = lax.broadcasted_iota(jnp.int32, (2, 4, 16, 128), 3) // 32
    merged = jnp.where(
        lane6 == 0,
        wide_lat[:, 0, :, 0],
        jnp.where(lane6 == 1, wide_lat[:, 0, :, 1], jnp.where(lane6 == 2, wide_lat[:, 1, :, 0], wide_lat[:, 1, :, 1])),
    )
    merged = merged.reshape(128, 128).astype(BF16)
    ri = lax.broadcasted_iota(jnp.int32, (64, 128), 0)
    ci = lax.broadcasted_iota(jnp.int32, (64, 128), 1)
    halves = [
        jnp.dot(
            jnp.where(ci == ri // 8 * 16 + 2 * (ri % 8) + q, 1.0, 0.0).astype(BF16),
            merged,
            preferred_element_type=F32,
        )
        for q in range(2)
    ]
    lat_pk[...] = (
        jnp.where(ci // 16 % 2 == 0, halves[0], halves[1]).astype(BF16).reshape(2, 32, 128)
    )

    pl.semaphore_wait(barrier, 1 + (n_dec - 1) + 2 * (n_row - 1))

    def remote(src, dst, ssem, rsem, dev):
        return pltpu.make_async_remote_copy(
            src_ref=src, dst_ref=dst, send_sem=ssem, recv_sem=rsem, device_id=dev, device_id_type=MESH
        )

    def lat_copy(k, origin):
        return remote(
            lat_pk, lat_all.at[pl.ds(2 * origin, 2)], lat_s.at[k - 1], lat_r.at[k - 1],
            (s, lax.rem(d + k, n_dec), r),
        )

    def mid_copy(k, origin, f):
        return remote(
            mid.at[:, f], gm[f].at[pl.ds(2 * origin, 2)], mid_s.at[k - 1, f], mid_r.at[k - 1, f],
            (s, lax.rem(d + k, n_dec), r),
        )

    line = n_dec == 4
    inner = (d == 1) | (d == 2)
    end = 3 * (d - 1)
    near = 1 + d // 3

    def end_copy(f):
        return remote(
            mid.at[:, f], gm[f].at[pl.ds(2 * d, 2)], hop_s.at[0, f], hop_r.at[0, f], (s, near, r)
        )

    def cross_copy(f):
        return remote(
            mid.at[:, f], gm[f].at[pl.ds(2 * d, 2)], hop_s.at[1, f], hop_r.at[1, f], (s, 3 - d, r)
        )

    def pass_copy(f):
        slots = pl.ds(2 * end, 2)
        return remote(
            gm[f].at[slots], gm[f].at[slots], hop_s.at[2, f], hop_r.at[2, f], (s, 3 - d, r)
        )

    def pick_copy(f, target):
        return remote(sel.at[f], sel.at[f], hop_s.at[3, f], hop_r.at[3, f], (s, target, r))

    def pass_on(f):
        if line:

            @pl.when(inner)
            def _():
                end_copy(f).wait_recv()
                pass_copy(f).start()

    for k in range(1, n_dec):
        lat_copy(k, d).start()

    half = lax.rem(r, 2)
    half_lanes = pl.ds(pl.multiple_of(half * 128, 128), 128)
    out_lanes = pl.ds(pl.multiple_of(s * 256 + half * 128, 128), 128)
    in_lanes = pl.ds(pl.multiple_of(o * 256 + half * 128, 128), 128)
    cw_copy = remote(
        cw.at[:, :, half_lanes], cw_all.at[:, :, out_lanes], w_s.at[0], w_r.at[0], (o, d, r)
    )
    cw_copy.start()
    cw_pass = remote(
        cw_all.at[:, :, in_lanes], cw_all.at[:, :, in_lanes], w_s.at[4], w_r.at[4],
        (s, d, r + 1 - 2 * half),
    )
    par_copies = [
        remote(ref, par_all.at[n, :, lanes], w_s.at[n + 1], w_r.at[n + 1], (o, d, r))
        for n, ref in enumerate((cb, gain, gbias))
    ]
    for c in par_copies:
        c.start()
    if line:

        @pl.when(inner)
        def _():
            for f in range(2):
                cross_copy(f).start()

        @pl.when(jnp.logical_not(inner))
        def _():
            for f in range(2):
                end_copy(f).start()

    else:
        for k in range(1, n_dec):
            for f in range(2):
                mid_copy(k, d, f).start()

    load_hidden.wait()
    head = lax.dot_general(
        hid_v[...],
        jnp.concatenate([head_t[...], jnp.zeros_like(head_t)], axis=0),
        (((1,), (1,)), ((), ())),
        preferred_element_type=F32,
    )
    head = head.reshape(2, 4, 4, 8, 128)
    lane = lax.broadcasted_iota(jnp.int32, (4, 8, 128), 2)
    for t in range(2):
        for st in range(2):
            high = pltpu.roll(head[st, t + 2].reshape(32, 128), 64, 1).reshape(4, 8, 128)
            part[t, :, pl.ds(8 * st, 8), :] = jnp.where(lane < 64, head[st, t], high)

    def part_copies():
        full = remote(part, part_x, part_s.at[0], part_r.at[0], (o, d, r))
        up = [
            remote(part.at[:, 0], part_h.at[1, n], part_s.at[1 + n], part_r.at[1 + n], (dev, d, r - 1))
            for n, dev in enumerate((s, o))
        ]
        down = [
            remote(part.at[:, 3], part_h.at[0, n], part_s.at[3 + n], part_r.at[3 + n], (dev, d, r + 1))
            for n, dev in enumerate((s, o))
        ]
        return full, up, down

    full, up, down = part_copies()

    @pl.when(has_up)
    def _():
        for c in up:
            c.start()

    @pl.when(has_down)
    def _():
        for c in down:
            c.start()

    full.start()

    lat_all[pl.ds(2 * d, 2)] = lat_pk[...]
    cw_all[:, :, lanes] = cw[...]
    for n, ref in enumerate((cb, gain, gbias)):
        par_all[n, :, lanes] = ref[...]

    for k in range(1, n_dec):
        lat_copy(k, lax.rem(d + n_dec - k, n_dec)).wait_recv()
    for st in range(2):
        live = (span[st] > 0).astype(F32)
        x = lat_all[moves[2 * d + st]].astype(F32) * live
        lat_own[:, pl.ds(8 * st, 8), :] = x.reshape(4, 8, 128)
    lat_edge_up = remote(lat_own.at[0], lat_h.at[1], lh_s.at[0], lh_r.at[0], (s, d, r - 1))
    lat_edge_down = remote(lat_own.at[3], lat_h.at[0], lh_s.at[1], lh_r.at[1], (s, d, r + 1))

    @pl.when(has_up)
    def _():
        lat_edge_up.start()

    @pl.when(has_down)
    def _():
        lat_edge_down.start()

    cw_copy.wait_recv()
    cw_pass.start()
    for n, ref in enumerate((cb, gain, gbias)):
        remote(ref, par_all.at[n, :, olanes], w_s.at[n + 1], w_r.at[n + 1], (o, d, r)).wait_recv()
    cw_pass.wait_recv()
    zero_slab = jnp.zeros((CZ, 512), BF16)

    def build(a, carry):
        for pp in range(2):
            for qq in range(2):
                for di in range(2):
                    for dj in range(2):
                        for p in range(2):
                            for q in range(2):
                                b = 2 * di + p - 1 + pp
                                e = 2 * dj + q - 1 + qq
                                row = di * 128 + dj * 64 + p * 32 + q * 16
                                if 0 <= b < 3 and 0 <= e < 3:
                                    slab = cw_all[a * 9 + b * 3 + e]
                                else:
                                    slab = zero_slab
                                wide[pp * 2 + qq, a, pl.ds(row, 16), :] = slab
        return carry

    lax.fori_loop(0, 3, build, 0)
    pass_on(0)

    full.wait_recv()

    @pl.when(has_up)
    def _():
        for c in down:
            c.wait_recv()
        lat_edge_down.wait_recv()

    @pl.when(has_down)
    def _():
        for c in up:
            c.wait_recv()
        lat_edge_up.wait_recv()

    bias = jnp.concatenate([head_bias[...], head_bias[...]], axis=1)

    def place(low, base, step, packed):
        count = packed.shape[0]
        flat = packed.astype(BF16).astype(F32).reshape(count * 16, 128)
        lane = lax.broadcasted_iota(jnp.int32, flat.shape, 1) < 64
        turn = pltpu.roll(flat, 64, 1)
        before = shifted(flat, -1)
        after = shifted(flat, 1)
        turn_before = pltpu.roll(before, 64, 1)
        turn_after = pltpu.roll(after, 64, 1)
        for q, frame, left, right in (
            (0, base, before, turn),
            (0, base + step, turn_before, flat),
            (1, base, flat, turn_after),
            (1, base + step, turn, after),
        ):
            z[q, frame, pl.ds(low, count)] = (
                jnp.where(lane, left, right).astype(BF16).reshape(count, 16, 128)
            )

    up_live = has_up.astype(F32)
    down_live = has_down.astype(F32)

    @pl.when(jnp.logical_not(has_up))
    def _():
        part_h[0] = jnp.zeros((2, 2, 16, 128), F32)
        lat_h[0] = jnp.zeros((16, 128), F32)

    @pl.when(jnp.logical_not(has_down))
    def _():
        part_h[1] = jnp.zeros((2, 2, 16, 128), F32)
        lat_h[1] = jnp.zeros((16, 128), F32)

    for t in range(2):
        own = part[t] + part_x[t] + bias
        new_lat[t] = own.astype(BF16)
        place(1, 2 + t, 2, own)
        place(0, 2 + t, 2, ((part_h[0, 0, t] + part_h[0, 1, t] + bias) * up_live)[None])
        place(5, 2 + t, 2, ((part_h[1, 0, t] + part_h[1, 1, t] + bias) * down_live)[None])
    place(1, 0, 1, lat_own[...])
    place(0, 0, 1, lat_h[0][None])
    place(5, 0, 1, lat_h[1][None])

    total = jnp.zeros((16, 512), F32)
    square = jnp.zeros((16, 512), F32)
    conv_bias = par_all[0]
    for pp in range(2):
        for qq in range(2):
            out = jnp.zeros((320, 512), F32)
            for a in range(3):
                lhs = jnp.concatenate(
                    [z[qq, a : a + 4, di : di + 5].reshape(320, 128) for di in range(2)], axis=1
                )
                out = out + jnp.dot(lhs, wide[pp * 2 + qq, a], preferred_element_type=F32)
            first = (out + conv_bias).astype(BF16)
            h1[pp * 2 + qq] = first.reshape(4, 5, 16, 512)
            mine = first.astype(F32).reshape(4, 5, 16, 512)[:, pp : pp + 4].reshape(16, 16, 512)
            total = total + jnp.sum(mine, axis=0)
            square = square + jnp.sum(mine * mine, axis=0)
    stats[...] = jnp.concatenate(
        [
            jnp.sum(total[0:8], axis=0, keepdims=True),
            jnp.sum(total[8:16], axis=0, keepdims=True),
            jnp.sum(square[0:8], axis=0, keepdims=True),
            jnp.sum(square[8:16], axis=0, keepdims=True),
            jnp.zeros((4, 512), F32),
        ],
        axis=0,
    )
    stat_copies = [
        remote(stats, stats_in.at[k - 1], st_s.at[k - 1], st_r.at[k - 1], (s, d, lax.rem(r + k, n_row)))
        for k in range(1, n_row)
    ]
    for c in stat_copies:
        c.start()
    pass_on(1)
    for c in stat_copies:
        c.wait_recv()
    sums = stats[...]
    for k in range(1, n_row):
        sums = sums + stats_in[k - 1]
    lane8 = lax.broadcasted_iota(jnp.int32, (8, 512), 1)
    for k in (1, 2, 4, 8):
        other = jnp.where((lane8 & k) > 0, pltpu.roll(sums, k, 1), pltpu.roll(sums, 512 - k, 1))
        sums = sums + other
    sums = sums / (4 * 8 * 16 * GROUP * n_row)
    gv = sums[2:4] - sums[0:2] * sums[0:2]
    scale = lax.rsqrt(gv + 1e-5) * par_all[1]
    shift = par_all[2]

    def spread(v):
        return jnp.concatenate(
            [jnp.broadcast_to(v[0:1], (8, 512)), jnp.broadcast_to(v[1:2], (8, 512))], axis=0
        )

    mean16 = spread(sums[0:2])
    scale16 = spread(scale)

    def activate(t, carry):
        for pp in range(2):
            for qq in range(2):
                v = (h1[pp * 2 + qq, t].astype(F32) - mean16) * scale16 + shift
                v = v * (0.5 * jnp.tanh(0.5 * v) + 0.5)
                edge = lax.broadcasted_iota(jnp.int32, (5, 16, 512), 0)
                if pp == 1:
                    v = jnp.where((edge == 0) & jnp.logical_not(has_up), 0.0, v)
                else:
                    v = jnp.where((edge == 4) & jnp.logical_not(has_down), 0.0, v)
                v = v.astype(BF16)
                mb[pp, qq, t + 2] = v
                moved = shifted(v.astype(F32).reshape(80, 512), -1 if qq == 1 else 1)
                mb[pp, 2 if qq == 1 else 3, t + 2] = moved.astype(BF16).reshape(5, 16, 512)
        return carry

    lax.fori_loop(0, 4, activate, 0)

    acc[...] = jnp.zeros_like(acc)

    def conv(k, pairs):
        b = k // 3
        e = k % 3
        for a, t0, nt in pairs:
            pieces = []
            for pp in range(2):
                src = (b + 1) % 2 if pp == 0 else b % 2
                off = b // 2 if pp == 0 else (b + 1) // 2
                for qq in range(2):
                    var = (e + 2) % 3 if qq == 0 else e + e // 2
                    pieces.append(
                        mb[src, var, t0 + a : t0 + a + nt, pl.ds(off, 4)].reshape(nt * 64, 512)
                    )
            lhs = jnp.concatenate(pieces, axis=0)
            got = jnp.dot(lhs, midw_v[a * 9 + k], preferred_element_type=F32)
            acc[:, t0 : t0 + nt] += got.reshape(4, nt, 64, 256)

    load_w.wait()

    def tap_late(k, carry):
        conv(k, ((2, 0, 4),))
        return carry

    zero_row = jnp.zeros((2, 32, 512), BF16)

    @pl.when(jnp.logical_not(has_up))
    def _():
        pm[:, 0] = zero_row

    @pl.when(jnp.logical_not(has_down))
    def _():
        pm[:, 9] = zero_row

    def pm_full(f):
        block = pm.at[f, 1:9, :, lanes]
        return remote(block, block, pm_s.at[f, 0], pm_r.at[f, 0], (o, d, r))

    def pm_up(f):
        return [
            remote(pm.at[f, 1, :, lanes], pm.at[f, 9, :, lanes], pm_s.at[f, 1 + n], pm_r.at[f, 1 + n], (dev, d, r - 1))
            for n, dev in enumerate((s, o))
        ]

    def pm_down(f):
        return [
            remote(pm.at[f, 8, :, lanes], pm.at[f, 0, :, lanes], pm_s.at[f, 3 + n], pm_r.at[f, 3 + n], (dev, d, r + 1))
            for n, dev in enumerate((s, o))
        ]

    def share(f, pick):
        for st in range(2):
            live = (span[st] > 0).astype(BF16)
            pm[f, 1:9, pl.ds(16 * st, 16), lanes] = pick(st) * live
        pm_full(f).start()

        @pl.when(has_up)
        def _():
            for c in pm_up(f):
                c.start()

        @pl.when(has_down)
        def _():
            for c in pm_down(f):
                c.start()

    def share_inner(f):
        if line:

            @pl.when(inner)
            def _():
                own_mid[f].wait()
                cross_copy(f).wait_recv()
                pass_copy(f).wait_recv()
                for st in range(2):
                    sel[f, :, pl.ds(16 * st, 16), :] = gm[f][moves[2 * end + st]]
                pick_copy(f, end).start()
                share(f, lambda st: gm[f][moves[2 * d + st]])

    def share_end(f):
        if line:

            @pl.when(jnp.logical_not(inner))
            def _():
                pick_copy(f, near).wait_recv()
                share(f, lambda st: sel[f, :, pl.ds(16 * st, 16), :])

        else:
            own_mid[f].wait()
            for k in range(1, n_dec):
                mid_copy(k, lax.rem(d + n_dec - k, n_dec), f).wait_recv()
            share(f, lambda st: gm[f][moves[2 * d + st]])

    share_inner(0)
    lax.fori_loop(0, 4, tap_late, 0)
    share_inner(1)
    lax.fori_loop(4, 9, tap_late, 0)
    share_end(0)
    share_end(1)

    def tap_mid(k, carry):
        conv(k, ((1, 1, 3), (0, 2, 2)))
        return carry

    lax.fori_loop(0, 9, tap_mid, 0)

    ro = lax.broadcasted_iota(jnp.int32, (64, 32), 0)
    co = lax.broadcasted_iota(jnp.int32, (64, 32), 1)
    v4 = ro // 16
    j2 = 2 * (ro % 8)
    col = jnp.where(v4 == 0, j2, jnp.where(v4 == 1, j2 + 1, jnp.where(v4 == 2, j2 - 1, j2 + 2)))
    fits = (col >= 0) & (col < 16) & (co == (ro // 8) % 2 * 16 + col)
    deal = jnp.where(fits, 1.0, 0.0).astype(BF16)

    for t in range(2):
        for pp in range(2):
            for qq in range(2):
                new_mid[t, pp, :, pl.ds(16 * qq, 16), :] = mb[pp, qq, t + 4, pp : pp + 4, :, lanes]

    for f in range(2):
        pm_full(f).wait_recv()

        @pl.when(has_up)
        def _():
            for c in pm_down(f):
                c.wait_recv()

        @pl.when(has_down)
        def _():
            for c in pm_up(f):
                c.wait_recv()

    def unfold(f, carry):
        for row in range(10):
            y = jnp.dot(deal, pm[f, row], preferred_element_type=F32).astype(BF16)
            for v in range(4):
                mb[(row + 1) % 2, v, f, row // 2] = y[16 * v : 16 * v + 16]
        return carry

    lax.fori_loop(0, 2, unfold, 0)

    def tap_early(k, carry):
        conv(k, ((1, 0, 1), (0, 0, 2)))
        return carry

    lax.fori_loop(0, 9, tap_early, 0)

    def finish(t, carry):
        for pp in range(2):
            for qq in range(2):
                y = (
                    h1[pp * 2 + qq, t, pp : pp + 4, :, lanes].astype(F32)
                    + acc[pp * 2 + qq, t].reshape(4, 16, 256)
                    + midb[...]
                )
                decoded[t, pp, :, pl.ds(16 * qq, 16), :] = y.astype(BF16)
        return carry

    lax.fori_loop(0, 4, finish, 0)

    for k in range(1, n_dec):
        lat_copy(k, d).wait_send()
    for c in par_copies + stat_copies + [full, cw_copy, cw_pass, pm_full(0), pm_full(1)]:
        c.wait_send()
    if line:

        @pl.when(inner)
        def _():
            for f in range(2):
                cross_copy(f).wait_send()
                pass_copy(f).wait_send()
                pick_copy(f, end).wait_send()

        @pl.when(jnp.logical_not(inner))
        def _():
            for f in range(2):
                end_copy(f).wait_send()
                own_mid[f].wait()

    else:
        for k in range(1, n_dec):
            for f in range(2):
                mid_copy(k, d, f).wait_send()

    @pl.when(has_up)
    def _():
        for c in up + pm_up(0) + pm_up(1) + [lat_edge_up]:
            c.wait_send()

    @pl.when(has_down)
    def _():
        for c in down + pm_down(0) + pm_down(1) + [lat_edge_down]:
            c.wait_send()


def weave_kernel(decoded, new_lat, new_mid, decoded_out, new_lat_out, new_mid_out):
    ro = lax.broadcasted_iota(jnp.int32, (32, 32), 0)
    co = lax.broadcasted_iota(jnp.int32, (32, 32), 1)
    weave = jnp.where(co == (ro % 2) * 16 + (ro // 16) * 8 + (ro % 16) // 2, 1.0, 0.0).astype(BF16)

    def spread(source, target, t):
        for pp in range(2):
            for i in range(4):
                y = jnp.dot(weave, source[t, pp, i], preferred_element_type=F32).astype(BF16)
                target[0, t, 2 * i + pp] = y[0:16]
                target[1, t, 2 * i + pp] = y[16:32]

    for t in range(4):
        spread(decoded, decoded_out, t)
    for t in range(2):
        spread(new_mid, new_mid_out, t)

    patches = new_lat[...].reshape(128, 128)
    ro = lax.broadcasted_iota(jnp.int32, (256, 128), 0)
    co = lax.broadcasted_iota(jnp.int32, (256, 128), 1)
    grown = [
        jnp.dot(
            jnp.where((co == ro // 16 * 8 + ro % 16 // 2) & (ro % 2 == q), 1.0, 0.0).astype(BF16),
            patches,
            preferred_element_type=F32,
        )
        for q in range(2)
    ]
    grown = jnp.where(co // 16 % 2 == 0, grown[0], grown[1])
    ro = lax.broadcasted_iota(jnp.int32, (128, CZ), 0)
    for p in range(2):
        fold = (ro // 32 == 2 + p) & (ro % CZ == lax.broadcasted_iota(jnp.int32, (128, CZ), 1))
        y = jnp.dot(
            grown.astype(BF16), jnp.where(fold, 1.0, 0.0).astype(BF16), preferred_element_type=F32
        ).astype(BF16)
        for t in range(2):
            for i in range(4):
                for st in range(2):
                    row = ((t * 4 + i) * 2 + st) * 16
                    new_lat_out[st, t, 2 * i + p] = y[row : row + 16]


def shards(
    n_dec,
    n_row,
    hidden,
    head_weight,
    head_bias,
    lat_cache,
    mid_cache,
    moves,
    span_index,
    conv_in_weight,
    conv_in_bias,
    gn_gain,
    gn_bias,
    mid_weight,
    mid_bias,
):
    slots = n_dec * 2
    depth = hidden.shape[-1]
    vm = pl.BlockSpec(memory_space=pltpu.VMEM)
    sm = pl.BlockSpec(memory_space=pltpu.SMEM)
    hbm = pl.BlockSpec(memory_space=pl.ANY)
    dma = pltpu.SemaphoreType.DMA
    parts = pl.pallas_call(
        functools.partial(kernel, n_dec, n_row),
        out_shape=(
            jax.ShapeDtypeStruct((4, 2, 4, 32, 256), BF16),
            jax.ShapeDtypeStruct((2, 4, 16, 128), BF16),
            jax.ShapeDtypeStruct((2, 2, 4, 32, 256), BF16),
        ),
        in_specs=[hbm, vm, vm, vm, hbm, sm, sm, vm, vm, vm, vm, hbm, vm],
        out_specs=(vm, vm, vm),
        scratch_shapes=[
            pltpu.VMEM((2, 32, 128), BF16),
            pltpu.VMEM((256, depth), BF16),
            pltpu.VMEM((27, 512, 256), BF16),
            pltpu.VMEM((2, 4, 16, 128), F32),
            pltpu.VMEM((2, 4, 16, 128), F32),
            pltpu.VMEM((2, 2, 2, 16, 128), F32),
            pltpu.VMEM((slots, 32, 128), BF16),
            pltpu.VMEM((4, 16, 128), F32),
            pltpu.VMEM((2, 16, 128), F32),
            pltpu.VMEM((27, CZ, 512), BF16),
            pltpu.VMEM((3, 1, 512), F32),
            pltpu.VMEM((4, 3, 256, 512), BF16),
            pltpu.VMEM((2, 6, 6, 16, 128), BF16),
            pltpu.VMEM((4, 4, 5, 16, 512), BF16),
            pltpu.VMEM((8, 512), F32),
            pltpu.VMEM((n_row - 1, 8, 512), F32),
            pltpu.VMEM((slots, 8, 16, 256), BF16),
            pltpu.VMEM((slots, 8, 16, 256), BF16),
            pltpu.VMEM((2, 8, 32, 256), BF16),
            pltpu.VMEM((2, 10, 32, 512), BF16),
            pltpu.VMEM((2, 4, 6, 5, 16, 512), BF16),
            pltpu.VMEM((4, 4, 64, 256), F32),
            dma((4,)),
            dma((n_dec - 1,)),
            dma((n_dec - 1,)),
            dma((n_dec - 1, 2)),
            dma((n_dec - 1, 2)),
            dma((4, 2)),
            dma((4, 2)),
            dma((5,)),
            dma((5,)),
            dma((5,)),
            dma((5,)),
            dma((2,)),
            dma((2,)),
            dma((n_row - 1,)),
            dma((n_row - 1,)),
            dma((2, 5)),
            dma((2, 5)),
        ],
        compiler_params=pltpu.CompilerParams(
            collective_id=0, has_side_effects=True, vmem_limit_bytes=56 * 1024 * 1024
        ),
        cost_estimate=pl.CostEstimate(
            flops=9_000_000_000, bytes_accessed=12_000_000, transcendentals=700_000
        ),
    )(
        hidden.reshape(256, depth),
        head_weight.T,
        head_bias.reshape(1, 64),
        lat_cache,
        mid_cache,
        moves,
        span_index,
        conv_in_weight.reshape(27, CZ, 256),
        conv_in_bias.reshape(1, 256),
        gn_gain.reshape(1, 256),
        gn_bias.reshape(1, 256),
        mid_weight.reshape(27, 512, 256),
        mid_bias.reshape(1, 256),
    )
    return pl.pallas_call(
        weave_kernel,
        out_shape=(
            jax.ShapeDtypeStruct((2, 4, 8, 16, 256), BF16),
            jax.ShapeDtypeStruct((2, 2, 8, 16, CZ), BF16),
            jax.ShapeDtypeStruct((2, 2, 8, 16, 256), BF16),
        ),
        in_specs=[vm, vm, vm],
        out_specs=(vm, vm, vm),
        compiler_params=pltpu.CompilerParams(vmem_limit_bytes=16 * 1024 * 1024),
        cost_estimate=pl.CostEstimate(flops=30_000_000, bytes_accessed=1_600_000, transcendentals=0),
    )(*parts)


def solution(mesh):
    placed = (
        P("dec", None, "row", None, "section"),
        P("section", None),
        P(),
        P("dec", None, "row", None, None),
        P("dec", None, "row", None, "section"),
        P(),
        P("dec"),
        P(None, None, None, None, "section"),
        P("section"),
        P("section"),
        P("section"),
        P(None, None, None, None, "section"),
        P("section"),
    )
    return jax.shard_map(
        functools.partial(shards, mesh.shape["dec"], mesh.shape["row"]),
        mesh=mesh,
        in_specs=placed,
        out_specs=(
            P("dec", None, "row", None, "section"),
            P("dec", None, "row", None, None),
            P("dec", None, "row", None, "section"),
        ),
        check_vma=False,
    )
```

```python
import functools

import jax
import jax.numpy as jnp
from jax import lax
from jax.experimental import pallas as pl
from jax.experimental.pallas import tpu as pltpu
from jax.sharding import PartitionSpec as P

CZ = 16
GROUP = 16
MESH = pl.DeviceIdType.MESH
F32 = jnp.float32
BF16 = jnp.bfloat16


def shifted(flat, step):
    n = flat.shape[0]
    j = lax.broadcasted_iota(jnp.int32, flat.shape, 0) % 8
    if step < 0:
        return jnp.where(j == 0, 0.0, pltpu.roll(flat, 1, 0))
    return jnp.where(j == 7, 0.0, pltpu.roll(flat, n - 1, 0))


def kernel(
    n_dec,
    n_row,
    hidden,
    head_t,
    head_bias,
    lat,
    mid,
    moves,
    span,
    cw,
    cb,
    gain,
    gbias,
    midw,
    midb,
    decoded,
    new_lat,
    new_mid,
    dec_v,
    nl_v,
    nm_v,
    lat_pk,
    hid_v,
    midw_v,
    part,
    part_x,
    part_h,
    lat_all,
    lat_own,
    lat_h,
    cw_in,
    par_all,
    wide,
    z,
    h1,
    stats,
    stats_in,
    gm0,
    gm1,
    sel,
    pm,
    mb,
    acc,
    local_sem,
    lat_s,
    lat_r,
    mid_s,
    mid_r,
    hop_s,
    hop_r,
    w_s,
    w_r,
    part_s,
    part_r,
    lh_s,
    lh_r,
    st_s,
    st_r,
    pm_s,
    pm_r,
):
    s = lax.axis_index("section")
    d = lax.axis_index("dec")
    r = lax.axis_index("row")
    o = 1 - s
    lanes = pl.ds(pl.multiple_of(s * 256, 256), 256)
    olanes = pl.ds(pl.multiple_of(o * 256, 256), 256)
    has_up = r > 0
    has_down = r < n_row - 1

    barrier = pltpu.get_barrier_semaphore()

    def greet(dev):
        pl.semaphore_signal(barrier, inc=1, device_id=dev, device_id_type=MESH)

    greet((o, d, r))
    for k in range(1, n_dec):
        greet((s, lax.rem(d + k, n_dec), r))
    for k in range(1, n_row):
        greet((s, d, lax.rem(r + k, n_row)))
        greet((o, d, lax.rem(r + k, n_row)))

    load_hidden = pltpu.make_async_copy(hidden, hid_v, local_sem.at[0])
    load_hidden.start()
    gm = (gm0, gm1)
    own_mid = [
        pltpu.make_async_copy(mid.at[:, f], gm[f].at[pl.ds(2 * d, 2)], local_sem.at[1 + f])
        for f in range(2)
    ]
    for c in own_mid:
        c.start()
    load_w = pltpu.make_async_copy(midw, midw_v, local_sem.at[3])

    ri = lax.broadcasted_iota(jnp.int32, (CZ, 128), 0)
    ci = lax.broadcasted_iota(jnp.int32, (CZ, 128), 1)
    tile = jnp.where(ci % CZ == ri, 1.0, 0.0).astype(BF16)
    wide_lat = jnp.dot(lat[...].reshape(512, CZ), tile, preferred_element_type=F32)
    wide_lat = wide_lat.reshape(2, 2, 4, 2, 16, 128)
    lane6 = lax.broadcasted_iota(jnp.int32, (2, 4, 16, 128), 3) // 32
    merged = jnp.where(
        lane6 == 0,
        wide_lat[:, 0, :, 0],
        jnp.where(lane6 == 1, wide_lat[:, 0, :, 1], jnp.where(lane6 == 2, wide_lat[:, 1, :, 0], wide_lat[:, 1, :, 1])),
    )
    merged = merged.reshape(128, 128).astype(BF16)
    ri = lax.broadcasted_iota(jnp.int32, (64, 128), 0)
    ci = lax.broadcasted_iota(jnp.int32, (64, 128), 1)
    halves = [
        jnp.dot(
            jnp.where(ci == ri // 8 * 16 + 2 * (ri % 8) + q, 1.0, 0.0).astype(BF16),
            merged,
            preferred_element_type=F32,
        )
        for q in range(2)
    ]
    lat_pk[...] = (
        jnp.where(ci // 16 % 2 == 0, halves[0], halves[1]).astype(BF16).reshape(2, 32, 128)
    )

    zero_slab = jnp.zeros((CZ, 256), BF16)

    def build(source, target):
        def one(a, carry):
            for pp in range(2):
                for qq in range(2):
                    for pos in range(16):
                        di, dj, p, q = pos // 8, pos // 4 % 2, pos // 2 % 2, pos % 2
                        b = 2 * di + p - 1 + pp
                        e = 2 * dj + q - 1 + qq
                        if 0 <= b < 3 and 0 <= e < 3:
                            slab = source[a * 9 + b * 3 + e]
                        else:
                            slab = zero_slab
                        wide[pp * 2 + qq, a, pl.ds(pos * 16, 16), target] = slab
            return carry

        lax.fori_loop(0, 3, one, 0)

    build(cw, lanes)

    pl.semaphore_wait(barrier, 1 + (n_dec - 1) + 2 * (n_row - 1))

    def remote(src, dst, ssem, rsem, dev):
        return pltpu.make_async_remote_copy(
            src_ref=src, dst_ref=dst, send_sem=ssem, recv_sem=rsem, device_id=dev, device_id_type=MESH
        )

    def lat_copy(k, origin):
        return remote(
            lat_pk, lat_all.at[pl.ds(2 * origin, 2)], lat_s.at[k - 1], lat_r.at[k - 1],
            (s, lax.rem(d + k, n_dec), r),
        )

    def mid_copy(k, origin, f):
        return remote(
            mid.at[:, f], gm[f].at[pl.ds(2 * origin, 2)], mid_s.at[k - 1, f], mid_r.at[k - 1, f],
            (s, lax.rem(d + k, n_dec), r),
        )

    line = n_dec == 4
    inner = (d == 1) | (d == 2)
    end = 3 * (d - 1)
    near = 1 + d // 3

    def end_copy(f):
        return remote(
            mid.at[:, f], gm[f].at[pl.ds(2 * d, 2)], hop_s.at[0, f], hop_r.at[0, f], (s, near, r)
        )

    def cross_copy(f):
        return remote(
            mid.at[:, f], gm[f].at[pl.ds(2 * d, 2)], hop_s.at[1, f], hop_r.at[1, f], (s, 3 - d, r)
        )

    def pass_copy(f):
        slots = pl.ds(2 * end, 2)
        return remote(
            gm[f].at[slots], gm[f].at[slots], hop_s.at[2, f], hop_r.at[2, f], (s, 3 - d, r)
        )

    def pick_copy(f, target):
        return remote(sel.at[f], sel.at[f], hop_s.at[3, f], hop_r.at[3, f], (s, target, r))

    def pass_on(f):
        if line:

            @pl.when(inner)
            def _():
                end_copy(f).wait_recv()
                pass_copy(f).start()

    for k in range(1, n_dec):
        lat_copy(k, d).start()

    half = lax.rem(r, 2)
    half_lanes = pl.ds(pl.multiple_of(half * 128, 128), 128)
    cw_copy = remote(
        cw.at[:, :, half_lanes], cw_in.at[:, :, half_lanes], w_s.at[0], w_r.at[0], (o, d, r)
    )
    cw_copy.start()
    cw_pass = remote(
        cw_in.at[:, :, half_lanes], cw_in.at[:, :, half_lanes], w_s.at[4], w_r.at[4],
        (s, d, r + 1 - 2 * half),
    )
    par_copies = [
        remote(ref, par_all.at[n, :, lanes], w_s.at[n + 1], w_r.at[n + 1], (o, d, r))
        for n, ref in enumerate((cb, gain, gbias))
    ]
    for c in par_copies:
        c.start()
    if line:

        @pl.when(inner)
        def _():
            for f in (1, 0):
                cross_copy(f).start()

        @pl.when(jnp.logical_not(inner))
        def _():
            for f in (1, 0):
                end_copy(f).start()

    else:
        for k in range(1, n_dec):
            for f in (1, 0):
                mid_copy(k, d, f).start()

    load_hidden.wait()
    load_w.start()
    head = lax.dot_general(
        hid_v[...],
        jnp.concatenate([head_t[...], jnp.zeros_like(head_t)], axis=0),
        (((1,), (1,)), ((), ())),
        preferred_element_type=F32,
    )
    head = head.reshape(2, 4, 4, 8, 128)
    lane = lax.broadcasted_iota(jnp.int32, (4, 8, 128), 2)
    for t in range(2):
        for st in range(2):
            high = pltpu.roll(head[st, t + 2].reshape(32, 128), 64, 1).reshape(4, 8, 128)
            part[t, :, pl.ds(8 * st, 8), :] = jnp.where(lane < 64, head[st, t], high)

    def part_copies():
        full = remote(part, part_x, part_s.at[0], part_r.at[0], (o, d, r))
        up = [
            remote(part.at[:, 0], part_h.at[1, n], part_s.at[1 + n], part_r.at[1 + n], (dev, d, r - 1))
            for n, dev in enumerate((s, o))
        ]
        down = [
            remote(part.at[:, 3], part_h.at[0, n], part_s.at[3 + n], part_r.at[3 + n], (dev, d, r + 1))
            for n, dev in enumerate((s, o))
        ]
        return full, up, down

    full, up, down = part_copies()

    @pl.when(has_up)
    def _():
        for c in up:
            c.start()

    @pl.when(has_down)
    def _():
        for c in down:
            c.start()

    full.start()

    lat_all[pl.ds(2 * d, 2)] = lat_pk[...]
    for n, ref in enumerate((cb, gain, gbias)):
        par_all[n, :, lanes] = ref[...]

    for k in range(1, n_dec):
        lat_copy(k, lax.rem(d + n_dec - k, n_dec)).wait_recv()
    for st in range(2):
        live = (span[st] > 0).astype(F32)
        x = lat_all[moves[2 * d + st]].astype(F32) * live
        lat_own[:, pl.ds(8 * st, 8), :] = x.reshape(4, 8, 128)
    lat_edge_up = remote(lat_own.at[0], lat_h.at[1], lh_s.at[0], lh_r.at[0], (s, d, r - 1))
    lat_edge_down = remote(lat_own.at[3], lat_h.at[0], lh_s.at[1], lh_r.at[1], (s, d, r + 1))

    @pl.when(has_up)
    def _():
        lat_edge_up.start()

    @pl.when(has_down)
    def _():
        lat_edge_down.start()

    cw_copy.wait_recv()
    cw_pass.start()
    for n, ref in enumerate((cb, gain, gbias)):
        remote(ref, par_all.at[n, :, olanes], w_s.at[n + 1], w_r.at[n + 1], (o, d, r)).wait_recv()
    cw_pass.wait_recv()
    build(cw_in, olanes)
    pass_on(1)

    full.wait_recv()

    @pl.when(has_up)
    def _():
        for c in down:
            c.wait_recv()
        lat_edge_down.wait_recv()

    @pl.when(has_down)
    def _():
        for c in up:
            c.wait_recv()
        lat_edge_up.wait_recv()

    bias = jnp.concatenate([head_bias[...], head_bias[...]], axis=1)

    def place(low, base, step, packed):
        count = packed.shape[0]
        flat = packed.astype(BF16).astype(F32).reshape(count * 16, 128)
        lane = lax.broadcasted_iota(jnp.int32, flat.shape, 1) < 64
        turn = pltpu.roll(flat, 64, 1)
        before = shifted(flat, -1)
        after = shifted(flat, 1)
        turn_before = pltpu.roll(before, 64, 1)
        turn_after = pltpu.roll(after, 64, 1)
        for q, frame, left, right in (
            (0, base, before, turn),
            (0, base + step, turn_before, flat),
            (1, base, flat, turn_after),
            (1, base + step, turn, after),
        ):
            z[q, frame, pl.ds(low, count)] = (
                jnp.where(lane, left, right).astype(BF16).reshape(count, 16, 128)
            )

    up_live = has_up.astype(F32)
    down_live = has_down.astype(F32)

    @pl.when(jnp.logical_not(has_up))
    def _():
        part_h[0] = jnp.zeros((2, 2, 16, 128), F32)
        lat_h[0] = jnp.zeros((16, 128), F32)

    @pl.when(jnp.logical_not(has_down))
    def _():
        part_h[1] = jnp.zeros((2, 2, 16, 128), F32)
        lat_h[1] = jnp.zeros((16, 128), F32)

    for t in range(2):
        own = part[t] + part_x[t] + bias
        nl_v[t] = own.astype(BF16)
        place(1, 2 + t, 2, own)
        place(0, 2 + t, 2, ((part_h[0, 0, t] + part_h[0, 1, t] + bias) * up_live)[None])
        place(5, 2 + t, 2, ((part_h[1, 0, t] + part_h[1, 1, t] + bias) * down_live)[None])
    place(1, 0, 1, lat_own[...])
    place(0, 0, 1, lat_h[0][None])
    place(5, 0, 1, lat_h[1][None])

    out_lat = pltpu.make_async_copy(nl_v, new_lat, local_sem.at[4])
    out_lat.start()

    conv_bias = par_all[0]

    def input_conv(pp, qq, row, count):
        out = jnp.zeros((64 * count, 512), F32)
        for a in range(3):
            lhs = jnp.concatenate(
                [
                    z[qq, a : a + 4, row + di : row + di + count].reshape(64 * count, 128)
                    for di in range(2)
                ],
                axis=1,
            )
            out = out + jnp.dot(lhs, wide[pp * 2 + qq, a], preferred_element_type=F32)
        first = (out + conv_bias).astype(BF16)
        h1[pp * 2 + qq, :, row : row + count] = first.reshape(4, count, 16, 512)
        return first

    total = jnp.zeros((16, 512), F32)
    square = jnp.zeros((16, 512), F32)
    for pp in range(2):
        if pp == 1:
            pass_on(0)
        for qq in range(2):
            mine = input_conv(pp, qq, pp, 4).astype(F32).reshape(16, 16, 512)
            total = total + jnp.sum(mine, axis=0)
            square = square + jnp.sum(mine * mine, axis=0)
    stats[...] = jnp.concatenate(
        [
            jnp.sum(total[0:8], axis=0, keepdims=True),
            jnp.sum(total[8:16], axis=0, keepdims=True),
            jnp.sum(square[0:8], axis=0, keepdims=True),
            jnp.sum(square[8:16], axis=0, keepdims=True),
            jnp.zeros((4, 512), F32),
        ],
        axis=0,
    )
    stat_copies = [
        remote(stats, stats_in.at[k - 1], st_s.at[k - 1], st_r.at[k - 1], (s, d, lax.rem(r + k, n_row)))
        for k in range(1, n_row)
    ]
    for c in stat_copies:
        c.start()
    for pp in range(2):
        for qq in range(2):
            input_conv(pp, qq, 0 if pp == 1 else 4, 1)

    zero_row = jnp.zeros((2, 32, 512), BF16)

    @pl.when(jnp.logical_not(has_up))
    def _():
        pm[:, 0] = zero_row

    @pl.when(jnp.logical_not(has_down))
    def _():
        pm[:, 9] = zero_row

    def pm_full(f):
        block = pm.at[f, 1:9, :, lanes]
        return remote(block, block, pm_s.at[f, 0], pm_r.at[f, 0], (o, d, r))

    def pm_up(f):
        return [
            remote(pm.at[f, 1, :, lanes], pm.at[f, 9, :, lanes], pm_s.at[f, 1 + n], pm_r.at[f, 1 + n], (dev, d, r - 1))
            for n, dev in enumerate((s, o))
        ]

    def pm_down(f):
        return [
            remote(pm.at[f, 8, :, lanes], pm.at[f, 0, :, lanes], pm_s.at[f, 3 + n], pm_r.at[f, 3 + n], (dev, d, r + 1))
            for n, dev in enumerate((s, o))
        ]

    def share(f, pick):
        for st in range(2):
            live = (span[st] > 0).astype(BF16)
            pm[f, 1:9, pl.ds(16 * st, 16), lanes] = pick(st) * live
        pm_full(f).start()

        @pl.when(has_up)
        def _():
            for c in pm_up(f):
                c.start()

        @pl.when(has_down)
        def _():
            for c in pm_down(f):
                c.start()

    def share_inner(f):
        if line:

            @pl.when(inner)
            def _():
                own_mid[f].wait()
                cross_copy(f).wait_recv()
                pass_copy(f).wait_recv()
                for st in range(2):
                    sel[f, :, pl.ds(16 * st, 16), :] = gm[f][moves[2 * end + st]]
                pick_copy(f, end).start()
                share(f, lambda st: gm[f][moves[2 * d + st]])

    def share_end(f):
        if line:

            @pl.when(jnp.logical_not(inner))
            def _():
                pick_copy(f, near).wait_recv()
                share(f, lambda st: sel[f, :, pl.ds(16 * st, 16), :])

        else:
            own_mid[f].wait()
            for k in range(1, n_dec):
                mid_copy(k, lax.rem(d + n_dec - k, n_dec), f).wait_recv()
            share(f, lambda st: gm[f][moves[2 * d + st]])

    share_inner(1)
    for c in stat_copies:
        c.wait_recv()
    sums = stats[...]
    for k in range(1, n_row):
        sums = sums + stats_in[k - 1]
    lane8 = lax.broadcasted_iota(jnp.int32, (8, 512), 1)
    for k in (1, 2, 4, 8):
        other = jnp.where((lane8 & k) > 0, pltpu.roll(sums, k, 1), pltpu.roll(sums, 512 - k, 1))
        sums = sums + other
    sums = sums / (4 * 8 * 16 * GROUP * n_row)
    gv = sums[2:4] - sums[0:2] * sums[0:2]
    scale = lax.rsqrt(gv + 1e-5) * par_all[1]
    shift = par_all[2]

    def spread(v):
        return jnp.concatenate(
            [jnp.broadcast_to(v[0:1], (8, 512)), jnp.broadcast_to(v[1:2], (8, 512))], axis=0
        )

    mean16 = spread(sums[0:2])
    scale16 = spread(scale)

    def activate(t, carry):
        for pp in range(2):
            for qq in range(2):
                v = (h1[pp * 2 + qq, t].astype(F32) - mean16) * scale16 + shift
                v = v * (0.5 * jnp.tanh(0.5 * v) + 0.5)
                edge = lax.broadcasted_iota(jnp.int32, (5, 16, 512), 0)
                if pp == 1:
                    v = jnp.where((edge == 0) & jnp.logical_not(has_up), 0.0, v)
                else:
                    v = jnp.where((edge == 4) & jnp.logical_not(has_down), 0.0, v)
                v = v.astype(BF16)
                mb[pp, qq, t + 2] = v
                moved = shifted(v.astype(F32).reshape(80, 512), -1 if qq == 1 else 1)
                mb[pp, 2 if qq == 1 else 3, t + 2] = moved.astype(BF16).reshape(5, 16, 512)
        return carry

    lax.fori_loop(0, 4, activate, 0)

    acc[...] = jnp.zeros_like(acc)

    def conv(b, pairs):
        for a, t0, nt in pairs:
            pieces = []
            for pp in range(2):
                src = (b + 1) % 2 if pp == 0 else b % 2
                off = b // 2 if pp == 0 else (b + 1) // 2
                for qq in range(2):
                    taps = (2, 0, 1) if qq == 0 else (0, 1, 3)
                    pieces.append(
                        jnp.concatenate(
                            [
                                mb[src, var, t0 + a : t0 + a + nt, pl.ds(off, 4)].reshape(nt * 64, 512)
                                for var in taps
                            ],
                            axis=1,
                        )
                    )
            lhs = jnp.concatenate(pieces, axis=0)
            got = jnp.dot(lhs, midw_v[a * 3 + b], preferred_element_type=F32)
            acc[:, t0 : t0 + nt] += got.reshape(4, nt, 64, 256)

    share_inner(0)
    load_w.wait()

    def tap_late(b, carry):
        conv(b, ((2, 0, 4),))
        return carry

    lax.fori_loop(0, 1, tap_late, 0)
    share_end(1)
    lax.fori_loop(1, 2, tap_late, 0)
    share_end(0)
    lax.fori_loop(2, 3, tap_late, 0)

    def tap_mid(k, carry):
        conv(k, ((1, 1, 3), (0, 2, 2)))
        return carry

    lax.fori_loop(0, 3, tap_mid, 0)

    ro = lax.broadcasted_iota(jnp.int32, (64, 32), 0)
    co = lax.broadcasted_iota(jnp.int32, (64, 32), 1)
    v4 = ro // 16
    j2 = 2 * (ro % 8)
    col = jnp.where(v4 == 0, j2, jnp.where(v4 == 1, j2 + 1, jnp.where(v4 == 2, j2 - 1, j2 + 2)))
    fits = (col >= 0) & (col < 16) & (co == (ro // 8) % 2 * 16 + col)
    deal = jnp.where(fits, 1.0, 0.0).astype(BF16)

    for t in range(2):
        for pp in range(2):
            for qq in range(2):
                nm_v[t, pp, :, pl.ds(16 * qq, 16), :] = mb[pp, qq, t + 4, pp : pp + 4, :, lanes]
    out_mid = pltpu.make_async_copy(nm_v, new_mid, local_sem.at[5])
    out_mid.start()

    def finish(t, carry):
        for pp in range(2):
            for qq in range(2):
                y = (
                    h1[pp * 2 + qq, t, pp : pp + 4, :, lanes].astype(F32)
                    + acc[pp * 2 + qq, t].reshape(4, 16, 256)
                    + midb[...]
                )
                dec_v[t, pp, :, pl.ds(16 * qq, 16), :] = y.astype(BF16)
        return carry

    lax.fori_loop(2, 4, finish, 0)
    out_late = pltpu.make_async_copy(
        dec_v.at[pl.ds(2, 2)], decoded.at[pl.ds(2, 2)], local_sem.at[6]
    )
    out_late.start()

    for f, pairs in ((1, ((1, 0, 1), (0, 1, 1))), (0, ((0, 0, 1),))):
        pm_full(f).wait_recv()

        @pl.when(has_up)
        def _():
            for c in pm_down(f):
                c.wait_recv()

        @pl.when(has_down)
        def _():
            for c in pm_up(f):
                c.wait_recv()

        for row in range(10):
            y = jnp.dot(deal, pm[f, row], preferred_element_type=F32).astype(BF16)
            for v in range(4):
                mb[(row + 1) % 2, v, f, row // 2] = y[16 * v : 16 * v + 16]

        def tap_early(b, carry):
            conv(b, pairs)
            return carry

        lax.fori_loop(0, 3, tap_early, 0)

    lax.fori_loop(0, 2, finish, 0)
    out_early = pltpu.make_async_copy(
        dec_v.at[pl.ds(0, 2)], decoded.at[pl.ds(0, 2)], local_sem.at[7]
    )
    out_early.start()

    for k in range(1, n_dec):
        lat_copy(k, d).wait_send()
    for c in par_copies + stat_copies + [full, cw_copy, cw_pass, pm_full(0), pm_full(1)]:
        c.wait_send()
    if line:

        @pl.when(inner)
        def _():
            for f in range(2):
                cross_copy(f).wait_send()
                pass_copy(f).wait_send()
                pick_copy(f, end).wait_send()

        @pl.when(jnp.logical_not(inner))
        def _():
            for f in range(2):
                end_copy(f).wait_send()
                own_mid[f].wait()

    else:
        for k in range(1, n_dec):
            for f in range(2):
                mid_copy(k, d, f).wait_send()

    @pl.when(has_up)
    def _():
        for c in up + pm_up(0) + pm_up(1) + [lat_edge_up]:
            c.wait_send()

    @pl.when(has_down)
    def _():
        for c in down + pm_down(0) + pm_down(1) + [lat_edge_down]:
            c.wait_send()
    for c in (out_lat, out_mid, out_late, out_early):
        c.wait()


def weave_kernel(
    decoded_in, new_lat_in, new_mid_in, decoded_out, new_lat_out, new_mid_out, decoded, new_lat, new_mid, sem
):
    loads = [
        pltpu.make_async_copy(source, target, sem.at[n])
        for n, (source, target) in enumerate(
            ((new_lat_in, new_lat), (new_mid_in, new_mid), (decoded_in, decoded))
        )
    ]
    for c in loads:
        c.start()
    ro = lax.broadcasted_iota(jnp.int32, (32, 32), 0)
    co = lax.broadcasted_iota(jnp.int32, (32, 32), 1)
    weave = jnp.where(co == (ro % 2) * 16 + (ro // 16) * 8 + (ro % 16) // 2, 1.0, 0.0).astype(BF16)

    def spread(source, target, t):
        for pp in range(2):
            for i in range(4):
                y = jnp.dot(weave, source[t, pp, i], preferred_element_type=F32).astype(BF16)
                target[0, t, 2 * i + pp] = y[0:16]
                target[1, t, 2 * i + pp] = y[16:32]

    loads[0].wait()
    patches = new_lat[...].reshape(128, 128)
    ro = lax.broadcasted_iota(jnp.int32, (256, 128), 0)
    co = lax.broadcasted_iota(jnp.int32, (256, 128), 1)
    grown = [
        jnp.dot(
            jnp.where((co == ro // 16 * 8 + ro % 16 // 2) & (ro % 2 == q), 1.0, 0.0).astype(BF16),
            patches,
            preferred_element_type=F32,
        )
        for q in range(2)
    ]
    grown = jnp.where(co // 16 % 2 == 0, grown[0], grown[1])
    ro = lax.broadcasted_iota(jnp.int32, (128, CZ), 0)
    for p in range(2):
        fold = (ro // 32 == 2 + p) & (ro % CZ == lax.broadcasted_iota(jnp.int32, (128, CZ), 1))
        y = jnp.dot(
            grown.astype(BF16), jnp.where(fold, 1.0, 0.0).astype(BF16), preferred_element_type=F32
        ).astype(BF16)
        for t in range(2):
            for i in range(4):
                for st in range(2):
                    row = ((t * 4 + i) * 2 + st) * 16
                    new_lat_out[st, t, 2 * i + p] = y[row : row + 16]
    loads[1].wait()
    for t in range(2):
        spread(new_mid, new_mid_out, t)
    loads[2].wait()
    for t in range(4):
        spread(decoded, decoded_out, t)


def shards(
    n_dec,
    n_row,
    hidden,
    head_weight,
    head_bias,
    lat_cache,
    mid_cache,
    moves,
    span_index,
    conv_in_weight,
    conv_in_bias,
    gn_gain,
    gn_bias,
    mid_weight,
    mid_bias,
):
    slots = n_dec * 2
    depth = hidden.shape[-1]
    vm = pl.BlockSpec(memory_space=pltpu.VMEM)
    sm = pl.BlockSpec(memory_space=pltpu.SMEM)
    hbm = pl.BlockSpec(memory_space=pl.ANY)
    dma = pltpu.SemaphoreType.DMA
    parts = pl.pallas_call(
        functools.partial(kernel, n_dec, n_row),
        out_shape=(
            jax.ShapeDtypeStruct((4, 2, 4, 32, 256), BF16),
            jax.ShapeDtypeStruct((2, 4, 16, 128), BF16),
            jax.ShapeDtypeStruct((2, 2, 4, 32, 256), BF16),
        ),
        in_specs=[hbm, vm, vm, vm, hbm, sm, sm, vm, vm, vm, vm, hbm, vm],
        out_specs=(hbm, hbm, hbm),
        scratch_shapes=[
            pltpu.VMEM((4, 2, 4, 32, 256), BF16),
            pltpu.VMEM((2, 4, 16, 128), BF16),
            pltpu.VMEM((2, 2, 4, 32, 256), BF16),
            pltpu.VMEM((2, 32, 128), BF16),
            pltpu.VMEM((256, depth), BF16),
            pltpu.VMEM((9, 1536, 256), BF16),
            pltpu.VMEM((2, 4, 16, 128), F32),
            pltpu.VMEM((2, 4, 16, 128), F32),
            pltpu.VMEM((2, 2, 2, 16, 128), F32),
            pltpu.VMEM((slots, 32, 128), BF16),
            pltpu.VMEM((4, 16, 128), F32),
            pltpu.VMEM((2, 16, 128), F32),
            pltpu.VMEM((27, CZ, 256), BF16),
            pltpu.VMEM((3, 1, 512), F32),
            pltpu.VMEM((4, 3, 256, 512), BF16),
            pltpu.VMEM((2, 6, 6, 16, 128), BF16),
            pltpu.VMEM((4, 4, 5, 16, 512), BF16),
            pltpu.VMEM((8, 512), F32),
            pltpu.VMEM((n_row - 1, 8, 512), F32),
            pltpu.VMEM((slots, 8, 16, 256), BF16),
            pltpu.VMEM((slots, 8, 16, 256), BF16),
            pltpu.VMEM((2, 8, 32, 256), BF16),
            pltpu.VMEM((2, 10, 32, 512), BF16),
            pltpu.VMEM((2, 4, 6, 5, 16, 512), BF16),
            pltpu.VMEM((4, 4, 64, 256), F32),
            dma((8,)),
            dma((n_dec - 1,)),
            dma((n_dec - 1,)),
            dma((n_dec - 1, 2)),
            dma((n_dec - 1, 2)),
            dma((4, 2)),
            dma((4, 2)),
            dma((5,)),
            dma((5,)),
            dma((5,)),
            dma((5,)),
            dma((2,)),
            dma((2,)),
            dma((n_row - 1,)),
            dma((n_row - 1,)),
            dma((2, 5)),
            dma((2, 5)),
        ],
        compiler_params=pltpu.CompilerParams(
            collective_id=0, has_side_effects=True, vmem_limit_bytes=56 * 1024 * 1024
        ),
        cost_estimate=pl.CostEstimate(
            flops=9_000_000_000, bytes_accessed=12_000_000, transcendentals=700_000
        ),
    )(
        hidden.reshape(256, depth),
        head_weight.T,
        head_bias.reshape(1, 64),
        lat_cache,
        mid_cache,
        moves,
        span_index,
        conv_in_weight.reshape(27, CZ, 256),
        conv_in_bias.reshape(1, 256),
        gn_gain.reshape(1, 256),
        gn_bias.reshape(1, 256),
        mid_weight.reshape(9, 1536, 256),
        mid_bias.reshape(1, 256),
    )
    return pl.pallas_call(
        weave_kernel,
        out_shape=(
            jax.ShapeDtypeStruct((2, 4, 8, 16, 256), BF16),
            jax.ShapeDtypeStruct((2, 2, 8, 16, CZ), BF16),
            jax.ShapeDtypeStruct((2, 2, 8, 16, 256), BF16),
        ),
        in_specs=[hbm, hbm, hbm],
        out_specs=(vm, vm, vm),
        scratch_shapes=[
            pltpu.VMEM((4, 2, 4, 32, 256), BF16),
            pltpu.VMEM((2, 4, 16, 128), BF16),
            pltpu.VMEM((2, 2, 4, 32, 256), BF16),
            dma((3,)),
        ],
        compiler_params=pltpu.CompilerParams(vmem_limit_bytes=60 * 1024 * 1024),
        cost_estimate=pl.CostEstimate(flops=30_000_000, bytes_accessed=1_600_000, transcendentals=0),
    )(*parts)


def solution(mesh):
    placed = (
        P("dec", None, "row", None, "section"),
        P("section", None),
        P(),
        P("dec", None, "row", None, None),
        P("dec", None, "row", None, "section"),
        P(),
        P("dec"),
        P(None, None, None, None, "section"),
        P("section"),
        P("section"),
        P("section"),
        P(None, None, None, None, "section"),
        P("section"),
    )
    return jax.shard_map(
        functools.partial(shards, mesh.shape["dec"], mesh.shape["row"]),
        mesh=mesh,
        in_specs=placed,
        out_specs=(
            P("dec", None, "row", None, "section"),
            P("dec", None, "row", None, None),
            P("dec", None, "row", None, "section"),
        ),
        check_vma=False,
    )
```

```python
import functools

import jax
import jax.numpy as jnp
from jax import lax
from jax.experimental import pallas as pl
from jax.experimental.pallas import tpu as pltpu
from jax.sharding import PartitionSpec as P

CZ = 16
GROUP = 16
MESH = pl.DeviceIdType.MESH
F32 = jnp.float32
BF16 = jnp.bfloat16


def shifted(flat, step):
    n = flat.shape[0]
    j = lax.broadcasted_iota(jnp.int32, flat.shape, 0) % 8
    if step < 0:
        return jnp.where(j == 0, 0.0, pltpu.roll(flat, 1, 0))
    return jnp.where(j == 7, 0.0, pltpu.roll(flat, n - 1, 0))


def kernel(
    n_dec,
    n_row,
    hidden,
    head_t,
    head_bias,
    lat,
    mid,
    moves,
    span,
    cw,
    cb,
    gain,
    gbias,
    midw,
    midb,
    decoded,
    new_lat,
    new_mid,
    dec_v,
    nl_v,
    nm_v,
    lat_pk,
    hid_v,
    midw_v,
    part,
    part_x,
    part_h,
    lat_all,
    lat_own,
    lat_h,
    cw_in,
    par_all,
    wide,
    z,
    h1,
    stats,
    stats_in,
    gm0,
    gm1,
    sel,
    pm,
    mb,
    acc,
    local_sem,
    lat_s,
    lat_r,
    mid_s,
    mid_r,
    hop_s,
    hop_r,
    w_s,
    w_r,
    part_s,
    part_r,
    lh_s,
    lh_r,
    st_s,
    st_r,
    pm_s,
    pm_r,
):
    s = lax.axis_index("section")
    d = lax.axis_index("dec")
    r = lax.axis_index("row")
    o = 1 - s
    lanes = pl.ds(pl.multiple_of(s * 256, 256), 256)
    olanes = pl.ds(pl.multiple_of(o * 256, 256), 256)
    has_up = r > 0
    has_down = r < n_row - 1

    barrier = pltpu.get_barrier_semaphore()

    def greet(dev):
        pl.semaphore_signal(barrier, inc=1, device_id=dev, device_id_type=MESH)

    greet((o, d, r))
    for k in range(1, n_dec):
        greet((s, lax.rem(d + k, n_dec), r))
    for k in range(1, n_row):
        greet((s, d, lax.rem(r + k, n_row)))
        greet((o, d, lax.rem(r + k, n_row)))

    load_hidden = pltpu.make_async_copy(hidden, hid_v, local_sem.at[0])
    load_hidden.start()
    gm = (gm0, gm1)
    own_mid = [
        pltpu.make_async_copy(mid.at[:, f], gm[f].at[pl.ds(2 * d, 2)], local_sem.at[1 + f])
        for f in range(2)
    ]
    for c in own_mid:
        c.start()
    load_w = pltpu.make_async_copy(midw, midw_v, local_sem.at[3])

    pl.semaphore_wait(barrier, 1 + (n_dec - 1) + 2 * (n_row - 1))

    def remote(src, dst, ssem, rsem, dev):
        return pltpu.make_async_remote_copy(
            src_ref=src, dst_ref=dst, send_sem=ssem, recv_sem=rsem, device_id=dev, device_id_type=MESH
        )

    def lat_copy(k, origin):
        return remote(
            lat_pk, lat_all.at[pl.ds(2 * origin, 2)], lat_s.at[k - 1], lat_r.at[k - 1],
            (s, lax.rem(d + k, n_dec), r),
        )

    def mid_copy(k, origin, f):
        return remote(
            mid.at[:, f], gm[f].at[pl.ds(2 * origin, 2)], mid_s.at[k - 1, f], mid_r.at[k - 1, f],
            (s, lax.rem(d + k, n_dec), r),
        )

    line = n_dec == 4
    inner = (d == 1) | (d == 2)
    end = 3 * (d - 1)
    near = 1 + d // 3

    def end_copy(f):
        return remote(
            mid.at[:, f], gm[f].at[pl.ds(2 * d, 2)], hop_s.at[0, f], hop_r.at[0, f], (s, near, r)
        )

    def cross_copy(f):
        return remote(
            mid.at[:, f], gm[f].at[pl.ds(2 * d, 2)], hop_s.at[1, f], hop_r.at[1, f], (s, 3 - d, r)
        )

    def pass_copy(f):
        slots = pl.ds(2 * end, 2)
        return remote(
            gm[f].at[slots], gm[f].at[slots], hop_s.at[2, f], hop_r.at[2, f], (s, 3 - d, r)
        )

    def pick_copy(f, target):
        return remote(sel.at[f], sel.at[f], hop_s.at[3, f], hop_r.at[3, f], (s, target, r))

    def pass_on(f):
        if line:

            @pl.when(inner)
            def _():
                end_copy(f).wait_recv()
                pass_copy(f).start()

    half = lax.rem(r, 2)
    half_lanes = pl.ds(pl.multiple_of(half * 128, 128), 128)
    cw_copy = remote(
        cw.at[:, :, half_lanes], cw_in.at[:, :, half_lanes], w_s.at[0], w_r.at[0], (o, d, r)
    )
    cw_copy.start()
    cw_pass = remote(
        cw_in.at[:, :, half_lanes], cw_in.at[:, :, half_lanes], w_s.at[4], w_r.at[4],
        (s, d, r + 1 - 2 * half),
    )
    par_copies = [
        remote(ref, par_all.at[n, :, lanes], w_s.at[n + 1], w_r.at[n + 1], (o, d, r))
        for n, ref in enumerate((cb, gain, gbias))
    ]
    for c in par_copies:
        c.start()
    ri = lax.broadcasted_iota(jnp.int32, (CZ, 128), 0)
    ci = lax.broadcasted_iota(jnp.int32, (CZ, 128), 1)
    tile = jnp.where(ci % CZ == ri, 1.0, 0.0).astype(BF16)
    wide_lat = jnp.dot(lat[...].reshape(512, CZ), tile, preferred_element_type=F32)
    wide_lat = wide_lat.reshape(2, 2, 4, 2, 16, 128)
    lane6 = lax.broadcasted_iota(jnp.int32, (2, 4, 16, 128), 3) // 32
    merged = jnp.where(
        lane6 == 0,
        wide_lat[:, 0, :, 0],
        jnp.where(lane6 == 1, wide_lat[:, 0, :, 1], jnp.where(lane6 == 2, wide_lat[:, 1, :, 0], wide_lat[:, 1, :, 1])),
    )
    merged = merged.reshape(128, 128).astype(BF16)
    ri = lax.broadcasted_iota(jnp.int32, (64, 128), 0)
    ci = lax.broadcasted_iota(jnp.int32, (64, 128), 1)
    halves = [
        jnp.dot(
            jnp.where(ci == ri // 8 * 16 + 2 * (ri % 8) + q, 1.0, 0.0).astype(BF16),
            merged,
            preferred_element_type=F32,
        )
        for q in range(2)
    ]
    lat_pk[...] = (
        jnp.where(ci // 16 % 2 == 0, halves[0], halves[1]).astype(BF16).reshape(2, 32, 128)
    )

    for k in range(1, n_dec):
        lat_copy(k, d).start()

    if line:

        @pl.when(inner)
        def _():
            for f in (1, 0):
                cross_copy(f).start()

        @pl.when(jnp.logical_not(inner))
        def _():
            for f in (1, 0):
                end_copy(f).start()

    else:
        for k in range(1, n_dec):
            for f in (1, 0):
                mid_copy(k, d, f).start()

    load_hidden.wait()
    load_w.start()
    head = lax.dot_general(
        hid_v[...],
        jnp.concatenate([head_t[...], jnp.zeros_like(head_t)], axis=0),
        (((1,), (1,)), ((), ())),
        preferred_element_type=F32,
    )
    head = head.reshape(2, 4, 4, 8, 128)
    lane = lax.broadcasted_iota(jnp.int32, (4, 8, 128), 2)
    for t in range(2):
        for st in range(2):
            high = pltpu.roll(head[st, t + 2].reshape(32, 128), 64, 1).reshape(4, 8, 128)
            part[t, :, pl.ds(8 * st, 8), :] = jnp.where(lane < 64, head[st, t], high)

    def part_copies():
        full = remote(part, part_x, part_s.at[0], part_r.at[0], (o, d, r))
        up = [
            remote(part.at[:, 0], part_h.at[1, n], part_s.at[1 + n], part_r.at[1 + n], (dev, d, r - 1))
            for n, dev in enumerate((s, o))
        ]
        down = [
            remote(part.at[:, 3], part_h.at[0, n], part_s.at[3 + n], part_r.at[3 + n], (dev, d, r + 1))
            for n, dev in enumerate((s, o))
        ]
        return full, up, down

    full, up, down = part_copies()

    @pl.when(has_up)
    def _():
        for c in up:
            c.start()

    @pl.when(has_down)
    def _():
        for c in down:
            c.start()

    full.start()

    zero_slab = jnp.zeros((CZ, 256), BF16)

    def build(source, target):
        def one(a, carry):
            for pp in range(2):
                for qq in range(2):
                    for pos in range(16):
                        di, dj, p, q = pos // 8, pos // 4 % 2, pos // 2 % 2, pos % 2
                        b = 2 * di + p - 1 + pp
                        e = 2 * dj + q - 1 + qq
                        if 0 <= b < 3 and 0 <= e < 3:
                            slab = source[a * 9 + b * 3 + e]
                        else:
                            slab = zero_slab
                        wide[pp * 2 + qq, a, pl.ds(pos * 16, 16), target] = slab
            return carry

        lax.fori_loop(0, 3, one, 0)

    build(cw, lanes)
    lat_all[pl.ds(2 * d, 2)] = lat_pk[...]
    for n, ref in enumerate((cb, gain, gbias)):
        par_all[n, :, lanes] = ref[...]

    for k in range(1, n_dec):
        lat_copy(k, lax.rem(d + n_dec - k, n_dec)).wait_recv()
    for st in range(2):
        live = (span[st] > 0).astype(F32)
        x = lat_all[moves[2 * d + st]].astype(F32) * live
        lat_own[:, pl.ds(8 * st, 8), :] = x.reshape(4, 8, 128)
    lat_edge_up = remote(lat_own.at[0], lat_h.at[1], lh_s.at[0], lh_r.at[0], (s, d, r - 1))
    lat_edge_down = remote(lat_own.at[3], lat_h.at[0], lh_s.at[1], lh_r.at[1], (s, d, r + 1))

    @pl.when(has_up)
    def _():
        lat_edge_up.start()

    @pl.when(has_down)
    def _():
        lat_edge_down.start()

    cw_copy.wait_recv()
    cw_pass.start()
    pass_on(1)

    full.wait_recv()

    @pl.when(has_up)
    def _():
        for c in down:
            c.wait_recv()
        lat_edge_down.wait_recv()

    @pl.when(has_down)
    def _():
        for c in up:
            c.wait_recv()
        lat_edge_up.wait_recv()

    bias = jnp.concatenate([head_bias[...], head_bias[...]], axis=1)

    def place(low, base, step, packed):
        count = packed.shape[0]
        flat = packed.astype(BF16).astype(F32).reshape(count * 16, 128)
        lane = lax.broadcasted_iota(jnp.int32, flat.shape, 1) < 64
        turn = pltpu.roll(flat, 64, 1)
        before = shifted(flat, -1)
        after = shifted(flat, 1)
        turn_before = pltpu.roll(before, 64, 1)
        turn_after = pltpu.roll(after, 64, 1)
        for q, frame, left, right in (
            (0, base, before, turn),
            (0, base + step, turn_before, flat),
            (1, base, flat, turn_after),
            (1, base + step, turn, after),
        ):
            z[q, frame, pl.ds(low, count)] = (
                jnp.where(lane, left, right).astype(BF16).reshape(count, 16, 128)
            )

    up_live = has_up.astype(F32)
    down_live = has_down.astype(F32)

    @pl.when(jnp.logical_not(has_up))
    def _():
        part_h[0] = jnp.zeros((2, 2, 16, 128), F32)
        lat_h[0] = jnp.zeros((16, 128), F32)

    @pl.when(jnp.logical_not(has_down))
    def _():
        part_h[1] = jnp.zeros((2, 2, 16, 128), F32)
        lat_h[1] = jnp.zeros((16, 128), F32)

    for t in range(2):
        own = part[t] + part_x[t] + bias
        nl_v[t] = own.astype(BF16)
        place(1, 2 + t, 2, own)
        place(0, 2 + t, 2, ((part_h[0, 0, t] + part_h[0, 1, t] + bias) * up_live)[None])
        place(5, 2 + t, 2, ((part_h[1, 0, t] + part_h[1, 1, t] + bias) * down_live)[None])
    place(1, 0, 1, lat_own[...])
    place(0, 0, 1, lat_h[0][None])
    place(5, 0, 1, lat_h[1][None])

    out_lat = pltpu.make_async_copy(nl_v, new_lat, local_sem.at[4])
    out_lat.start()

    def input_conv(pp, qq, row, count, part_lanes):
        out = jnp.zeros((64 * count, 256), F32)
        for a in range(3):
            lhs = jnp.concatenate(
                [
                    z[qq, a : a + 4, row + di : row + di + count].reshape(64 * count, 128)
                    for di in range(2)
                ],
                axis=1,
            )
            out = out + jnp.dot(lhs, wide[pp * 2 + qq, a, :, part_lanes], preferred_element_type=F32)
        first = (out + par_all[0, :, part_lanes]).astype(BF16)
        h1[pp * 2 + qq, :, row : row + count, :, part_lanes] = first.reshape(4, count, 16, 256)
        return first

    def stat_copies(n):
        return [
            remote(
                stats.at[n], stats_in.at[n, k - 1], st_s.at[n, k - 1], st_r.at[n, k - 1],
                (s, d, lax.rem(r + k, n_row)),
            )
            for k in range(1, n_row)
        ]

    def input_half(n, part_lanes):
        total = jnp.zeros((16, 256), F32)
        square = jnp.zeros((16, 256), F32)
        for pp in range(2):
            for qq in range(2):
                mine = input_conv(pp, qq, pp, 4, part_lanes).astype(F32).reshape(16, 16, 256)
                total = total + jnp.sum(mine, axis=0)
                square = square + jnp.sum(mine * mine, axis=0)
        stats[n] = jnp.concatenate(
            [
                jnp.sum(total[0:8], axis=0, keepdims=True),
                jnp.sum(total[8:16], axis=0, keepdims=True),
                jnp.sum(square[0:8], axis=0, keepdims=True),
                jnp.sum(square[8:16], axis=0, keepdims=True),
                jnp.zeros((4, 256), F32),
            ],
            axis=0,
        )
        for c in stat_copies(n):
            c.start()
        for pp in range(2):
            for qq in range(2):
                input_conv(pp, qq, 0 if pp == 1 else 4, 1, part_lanes)

    input_half(0, lanes)
    pass_on(0)
    cw_pass.wait_recv()
    build(cw_in, olanes)
    for n, ref in enumerate((cb, gain, gbias)):
        remote(ref, par_all.at[n, :, olanes], w_s.at[n + 1], w_r.at[n + 1], (o, d, r)).wait_recv()
    input_half(1, olanes)

    zero_row = jnp.zeros((2, 32, 512), BF16)

    @pl.when(jnp.logical_not(has_up))
    def _():
        pm[:, 0] = zero_row

    @pl.when(jnp.logical_not(has_down))
    def _():
        pm[:, 9] = zero_row

    def pm_full(f):
        block = pm.at[f, 1:9, :, lanes]
        return remote(block, block, pm_s.at[f, 0], pm_r.at[f, 0], (o, d, r))

    def pm_up(f):
        return [
            remote(pm.at[f, 1, :, lanes], pm.at[f, 9, :, lanes], pm_s.at[f, 1 + n], pm_r.at[f, 1 + n], (dev, d, r - 1))
            for n, dev in enumerate((s, o))
        ]

    def pm_down(f):
        return [
            remote(pm.at[f, 8, :, lanes], pm.at[f, 0, :, lanes], pm_s.at[f, 3 + n], pm_r.at[f, 3 + n], (dev, d, r + 1))
            for n, dev in enumerate((s, o))
        ]

    def share(f, pick):
        for st in range(2):
            live = (span[st] > 0).astype(BF16)
            pm[f, 1:9, pl.ds(16 * st, 16), lanes] = pick(st) * live
        pm_full(f).start()

        @pl.when(has_up)
        def _():
            for c in pm_up(f):
                c.start()

        @pl.when(has_down)
        def _():
            for c in pm_down(f):
                c.start()

    def share_inner(f):
        if line:

            @pl.when(inner)
            def _():
                own_mid[f].wait()
                cross_copy(f).wait_recv()
                pass_copy(f).wait_recv()
                for st in range(2):
                    sel[f, :, pl.ds(16 * st, 16), :] = gm[f][moves[2 * end + st]]
                pick_copy(f, end).start()
                share(f, lambda st: gm[f][moves[2 * d + st]])

    def share_end(f):
        if line:

            @pl.when(jnp.logical_not(inner))
            def _():
                pick_copy(f, near).wait_recv()
                share(f, lambda st: sel[f, :, pl.ds(16 * st, 16), :])

        else:
            own_mid[f].wait()
            for k in range(1, n_dec):
                mid_copy(k, lax.rem(d + n_dec - k, n_dec), f).wait_recv()
            share(f, lambda st: gm[f][moves[2 * d + st]])

    share_inner(1)

    def activate_half(n, part_lanes):
        for c in stat_copies(n):
            c.wait_recv()
        sums = stats[n]
        for k in range(1, n_row):
            sums = sums + stats_in[n, k - 1]
        lane8 = lax.broadcasted_iota(jnp.int32, (8, 256), 1)
        for k in (1, 2, 4, 8):
            other = jnp.where((lane8 & k) > 0, pltpu.roll(sums, k, 1), pltpu.roll(sums, 256 - k, 1))
            sums = sums + other
        sums = sums / (4 * 8 * 16 * GROUP * n_row)
        gv = sums[2:4] - sums[0:2] * sums[0:2]
        scale = lax.rsqrt(gv + 1e-5) * par_all[1, :, part_lanes]
        shift = par_all[2, :, part_lanes]

        def spread(v):
            return jnp.concatenate(
                [jnp.broadcast_to(v[0:1], (8, 256)), jnp.broadcast_to(v[1:2], (8, 256))], axis=0
            )

        mean16 = spread(sums[0:2])
        scale16 = spread(scale)

        def activate(t, carry):
            for pp in range(2):
                for qq in range(2):
                    v = (h1[pp * 2 + qq, t, :, :, part_lanes].astype(F32) - mean16) * scale16 + shift
                    v = v * (0.5 * jnp.tanh(0.5 * v) + 0.5)
                    edge = lax.broadcasted_iota(jnp.int32, (5, 16, 256), 0)
                    if pp == 1:
                        v = jnp.where((edge == 0) & jnp.logical_not(has_up), 0.0, v)
                    else:
                        v = jnp.where((edge == 4) & jnp.logical_not(has_down), 0.0, v)
                    v = v.astype(BF16)
                    mb[pp, qq, t + 2, :, :, part_lanes] = v
                    moved = shifted(v.astype(F32).reshape(80, 256), -1 if qq == 1 else 1)
                    mb[pp, 2 if qq == 1 else 3, t + 2, :, :, part_lanes] = moved.astype(BF16).reshape(
                        5, 16, 256
                    )
            return carry

        lax.fori_loop(0, 4, activate, 0)

    activate_half(0, lanes)
    activate_half(1, olanes)

    acc[...] = jnp.zeros_like(acc)

    def conv(b, pairs):
        for a, t0, nt in pairs:
            pieces = []
            for pp in range(2):
                src = (b + 1) % 2 if pp == 0 else b % 2
                off = b // 2 if pp == 0 else (b + 1) // 2
                for qq in range(2):
                    taps = (2, 0, 1) if qq == 0 else (0, 1, 3)
                    pieces.append(
                        jnp.concatenate(
                            [
                                mb[src, var, t0 + a : t0 + a + nt, pl.ds(off, 4)].reshape(nt * 64, 512)
                                for var in taps
                            ],
                            axis=1,
                        )
                    )
            lhs = jnp.concatenate(pieces, axis=0)
            got = jnp.dot(lhs, midw_v[a * 3 + b], preferred_element_type=F32)
            acc[:, t0 : t0 + nt] += got.reshape(4, nt, 64, 256)

    share_inner(0)
    load_w.wait()

    def tap_late(b, carry):
        conv(b, ((2, 0, 4),))
        return carry

    lax.fori_loop(0, 1, tap_late, 0)
    share_end(1)
    lax.fori_loop(1, 2, tap_late, 0)
    share_end(0)
    lax.fori_loop(2, 3, tap_late, 0)

    def tap_mid(k, carry):
        conv(k, ((1, 1, 3), (0, 2, 2)))
        return carry

    lax.fori_loop(0, 3, tap_mid, 0)

    ro = lax.broadcasted_iota(jnp.int32, (64, 32), 0)
    co = lax.broadcasted_iota(jnp.int32, (64, 32), 1)
    v4 = ro // 16
    j2 = 2 * (ro % 8)
    col = jnp.where(v4 == 0, j2, jnp.where(v4 == 1, j2 + 1, jnp.where(v4 == 2, j2 - 1, j2 + 2)))
    fits = (col >= 0) & (col < 16) & (co == (ro // 8) % 2 * 16 + col)
    deal = jnp.where(fits, 1.0, 0.0).astype(BF16)

    for t in range(2):
        for pp in range(2):
            for qq in range(2):
                nm_v[t, pp, :, pl.ds(16 * qq, 16), :] = mb[pp, qq, t + 4, pp : pp + 4, :, lanes]
    out_mid = pltpu.make_async_copy(nm_v, new_mid, local_sem.at[5])
    out_mid.start()

    def finish(t, carry):
        for pp in range(2):
            for qq in range(2):
                y = (
                    h1[pp * 2 + qq, t, pp : pp + 4, :, lanes].astype(F32)
                    + acc[pp * 2 + qq, t].reshape(4, 16, 256)
                    + midb[...]
                )
                dec_v[t, pp, :, pl.ds(16 * qq, 16), :] = y.astype(BF16)
        return carry

    lax.fori_loop(2, 4, finish, 0)
    out_late = pltpu.make_async_copy(
        dec_v.at[pl.ds(2, 2)], decoded.at[pl.ds(2, 2)], local_sem.at[6]
    )
    out_late.start()

    for f, pairs in ((1, ((1, 0, 1), (0, 1, 1))), (0, ((0, 0, 1),))):
        pm_full(f).wait_recv()

        @pl.when(has_up)
        def _():
            for c in pm_down(f):
                c.wait_recv()

        @pl.when(has_down)
        def _():
            for c in pm_up(f):
                c.wait_recv()

        for row in range(10):
            y = jnp.dot(deal, pm[f, row], preferred_element_type=F32).astype(BF16)
            for v in range(4):
                mb[(row + 1) % 2, v, f, row // 2] = y[16 * v : 16 * v + 16]

        def tap_early(b, carry):
            conv(b, pairs)
            return carry

        lax.fori_loop(0, 3, tap_early, 0)

    lax.fori_loop(0, 2, finish, 0)
    out_early = pltpu.make_async_copy(
        dec_v.at[pl.ds(0, 2)], decoded.at[pl.ds(0, 2)], local_sem.at[7]
    )
    out_early.start()

    for k in range(1, n_dec):
        lat_copy(k, d).wait_send()
    for c in par_copies + stat_copies(0) + stat_copies(1) + [full, cw_copy, cw_pass, pm_full(0), pm_full(1)]:
        c.wait_send()
    if line:

        @pl.when(inner)
        def _():
            for f in range(2):
                cross_copy(f).wait_send()
                pass_copy(f).wait_send()
                pick_copy(f, end).wait_send()

        @pl.when(jnp.logical_not(inner))
        def _():
            for f in range(2):
                end_copy(f).wait_send()
                own_mid[f].wait()

    else:
        for k in range(1, n_dec):
            for f in range(2):
                mid_copy(k, d, f).wait_send()

    @pl.when(has_up)
    def _():
        for c in up + pm_up(0) + pm_up(1) + [lat_edge_up]:
            c.wait_send()

    @pl.when(has_down)
    def _():
        for c in down + pm_down(0) + pm_down(1) + [lat_edge_down]:
            c.wait_send()
    for c in (out_lat, out_mid, out_late, out_early):
        c.wait()


def weave_kernel(
    decoded_in, new_lat_in, new_mid_in, decoded_out, new_lat_out, new_mid_out, decoded, new_lat, new_mid, sem
):
    loads = [
        pltpu.make_async_copy(source, target, sem.at[n])
        for n, (source, target) in enumerate(
            ((new_lat_in, new_lat), (new_mid_in, new_mid), (decoded_in, decoded))
        )
    ]
    for c in loads:
        c.start()
    ro = lax.broadcasted_iota(jnp.int32, (32, 32), 0)
    co = lax.broadcasted_iota(jnp.int32, (32, 32), 1)
    weave = jnp.where(co == (ro % 2) * 16 + (ro // 16) * 8 + (ro % 16) // 2, 1.0, 0.0).astype(BF16)

    def spread(source, target, t):
        for pp in range(2):
            for i in range(4):
                y = jnp.dot(weave, source[t, pp, i], preferred_element_type=F32).astype(BF16)
                target[0, t, 2 * i + pp] = y[0:16]
                target[1, t, 2 * i + pp] = y[16:32]

    loads[0].wait()
    patches = new_lat[...].reshape(128, 128)
    ro = lax.broadcasted_iota(jnp.int32, (256, 128), 0)
    co = lax.broadcasted_iota(jnp.int32, (256, 128), 1)
    grown = [
        jnp.dot(
            jnp.where((co == ro // 16 * 8 + ro % 16 // 2) & (ro % 2 == q), 1.0, 0.0).astype(BF16),
            patches,
            preferred_element_type=F32,
        )
        for q in range(2)
    ]
    grown = jnp.where(co // 16 % 2 == 0, grown[0], grown[1])
    ro = lax.broadcasted_iota(jnp.int32, (128, CZ), 0)
    for p in range(2):
        fold = (ro // 32 == 2 + p) & (ro % CZ == lax.broadcasted_iota(jnp.int32, (128, CZ), 1))
        y = jnp.dot(
            grown.astype(BF16), jnp.where(fold, 1.0, 0.0).astype(BF16), preferred_element_type=F32
        ).astype(BF16)
        for t in range(2):
            for i in range(4):
                for st in range(2):
                    row = ((t * 4 + i) * 2 + st) * 16
                    new_lat_out[st, t, 2 * i + p] = y[row : row + 16]
    loads[1].wait()
    for t in range(2):
        spread(new_mid, new_mid_out, t)
    loads[2].wait()
    for t in range(4):
        spread(decoded, decoded_out, t)


def shards(
    n_dec,
    n_row,
    hidden,
    head_weight,
    head_bias,
    lat_cache,
    mid_cache,
    moves,
    span_index,
    conv_in_weight,
    conv_in_bias,
    gn_gain,
    gn_bias,
    mid_weight,
    mid_bias,
):
    slots = n_dec * 2
    depth = hidden.shape[-1]
    vm = pl.BlockSpec(memory_space=pltpu.VMEM)
    sm = pl.BlockSpec(memory_space=pltpu.SMEM)
    hbm = pl.BlockSpec(memory_space=pl.ANY)
    dma = pltpu.SemaphoreType.DMA
    parts = pl.pallas_call(
        functools.partial(kernel, n_dec, n_row),
        out_shape=(
            jax.ShapeDtypeStruct((4, 2, 4, 32, 256), BF16),
            jax.ShapeDtypeStruct((2, 4, 16, 128), BF16),
            jax.ShapeDtypeStruct((2, 2, 4, 32, 256), BF16),
        ),
        in_specs=[hbm, vm, vm, vm, hbm, sm, sm, vm, vm, vm, vm, hbm, vm],
        out_specs=(hbm, hbm, hbm),
        scratch_shapes=[
            pltpu.VMEM((4, 2, 4, 32, 256), BF16),
            pltpu.VMEM((2, 4, 16, 128), BF16),
            pltpu.VMEM((2, 2, 4, 32, 256), BF16),
            pltpu.VMEM((2, 32, 128), BF16),
            pltpu.VMEM((256, depth), BF16),
            pltpu.VMEM((9, 1536, 256), BF16),
            pltpu.VMEM((2, 4, 16, 128), F32),
            pltpu.VMEM((2, 4, 16, 128), F32),
            pltpu.VMEM((2, 2, 2, 16, 128), F32),
            pltpu.VMEM((slots, 32, 128), BF16),
            pltpu.VMEM((4, 16, 128), F32),
            pltpu.VMEM((2, 16, 128), F32),
            pltpu.VMEM((27, CZ, 256), BF16),
            pltpu.VMEM((3, 1, 512), F32),
            pltpu.VMEM((4, 3, 256, 512), BF16),
            pltpu.VMEM((2, 6, 6, 16, 128), BF16),
            pltpu.VMEM((4, 4, 5, 16, 512), BF16),
            pltpu.VMEM((2, 8, 256), F32),
            pltpu.VMEM((2, n_row - 1, 8, 256), F32),
            pltpu.VMEM((slots, 8, 16, 256), BF16),
            pltpu.VMEM((slots, 8, 16, 256), BF16),
            pltpu.VMEM((2, 8, 32, 256), BF16),
            pltpu.VMEM((2, 10, 32, 512), BF16),
            pltpu.VMEM((2, 4, 6, 5, 16, 512), BF16),
            pltpu.VMEM((4, 4, 64, 256), F32),
            dma((8,)),
            dma((n_dec - 1,)),
            dma((n_dec - 1,)),
            dma((n_dec - 1, 2)),
            dma((n_dec - 1, 2)),
            dma((4, 2)),
            dma((4, 2)),
            dma((5,)),
            dma((5,)),
            dma((5,)),
            dma((5,)),
            dma((2,)),
            dma((2,)),
            dma((2, n_row - 1)),
            dma((2, n_row - 1)),
            dma((2, 5)),
            dma((2, 5)),
        ],
        compiler_params=pltpu.CompilerParams(
            collective_id=0, has_side_effects=True, vmem_limit_bytes=56 * 1024 * 1024
        ),
        cost_estimate=pl.CostEstimate(
            flops=9_000_000_000, bytes_accessed=12_000_000, transcendentals=700_000
        ),
    )(
        hidden.reshape(256, depth),
        head_weight.T,
        head_bias.reshape(1, 64),
        lat_cache,
        mid_cache,
        moves,
        span_index,
        conv_in_weight.reshape(27, CZ, 256),
        conv_in_bias.reshape(1, 256),
        gn_gain.reshape(1, 256),
        gn_bias.reshape(1, 256),
        mid_weight.reshape(9, 1536, 256),
        mid_bias.reshape(1, 256),
    )
    return pl.pallas_call(
        weave_kernel,
        out_shape=(
            jax.ShapeDtypeStruct((2, 4, 8, 16, 256), BF16),
            jax.ShapeDtypeStruct((2, 2, 8, 16, CZ), BF16),
            jax.ShapeDtypeStruct((2, 2, 8, 16, 256), BF16),
        ),
        in_specs=[hbm, hbm, hbm],
        out_specs=(vm, vm, vm),
        scratch_shapes=[
            pltpu.VMEM((4, 2, 4, 32, 256), BF16),
            pltpu.VMEM((2, 4, 16, 128), BF16),
            pltpu.VMEM((2, 2, 4, 32, 256), BF16),
            dma((3,)),
        ],
        compiler_params=pltpu.CompilerParams(vmem_limit_bytes=60 * 1024 * 1024),
        cost_estimate=pl.CostEstimate(flops=30_000_000, bytes_accessed=1_600_000, transcendentals=0),
    )(*parts)


def solution(mesh):
    placed = (
        P("dec", None, "row", None, "section"),
        P("section", None),
        P(),
        P("dec", None, "row", None, None),
        P("dec", None, "row", None, "section"),
        P(),
        P("dec"),
        P(None, None, None, None, "section"),
        P("section"),
        P("section"),
        P("section"),
        P(None, None, None, None, "section"),
        P("section"),
    )
    return jax.shard_map(
        functools.partial(shards, mesh.shape["dec"], mesh.shape["row"]),
        mesh=mesh,
        in_specs=placed,
        out_specs=(
            P("dec", None, "row", None, "section"),
            P("dec", None, "row", None, None),
            P("dec", None, "row", None, "section"),
        ),
        check_vma=False,
    )
```

```python
import functools

import jax
import jax.numpy as jnp
from jax import lax
from jax.experimental import pallas as pl
from jax.experimental.pallas import tpu as pltpu
from jax.sharding import PartitionSpec as P

CZ = 16
GROUP = 16
MESH = pl.DeviceIdType.MESH
F32 = jnp.float32
BF16 = jnp.bfloat16


def shifted(flat, step):
    n = flat.shape[0]
    j = lax.broadcasted_iota(jnp.int32, flat.shape, 0) % 8
    if step < 0:
        return jnp.where(j == 0, 0.0, pltpu.roll(flat, 1, 0))
    return jnp.where(j == 7, 0.0, pltpu.roll(flat, n - 1, 0))


def kernel(
    n_dec,
    n_row,
    hidden,
    head_t,
    head_bias,
    lat,
    mid,
    moves,
    span,
    cw,
    cb,
    gain,
    gbias,
    midw,
    midb,
    decoded,
    new_lat,
    new_mid,
    dec_v,
    nl_v,
    nm_v,
    lat_pk,
    hid_v,
    midw_v,
    part,
    part_x,
    part_h,
    lat_all,
    lat_own,
    lat_h,
    cw_in,
    par_all,
    wide,
    z,
    h1,
    stats,
    stats_in,
    gm0,
    gm1,
    gm2,
    gm3,
    sel,
    pm,
    mb,
    acc,
    local_sem,
    lat_s,
    lat_r,
    mid_s,
    mid_r,
    hop_s,
    hop_r,
    w_s,
    w_r,
    part_s,
    part_r,
    lh_s,
    lh_r,
    st_s,
    st_r,
    pm_s,
    pm_r,
):
    s = lax.axis_index("section")
    d = lax.axis_index("dec")
    r = lax.axis_index("row")
    o = 1 - s
    lanes = pl.ds(pl.multiple_of(s * 256, 256), 256)
    olanes = pl.ds(pl.multiple_of(o * 256, 256), 256)
    has_up = r > 0
    has_down = r < n_row - 1

    barrier = pltpu.get_barrier_semaphore()

    def greet(dev):
        pl.semaphore_signal(barrier, inc=1, device_id=dev, device_id_type=MESH)

    greet((o, d, r))
    for k in range(1, n_dec):
        greet((s, lax.rem(d + k, n_dec), r))
    for k in range(1, n_row):
        greet((s, d, lax.rem(r + k, n_row)))
        greet((o, d, lax.rem(r + k, n_row)))

    load_hidden = pltpu.make_async_copy(hidden, hid_v, local_sem.at[0])
    load_hidden.start()
    gm = (gm0, gm1, gm2, gm3)

    def chunk(c):
        return mid.at[:, 1 - c // 2, 4 * (c % 2) : 4 * (c % 2) + 4]

    own_mid = [
        pltpu.make_async_copy(chunk(c), gm[c].at[pl.ds(2 * d, 2)], local_sem.at[8 + c])
        for c in range(4)
    ]
    for c in own_mid:
        c.start()
    load_w = pltpu.make_async_copy(midw, midw_v, local_sem.at[3])

    pl.semaphore_wait(barrier, 1 + (n_dec - 1) + 2 * (n_row - 1))

    def remote(src, dst, ssem, rsem, dev):
        return pltpu.make_async_remote_copy(
            src_ref=src, dst_ref=dst, send_sem=ssem, recv_sem=rsem, device_id=dev, device_id_type=MESH
        )

    def lat_copy(k, origin):
        return remote(
            lat_pk, lat_all.at[pl.ds(2 * origin, 2)], lat_s.at[k - 1], lat_r.at[k - 1],
            (s, lax.rem(d + k, n_dec), r),
        )

    def mid_copy(k, origin, f):
        return remote(
            chunk(f), gm[f].at[pl.ds(2 * origin, 2)], mid_s.at[k - 1, f], mid_r.at[k - 1, f],
            (s, lax.rem(d + k, n_dec), r),
        )

    line = n_dec == 4
    inner = (d == 1) | (d == 2)
    end = 3 * (d - 1)
    near = 1 + d // 3

    def end_copy(f):
        return remote(
            chunk(f), gm[f].at[pl.ds(2 * d, 2)], hop_s.at[0, f], hop_r.at[0, f], (s, near, r)
        )

    def cross_copy(f):
        return remote(
            chunk(f), gm[f].at[pl.ds(2 * d, 2)], hop_s.at[1, f], hop_r.at[1, f], (s, 3 - d, r)
        )

    def pass_copy(f):
        slots = pl.ds(2 * end, 2)
        return remote(
            gm[f].at[slots], gm[f].at[slots], hop_s.at[2, f], hop_r.at[2, f], (s, 3 - d, r)
        )

    def pick_copy(f, target):
        return remote(sel.at[f], sel.at[f], hop_s.at[3, f], hop_r.at[3, f], (s, target, r))

    def pass_on(f):
        if line:

            @pl.when(inner)
            def _():
                end_copy(f).wait_recv()
                pass_copy(f).start()

    half = lax.rem(r, 2)
    half_lanes = pl.ds(pl.multiple_of(half * 128, 128), 128)
    cw_copy = remote(
        cw.at[:, :, half_lanes], cw_in.at[:, :, half_lanes], w_s.at[0], w_r.at[0], (o, d, r)
    )
    cw_copy.start()
    cw_pass = remote(
        cw_in.at[:, :, half_lanes], cw_in.at[:, :, half_lanes], w_s.at[4], w_r.at[4],
        (s, d, r + 1 - 2 * half),
    )
    par_copies = [
        remote(ref, par_all.at[n, :, lanes], w_s.at[n + 1], w_r.at[n + 1], (o, d, r))
        for n, ref in enumerate((cb, gain, gbias))
    ]
    for c in par_copies:
        c.start()
    ri = lax.broadcasted_iota(jnp.int32, (CZ, 128), 0)
    ci = lax.broadcasted_iota(jnp.int32, (CZ, 128), 1)
    tile = jnp.where(ci % CZ == ri, 1.0, 0.0).astype(BF16)
    wide_lat = jnp.dot(lat[...].reshape(512, CZ), tile, preferred_element_type=F32)
    wide_lat = wide_lat.reshape(2, 2, 4, 2, 16, 128)
    lane6 = lax.broadcasted_iota(jnp.int32, (2, 4, 16, 128), 3) // 32
    merged = jnp.where(
        lane6 == 0,
        wide_lat[:, 0, :, 0],
        jnp.where(lane6 == 1, wide_lat[:, 0, :, 1], jnp.where(lane6 == 2, wide_lat[:, 1, :, 0], wide_lat[:, 1, :, 1])),
    )
    merged = merged.reshape(128, 128).astype(BF16)
    ri = lax.broadcasted_iota(jnp.int32, (64, 128), 0)
    ci = lax.broadcasted_iota(jnp.int32, (64, 128), 1)
    halves = [
        jnp.dot(
            jnp.where(ci == ri // 8 * 16 + 2 * (ri % 8) + q, 1.0, 0.0).astype(BF16),
            merged,
            preferred_element_type=F32,
        )
        for q in range(2)
    ]
    lat_pk[...] = (
        jnp.where(ci // 16 % 2 == 0, halves[0], halves[1]).astype(BF16).reshape(2, 32, 128)
    )

    for k in range(1, n_dec):
        lat_copy(k, d).start()

    def send_end(*chunks):
        if line:

            @pl.when(jnp.logical_not(inner))
            def _():
                for c in chunks:
                    end_copy(c).start()

    def send_cross(*chunks):
        if line:

            @pl.when(inner)
            def _():
                for c in chunks:
                    cross_copy(c).start()

    send_end(0)
    send_cross(0, 1)
    if not line:
        for k in range(1, n_dec):
            for f in range(4):
                mid_copy(k, d, f).start()

    load_hidden.wait()
    load_w.start()
    head = lax.dot_general(
        hid_v[...],
        jnp.concatenate([head_t[...], jnp.zeros_like(head_t)], axis=0),
        (((1,), (1,)), ((), ())),
        preferred_element_type=F32,
    )
    head = head.reshape(2, 4, 4, 8, 128)
    lane = lax.broadcasted_iota(jnp.int32, (4, 8, 128), 2)
    for t in range(2):
        for st in range(2):
            high = pltpu.roll(head[st, t + 2].reshape(32, 128), 64, 1).reshape(4, 8, 128)
            part[t, :, pl.ds(8 * st, 8), :] = jnp.where(lane < 64, head[st, t], high)

    def part_copies():
        full = remote(part, part_x, part_s.at[0], part_r.at[0], (o, d, r))
        up = [
            remote(part.at[:, 0], part_h.at[1, n], part_s.at[1 + n], part_r.at[1 + n], (dev, d, r - 1))
            for n, dev in enumerate((s, o))
        ]
        down = [
            remote(part.at[:, 3], part_h.at[0, n], part_s.at[3 + n], part_r.at[3 + n], (dev, d, r + 1))
            for n, dev in enumerate((s, o))
        ]
        return full, up, down

    full, up, down = part_copies()

    @pl.when(has_up)
    def _():
        for c in up:
            c.start()

    @pl.when(has_down)
    def _():
        for c in down:
            c.start()

    full.start()
    send_end(1)

    zero_slab = jnp.zeros((CZ, 256), BF16)

    def build(source, target):
        def one(a, carry):
            for pp in range(2):
                for qq in range(2):
                    for pos in range(16):
                        di, dj, p, q = pos // 8, pos // 4 % 2, pos // 2 % 2, pos % 2
                        b = 2 * di + p - 1 + pp
                        e = 2 * dj + q - 1 + qq
                        if 0 <= b < 3 and 0 <= e < 3:
                            slab = source[a * 9 + b * 3 + e]
                        else:
                            slab = zero_slab
                        wide[pp * 2 + qq, a, pl.ds(pos * 16, 16), target] = slab
            return carry

        lax.fori_loop(0, 3, one, 0)

    build(cw, lanes)
    lat_all[pl.ds(2 * d, 2)] = lat_pk[...]
    for n, ref in enumerate((cb, gain, gbias)):
        par_all[n, :, lanes] = ref[...]

    for k in range(1, n_dec):
        lat_copy(k, lax.rem(d + n_dec - k, n_dec)).wait_recv()
    for st in range(2):
        live = (span[st] > 0).astype(F32)
        x = lat_all[moves[2 * d + st]].astype(F32) * live
        lat_own[:, pl.ds(8 * st, 8), :] = x.reshape(4, 8, 128)
    lat_edge_up = remote(lat_own.at[0], lat_h.at[1], lh_s.at[0], lh_r.at[0], (s, d, r - 1))
    lat_edge_down = remote(lat_own.at[3], lat_h.at[0], lh_s.at[1], lh_r.at[1], (s, d, r + 1))

    @pl.when(has_up)
    def _():
        lat_edge_up.start()

    @pl.when(has_down)
    def _():
        lat_edge_down.start()

    send_end(2)
    send_cross(2)
    cw_copy.wait_recv()
    cw_pass.start()
    pass_on(0)
    send_end(3)

    full.wait_recv()

    @pl.when(has_up)
    def _():
        for c in down:
            c.wait_recv()
        lat_edge_down.wait_recv()

    @pl.when(has_down)
    def _():
        for c in up:
            c.wait_recv()
        lat_edge_up.wait_recv()

    bias = jnp.concatenate([head_bias[...], head_bias[...]], axis=1)

    def place(low, base, step, packed):
        count = packed.shape[0]
        flat = packed.astype(BF16).astype(F32).reshape(count * 16, 128)
        lane = lax.broadcasted_iota(jnp.int32, flat.shape, 1) < 64
        turn = pltpu.roll(flat, 64, 1)
        before = shifted(flat, -1)
        after = shifted(flat, 1)
        turn_before = pltpu.roll(before, 64, 1)
        turn_after = pltpu.roll(after, 64, 1)
        for q, frame, left, right in (
            (0, base, before, turn),
            (0, base + step, turn_before, flat),
            (1, base, flat, turn_after),
            (1, base + step, turn, after),
        ):
            z[q, frame, pl.ds(low, count)] = (
                jnp.where(lane, left, right).astype(BF16).reshape(count, 16, 128)
            )

    up_live = has_up.astype(F32)
    down_live = has_down.astype(F32)

    @pl.when(jnp.logical_not(has_up))
    def _():
        part_h[0] = jnp.zeros((2, 2, 16, 128), F32)
        lat_h[0] = jnp.zeros((16, 128), F32)

    @pl.when(jnp.logical_not(has_down))
    def _():
        part_h[1] = jnp.zeros((2, 2, 16, 128), F32)
        lat_h[1] = jnp.zeros((16, 128), F32)

    for t in range(2):
        own = part[t] + part_x[t] + bias
        nl_v[t] = own.astype(BF16)
        place(1, 2 + t, 2, own)
        place(0, 2 + t, 2, ((part_h[0, 0, t] + part_h[0, 1, t] + bias) * up_live)[None])
        place(5, 2 + t, 2, ((part_h[1, 0, t] + part_h[1, 1, t] + bias) * down_live)[None])
    place(1, 0, 1, lat_own[...])
    place(0, 0, 1, lat_h[0][None])
    place(5, 0, 1, lat_h[1][None])

    out_lat = pltpu.make_async_copy(nl_v, new_lat, local_sem.at[4])
    out_lat.start()
    pass_on(1)
    send_cross(3)

    def input_conv(pp, qq, row, count, part_lanes):
        out = jnp.zeros((64 * count, 256), F32)
        for a in range(3):
            lhs = jnp.concatenate(
                [
                    z[qq, a : a + 4, row + di : row + di + count].reshape(64 * count, 128)
                    for di in range(2)
                ],
                axis=1,
            )
            out = out + jnp.dot(lhs, wide[pp * 2 + qq, a, :, part_lanes], preferred_element_type=F32)
        first = (out + par_all[0, :, part_lanes]).astype(BF16)
        h1[pp * 2 + qq, :, row : row + count, :, part_lanes] = first.reshape(4, count, 16, 256)
        return first

    def stat_copies(n):
        return [
            remote(
                stats.at[n], stats_in.at[n, k - 1], st_s.at[n, k - 1], st_r.at[n, k - 1],
                (s, d, lax.rem(r + k, n_row)),
            )
            for k in range(1, n_row)
        ]

    def input_half(n, part_lanes):
        total = jnp.zeros((16, 256), F32)
        square = jnp.zeros((16, 256), F32)
        for pp in range(2):
            for qq in range(2):
                mine = input_conv(pp, qq, pp, 4, part_lanes).astype(F32).reshape(16, 16, 256)
                total = total + jnp.sum(mine, axis=0)
                square = square + jnp.sum(mine * mine, axis=0)
        stats[n] = jnp.concatenate(
            [
                jnp.sum(total[0:8], axis=0, keepdims=True),
                jnp.sum(total[8:16], axis=0, keepdims=True),
                jnp.sum(square[0:8], axis=0, keepdims=True),
                jnp.sum(square[8:16], axis=0, keepdims=True),
                jnp.zeros((4, 256), F32),
            ],
            axis=0,
        )
        for c in stat_copies(n):
            c.start()
        for pp in range(2):
            for qq in range(2):
                input_conv(pp, qq, 0 if pp == 1 else 4, 1, part_lanes)

    input_half(0, lanes)
    pass_on(2)
    cw_pass.wait_recv()
    build(cw_in, olanes)
    for n, ref in enumerate((cb, gain, gbias)):
        remote(ref, par_all.at[n, :, olanes], w_s.at[n + 1], w_r.at[n + 1], (o, d, r)).wait_recv()
    input_half(1, olanes)

    zero_row = jnp.zeros((2, 32, 512), BF16)

    @pl.when(jnp.logical_not(has_up))
    def _():
        pm[:, 0] = zero_row

    @pl.when(jnp.logical_not(has_down))
    def _():
        pm[:, 9] = zero_row

    def pm_full(c):
        low = 1 + 4 * (c % 2)
        block = pm.at[1 - c // 2, low : low + 4, :, lanes]
        return remote(block, block, pm_s.at[c, 0], pm_r.at[c, 0], (o, d, r))

    def pm_up(c):
        f = 1 - c // 2
        return [
            remote(pm.at[f, 1, :, lanes], pm.at[f, 9, :, lanes], pm_s.at[c, 1 + n], pm_r.at[c, 1 + n], (dev, d, r - 1))
            for n, dev in enumerate((s, o))
        ]

    def pm_down(c):
        f = 1 - c // 2
        return [
            remote(pm.at[f, 8, :, lanes], pm.at[f, 0, :, lanes], pm_s.at[c, 1 + n], pm_r.at[c, 1 + n], (dev, d, r + 1))
            for n, dev in enumerate((s, o))
        ]

    def share(c, pick):
        low = 1 + 4 * (c % 2)
        for st in range(2):
            live = (span[st] > 0).astype(BF16)
            pm[1 - c // 2, low : low + 4, pl.ds(16 * st, 16), lanes] = pick(st) * live
        pm_full(c).start()
        if c % 2 == 0:

            @pl.when(has_up)
            def _():
                for e in pm_up(c):
                    e.start()

        else:

            @pl.when(has_down)
            def _():
                for e in pm_down(c):
                    e.start()

    def share_inner(f):
        if line:

            @pl.when(inner)
            def _():
                own_mid[f].wait()
                cross_copy(f).wait_recv()
                pass_copy(f).wait_recv()
                for st in range(2):
                    sel[f, :, pl.ds(16 * st, 16), :] = gm[f][moves[2 * end + st]]
                pick_copy(f, end).start()
                share(f, lambda st: gm[f][moves[2 * d + st]])

    def share_end(f):
        if line:

            @pl.when(jnp.logical_not(inner))
            def _():
                pick_copy(f, near).wait_recv()
                share(f, lambda st: sel[f, :, pl.ds(16 * st, 16), :])

        else:
            own_mid[f].wait()
            for k in range(1, n_dec):
                mid_copy(k, lax.rem(d + n_dec - k, n_dec), f).wait_recv()
            share(f, lambda st: gm[f][moves[2 * d + st]])

    pass_on(3)
    share_inner(0)

    def activate_half(n, part_lanes):
        for c in stat_copies(n):
            c.wait_recv()
        sums = stats[n]
        for k in range(1, n_row):
            sums = sums + stats_in[n, k - 1]
        lane8 = lax.broadcasted_iota(jnp.int32, (8, 256), 1)
        for k in (1, 2, 4, 8):
            other = jnp.where((lane8 & k) > 0, pltpu.roll(sums, k, 1), pltpu.roll(sums, 256 - k, 1))
            sums = sums + other
        sums = sums / (4 * 8 * 16 * GROUP * n_row)
        gv = sums[2:4] - sums[0:2] * sums[0:2]
        scale = lax.rsqrt(gv + 1e-5) * par_all[1, :, part_lanes]
        shift = par_all[2, :, part_lanes]

        def spread(v):
            return jnp.concatenate(
                [jnp.broadcast_to(v[0:1], (8, 256)), jnp.broadcast_to(v[1:2], (8, 256))], axis=0
            )

        mean16 = spread(sums[0:2])
        scale16 = spread(scale)

        def activate(t, carry):
            for pp in range(2):
                for qq in range(2):
                    v = (h1[pp * 2 + qq, t, :, :, part_lanes].astype(F32) - mean16) * scale16 + shift
                    v = v * (0.5 * jnp.tanh(0.5 * v) + 0.5)
                    edge = lax.broadcasted_iota(jnp.int32, (5, 16, 256), 0)
                    if pp == 1:
                        v = jnp.where((edge == 0) & jnp.logical_not(has_up), 0.0, v)
                    else:
                        v = jnp.where((edge == 4) & jnp.logical_not(has_down), 0.0, v)
                    v = v.astype(BF16)
                    mb[pp, qq, t + 2, :, :, part_lanes] = v
                    moved = shifted(v.astype(F32).reshape(80, 256), -1 if qq == 1 else 1)
                    mb[pp, 2 if qq == 1 else 3, t + 2, :, :, part_lanes] = moved.astype(BF16).reshape(
                        5, 16, 256
                    )
            return carry

        lax.fori_loop(0, 4, activate, 0)

    activate_half(0, lanes)
    share_inner(1)
    activate_half(1, olanes)
    share_inner(2)
    share_end(0)

    acc[...] = jnp.zeros_like(acc)

    def conv(b, pairs):
        for a, t0, nt in pairs:
            pieces = []
            for pp in range(2):
                src = (b + 1) % 2 if pp == 0 else b % 2
                off = b // 2 if pp == 0 else (b + 1) // 2
                for qq in range(2):
                    taps = (2, 0, 1) if qq == 0 else (0, 1, 3)
                    pieces.append(
                        jnp.concatenate(
                            [
                                mb[src, var, t0 + a : t0 + a + nt, pl.ds(off, 4)].reshape(nt * 64, 512)
                                for var in taps
                            ],
                            axis=1,
                        )
                    )
            lhs = jnp.concatenate(pieces, axis=0)
            got = jnp.dot(lhs, midw_v[a * 3 + b], preferred_element_type=F32)
            acc[:, t0 : t0 + nt] += got.reshape(4, nt, 64, 256)

    load_w.wait()

    def tap_late(b, carry):
        conv(b, ((2, 0, 4),))
        return carry

    lax.fori_loop(0, 1, tap_late, 0)
    share_inner(3)
    share_end(1)
    lax.fori_loop(1, 2, tap_late, 0)
    share_end(2)
    lax.fori_loop(2, 3, tap_late, 0)
    share_end(3)

    def tap_mid(k, carry):
        conv(k, ((1, 1, 3), (0, 2, 2)))
        return carry

    lax.fori_loop(0, 3, tap_mid, 0)

    ro = lax.broadcasted_iota(jnp.int32, (64, 32), 0)
    co = lax.broadcasted_iota(jnp.int32, (64, 32), 1)
    v4 = ro // 16
    j2 = 2 * (ro % 8)
    col = jnp.where(v4 == 0, j2, jnp.where(v4 == 1, j2 + 1, jnp.where(v4 == 2, j2 - 1, j2 + 2)))
    fits = (col >= 0) & (col < 16) & (co == (ro // 8) % 2 * 16 + col)
    deal = jnp.where(fits, 1.0, 0.0).astype(BF16)

    for t in range(2):
        for pp in range(2):
            for qq in range(2):
                nm_v[t, pp, :, pl.ds(16 * qq, 16), :] = mb[pp, qq, t + 4, pp : pp + 4, :, lanes]
    out_mid = pltpu.make_async_copy(nm_v, new_mid, local_sem.at[5])
    out_mid.start()

    def finish(t, carry):
        for pp in range(2):
            for qq in range(2):
                y = (
                    h1[pp * 2 + qq, t, pp : pp + 4, :, lanes].astype(F32)
                    + acc[pp * 2 + qq, t].reshape(4, 16, 256)
                    + midb[...]
                )
                dec_v[t, pp, :, pl.ds(16 * qq, 16), :] = y.astype(BF16)
        return carry

    lax.fori_loop(2, 4, finish, 0)
    out_late = pltpu.make_async_copy(
        dec_v.at[pl.ds(2, 2)], decoded.at[pl.ds(2, 2)], local_sem.at[6]
    )
    out_late.start()

    for f, pairs in ((1, ((1, 0, 1), (0, 1, 1))), (0, ((0, 0, 1),))):
        first = 2 - 2 * f
        pm_full(first).wait_recv()
        pm_full(first + 1).wait_recv()

        @pl.when(has_up)
        def _():
            for c in pm_down(first + 1):
                c.wait_recv()

        @pl.when(has_down)
        def _():
            for c in pm_up(first):
                c.wait_recv()

        for row in range(10):
            y = jnp.dot(deal, pm[f, row], preferred_element_type=F32).astype(BF16)
            for v in range(4):
                mb[(row + 1) % 2, v, f, row // 2] = y[16 * v : 16 * v + 16]

        def tap_early(b, carry):
            conv(b, pairs)
            return carry

        lax.fori_loop(0, 3, tap_early, 0)

    lax.fori_loop(0, 2, finish, 0)
    out_early = pltpu.make_async_copy(
        dec_v.at[pl.ds(0, 2)], decoded.at[pl.ds(0, 2)], local_sem.at[7]
    )
    out_early.start()

    for k in range(1, n_dec):
        lat_copy(k, d).wait_send()
    for c in par_copies + stat_copies(0) + stat_copies(1) + [full, cw_copy, cw_pass] + [pm_full(c) for c in range(4)]:
        c.wait_send()
    if line:

        @pl.when(inner)
        def _():
            for f in range(4):
                cross_copy(f).wait_send()
                pass_copy(f).wait_send()
                pick_copy(f, end).wait_send()

        @pl.when(jnp.logical_not(inner))
        def _():
            for f in range(4):
                end_copy(f).wait_send()
                own_mid[f].wait()

    else:
        for k in range(1, n_dec):
            for f in range(4):
                mid_copy(k, d, f).wait_send()

    @pl.when(has_up)
    def _():
        for c in up + pm_up(0) + pm_up(2) + [lat_edge_up]:
            c.wait_send()

    @pl.when(has_down)
    def _():
        for c in down + pm_down(1) + pm_down(3) + [lat_edge_down]:
            c.wait_send()
    for c in (out_lat, out_mid, out_late, out_early):
        c.wait()


def weave_kernel(
    decoded_in, new_lat_in, new_mid_in, decoded_out, new_lat_out, new_mid_out, decoded, new_lat, new_mid, sem
):
    loads = [
        pltpu.make_async_copy(source, target, sem.at[n])
        for n, (source, target) in enumerate(
            ((new_lat_in, new_lat), (new_mid_in, new_mid), (decoded_in, decoded))
        )
    ]
    for c in loads:
        c.start()
    ro = lax.broadcasted_iota(jnp.int32, (32, 32), 0)
    co = lax.broadcasted_iota(jnp.int32, (32, 32), 1)
    weave = jnp.where(co == (ro % 2) * 16 + (ro // 16) * 8 + (ro % 16) // 2, 1.0, 0.0).astype(BF16)

    def spread(source, target, t):
        for pp in range(2):
            for i in range(4):
                y = jnp.dot(weave, source[t, pp, i], preferred_element_type=F32).astype(BF16)
                target[0, t, 2 * i + pp] = y[0:16]
                target[1, t, 2 * i + pp] = y[16:32]

    loads[0].wait()
    patches = new_lat[...].reshape(128, 128)
    ro = lax.broadcasted_iota(jnp.int32, (256, 128), 0)
    co = lax.broadcasted_iota(jnp.int32, (256, 128), 1)
    grown = [
        jnp.dot(
            jnp.where((co == ro // 16 * 8 + ro % 16 // 2) & (ro % 2 == q), 1.0, 0.0).astype(BF16),
            patches,
            preferred_element_type=F32,
        )
        for q in range(2)
    ]
    grown = jnp.where(co // 16 % 2 == 0, grown[0], grown[1])
    ro = lax.broadcasted_iota(jnp.int32, (128, CZ), 0)
    for p in range(2):
        fold = (ro // 32 == 2 + p) & (ro % CZ == lax.broadcasted_iota(jnp.int32, (128, CZ), 1))
        y = jnp.dot(
            grown.astype(BF16), jnp.where(fold, 1.0, 0.0).astype(BF16), preferred_element_type=F32
        ).astype(BF16)
        for t in range(2):
            for i in range(4):
                for st in range(2):
                    row = ((t * 4 + i) * 2 + st) * 16
                    new_lat_out[st, t, 2 * i + p] = y[row : row + 16]
    loads[1].wait()
    for t in range(2):
        spread(new_mid, new_mid_out, t)
    loads[2].wait()
    for t in range(4):
        spread(decoded, decoded_out, t)


def shards(
    n_dec,
    n_row,
    hidden,
    head_weight,
    head_bias,
    lat_cache,
    mid_cache,
    moves,
    span_index,
    conv_in_weight,
    conv_in_bias,
    gn_gain,
    gn_bias,
    mid_weight,
    mid_bias,
):
    slots = n_dec * 2
    depth = hidden.shape[-1]
    vm = pl.BlockSpec(memory_space=pltpu.VMEM)
    sm = pl.BlockSpec(memory_space=pltpu.SMEM)
    hbm = pl.BlockSpec(memory_space=pl.ANY)
    dma = pltpu.SemaphoreType.DMA
    parts = pl.pallas_call(
        functools.partial(kernel, n_dec, n_row),
        out_shape=(
            jax.ShapeDtypeStruct((4, 2, 4, 32, 256), BF16),
            jax.ShapeDtypeStruct((2, 4, 16, 128), BF16),
            jax.ShapeDtypeStruct((2, 2, 4, 32, 256), BF16),
        ),
        in_specs=[hbm, vm, vm, vm, hbm, sm, sm, vm, vm, vm, vm, hbm, vm],
        out_specs=(hbm, hbm, hbm),
        scratch_shapes=[
            pltpu.VMEM((4, 2, 4, 32, 256), BF16),
            pltpu.VMEM((2, 4, 16, 128), BF16),
            pltpu.VMEM((2, 2, 4, 32, 256), BF16),
            pltpu.VMEM((2, 32, 128), BF16),
            pltpu.VMEM((256, depth), BF16),
            pltpu.VMEM((9, 1536, 256), BF16),
            pltpu.VMEM((2, 4, 16, 128), F32),
            pltpu.VMEM((2, 4, 16, 128), F32),
            pltpu.VMEM((2, 2, 2, 16, 128), F32),
            pltpu.VMEM((slots, 32, 128), BF16),
            pltpu.VMEM((4, 16, 128), F32),
            pltpu.VMEM((2, 16, 128), F32),
            pltpu.VMEM((27, CZ, 256), BF16),
            pltpu.VMEM((3, 1, 512), F32),
            pltpu.VMEM((4, 3, 256, 512), BF16),
            pltpu.VMEM((2, 6, 6, 16, 128), BF16),
            pltpu.VMEM((4, 4, 5, 16, 512), BF16),
            pltpu.VMEM((2, 8, 256), F32),
            pltpu.VMEM((2, n_row - 1, 8, 256), F32),
            pltpu.VMEM((slots, 4, 16, 256), BF16),
            pltpu.VMEM((slots, 4, 16, 256), BF16),
            pltpu.VMEM((slots, 4, 16, 256), BF16),
            pltpu.VMEM((slots, 4, 16, 256), BF16),
            pltpu.VMEM((4, 4, 32, 256), BF16),
            pltpu.VMEM((2, 10, 32, 512), BF16),
            pltpu.VMEM((2, 4, 6, 5, 16, 512), BF16),
            pltpu.VMEM((4, 4, 64, 256), F32),
            dma((12,)),
            dma((n_dec - 1,)),
            dma((n_dec - 1,)),
            dma((n_dec - 1, 4)),
            dma((n_dec - 1, 4)),
            dma((4, 4)),
            dma((4, 4)),
            dma((5,)),
            dma((5,)),
            dma((5,)),
            dma((5,)),
            dma((2,)),
            dma((2,)),
            dma((2, n_row - 1)),
            dma((2, n_row - 1)),
            dma((4, 3)),
            dma((4, 3)),
        ],
        compiler_params=pltpu.CompilerParams(
            collective_id=0, has_side_effects=True, vmem_limit_bytes=56 * 1024 * 1024
        ),
        cost_estimate=pl.CostEstimate(
            flops=9_000_000_000, bytes_accessed=12_000_000, transcendentals=700_000
        ),
    )(
        hidden.reshape(256, depth),
        head_weight.T,
        head_bias.reshape(1, 64),
        lat_cache,
        mid_cache,
        moves,
        span_index,
        conv_in_weight.reshape(27, CZ, 256),
        conv_in_bias.reshape(1, 256),
        gn_gain.reshape(1, 256),
        gn_bias.reshape(1, 256),
        mid_weight.reshape(9, 1536, 256),
        mid_bias.reshape(1, 256),
    )
    return pl.pallas_call(
        weave_kernel,
        out_shape=(
            jax.ShapeDtypeStruct((2, 4, 8, 16, 256), BF16),
            jax.ShapeDtypeStruct((2, 2, 8, 16, CZ), BF16),
            jax.ShapeDtypeStruct((2, 2, 8, 16, 256), BF16),
        ),
        in_specs=[hbm, hbm, hbm],
        out_specs=(vm, vm, vm),
        scratch_shapes=[
            pltpu.VMEM((4, 2, 4, 32, 256), BF16),
            pltpu.VMEM((2, 4, 16, 128), BF16),
            pltpu.VMEM((2, 2, 4, 32, 256), BF16),
            dma((3,)),
        ],
        compiler_params=pltpu.CompilerParams(vmem_limit_bytes=60 * 1024 * 1024),
        cost_estimate=pl.CostEstimate(flops=30_000_000, bytes_accessed=1_600_000, transcendentals=0),
    )(*parts)


def solution(mesh):
    placed = (
        P("dec", None, "row", None, "section"),
        P("section", None),
        P(),
        P("dec", None, "row", None, None),
        P("dec", None, "row", None, "section"),
        P(),
        P("dec"),
        P(None, None, None, None, "section"),
        P("section"),
        P("section"),
        P("section"),
        P(None, None, None, None, "section"),
        P("section"),
    )
    return jax.shard_map(
        functools.partial(shards, mesh.shape["dec"], mesh.shape["row"]),
        mesh=mesh,
        in_specs=placed,
        out_specs=(
            P("dec", None, "row", None, "section"),
            P("dec", None, "row", None, None),
            P("dec", None, "row", None, "section"),
        ),
        check_vma=False,
    )
```

```python
import functools

import jax
import jax.numpy as jnp
from jax import lax
from jax.experimental import pallas as pl
from jax.experimental.pallas import tpu as pltpu
from jax.sharding import PartitionSpec as P

CZ = 16
GROUP = 16
MESH = pl.DeviceIdType.MESH
F32 = jnp.float32
BF16 = jnp.bfloat16


def shifted(flat, step):
    n = flat.shape[0]
    j = lax.broadcasted_iota(jnp.int32, flat.shape, 0) % 8
    if step < 0:
        return jnp.where(j == 0, 0.0, pltpu.roll(flat, 1, 0))
    return jnp.where(j == 7, 0.0, pltpu.roll(flat, n - 1, 0))


def kernel(
    n_dec,
    n_row,
    hidden,
    head_t,
    head_bias,
    lat,
    mid,
    moves,
    span,
    cw,
    cb,
    gain,
    gbias,
    midw,
    midb,
    decoded,
    new_lat,
    new_mid,
    dec_v,
    nl_v,
    nm_v,
    lat_pk,
    hid_v,
    midw_v,
    part,
    part_x,
    part_h,
    lat_all,
    lat_own,
    lat_h,
    cw_in,
    par_all,
    wide,
    z,
    h1,
    stats,
    stats_in,
    gm0,
    gm1,
    gm2,
    gm3,
    sel,
    pm,
    mb,
    acc,
    local_sem,
    lat_s,
    lat_r,
    mid_s,
    mid_r,
    hop_s,
    hop_r,
    w_s,
    w_r,
    part_s,
    part_r,
    lh_s,
    lh_r,
    st_s,
    st_r,
    pm_s,
    pm_r,
):
    s = lax.axis_index("section")
    d = lax.axis_index("dec")
    r = lax.axis_index("row")
    o = 1 - s
    lanes = pl.ds(pl.multiple_of(s * 256, 256), 256)
    olanes = pl.ds(pl.multiple_of(o * 256, 256), 256)
    has_up = r > 0
    has_down = r < n_row - 1

    barrier = pltpu.get_barrier_semaphore()

    def greet(dev):
        pl.semaphore_signal(barrier, inc=1, device_id=dev, device_id_type=MESH)

    greet((o, d, r))
    for k in range(1, n_dec):
        greet((s, lax.rem(d + k, n_dec), r))
    for k in range(1, n_row):
        greet((s, d, lax.rem(r + k, n_row)))
        greet((o, d, lax.rem(r + k, n_row)))

    load_hidden = pltpu.make_async_copy(hidden, hid_v, local_sem.at[0])
    load_hidden.start()
    gm = (gm0, gm1, gm2, gm3)

    def chunk(c):
        return mid.at[:, 1 - c // 2, 4 * (c % 2) : 4 * (c % 2) + 4]

    own_mid = [
        pltpu.make_async_copy(chunk(c), gm[c].at[pl.ds(2 * d, 2)], local_sem.at[8 + c])
        for c in range(4)
    ]
    for c in own_mid:
        c.start()
    load_w = pltpu.make_async_copy(midw, midw_v, local_sem.at[3])

    pl.semaphore_wait(barrier, 1 + (n_dec - 1) + 2 * (n_row - 1))

    def remote(src, dst, ssem, rsem, dev):
        return pltpu.make_async_remote_copy(
            src_ref=src, dst_ref=dst, send_sem=ssem, recv_sem=rsem, device_id=dev, device_id_type=MESH
        )

    def lat_copy(k, origin):
        return remote(
            lat_pk, lat_all.at[pl.ds(2 * origin, 2)], lat_s.at[k - 1], lat_r.at[k - 1],
            (s, lax.rem(d + k, n_dec), r),
        )

    def mid_copy(k, origin, f):
        return remote(
            chunk(f), gm[f].at[pl.ds(2 * origin, 2)], mid_s.at[k - 1, f], mid_r.at[k - 1, f],
            (s, lax.rem(d + k, n_dec), r),
        )

    line = n_dec == 4
    inner = (d == 1) | (d == 2)
    end = 3 * (d - 1)
    near = 1 + d // 3

    def end_copy(f):
        return remote(
            chunk(f), gm[f].at[pl.ds(2 * d, 2)], hop_s.at[0, f], hop_r.at[0, f], (s, near, r)
        )

    def cross_copy(f):
        return remote(
            chunk(f), gm[f].at[pl.ds(2 * d, 2)], hop_s.at[1, f], hop_r.at[1, f], (s, 3 - d, r)
        )

    def pass_copy(f):
        slots = pl.ds(2 * end, 2)
        return remote(
            gm[f].at[slots], gm[f].at[slots], hop_s.at[2, f], hop_r.at[2, f], (s, 3 - d, r)
        )

    def pick_copy(f, target):
        return remote(sel.at[f], sel.at[f], hop_s.at[3, f], hop_r.at[3, f], (s, target, r))

    def pass_on(f):
        if line:

            @pl.when(inner)
            def _():
                end_copy(f).wait_recv()
                pass_copy(f).start()

    half = lax.rem(r, 2)
    half_lanes = pl.ds(pl.multiple_of(half * 128, 128), 128)
    cw_copy = remote(
        cw.at[:, :, half_lanes], cw_in.at[:, :, half_lanes], w_s.at[0], w_r.at[0], (o, d, r)
    )
    cw_copy.start()
    cw_pass = remote(
        cw_in.at[:, :, half_lanes], cw_in.at[:, :, half_lanes], w_s.at[4], w_r.at[4],
        (s, d, r + 1 - 2 * half),
    )
    par_copies = [
        remote(ref, par_all.at[n, :, lanes], w_s.at[n + 1], w_r.at[n + 1], (o, d, r))
        for n, ref in enumerate((cb, gain, gbias))
    ]
    for c in par_copies:
        c.start()
    ri = lax.broadcasted_iota(jnp.int32, (CZ, 128), 0)
    ci = lax.broadcasted_iota(jnp.int32, (CZ, 128), 1)
    tile = jnp.where(ci % CZ == ri, 1.0, 0.0).astype(BF16)
    wide_lat = jnp.dot(lat[...].reshape(512, CZ), tile, preferred_element_type=F32)
    wide_lat = wide_lat.reshape(2, 2, 4, 2, 16, 128)
    lane6 = lax.broadcasted_iota(jnp.int32, (2, 4, 16, 128), 3) // 32
    merged = jnp.where(
        lane6 == 0,
        wide_lat[:, 0, :, 0],
        jnp.where(lane6 == 1, wide_lat[:, 0, :, 1], jnp.where(lane6 == 2, wide_lat[:, 1, :, 0], wide_lat[:, 1, :, 1])),
    )
    merged = merged.reshape(128, 128).astype(BF16)
    ri = lax.broadcasted_iota(jnp.int32, (64, 128), 0)
    ci = lax.broadcasted_iota(jnp.int32, (64, 128), 1)
    halves = [
        jnp.dot(
            jnp.where(ci == ri // 8 * 16 + 2 * (ri % 8) + q, 1.0, 0.0).astype(BF16),
            merged,
            preferred_element_type=F32,
        )
        for q in range(2)
    ]
    lat_pk[...] = (
        jnp.where(ci // 16 % 2 == 0, halves[0], halves[1]).astype(BF16).reshape(2, 32, 128)
    )

    for k in range(1, n_dec):
        lat_copy(k, d).start()

    def send_end(*chunks):
        if line:

            @pl.when(jnp.logical_not(inner))
            def _():
                for c in chunks:
                    end_copy(c).start()

    def send_cross(*chunks):
        if line:

            @pl.when(inner)
            def _():
                for c in chunks:
                    cross_copy(c).start()

    send_end(0)
    send_cross(0, 1)
    if not line:
        for k in range(1, n_dec):
            for f in range(4):
                mid_copy(k, d, f).start()

    load_hidden.wait()
    load_w.start()
    head = lax.dot_general(
        hid_v[...],
        jnp.concatenate([head_t[...], jnp.zeros_like(head_t)], axis=0),
        (((1,), (1,)), ((), ())),
        preferred_element_type=F32,
    )
    head = head.reshape(2, 4, 4, 8, 128)
    lane = lax.broadcasted_iota(jnp.int32, (4, 8, 128), 2)
    for t in range(2):
        for st in range(2):
            high = pltpu.roll(head[st, t + 2].reshape(32, 128), 64, 1).reshape(4, 8, 128)
            part[t, :, pl.ds(8 * st, 8), :] = jnp.where(lane < 64, head[st, t], high)

    def part_copies():
        full = remote(part, part_x, part_s.at[0], part_r.at[0], (o, d, r))
        up = [
            remote(part.at[:, 0], part_h.at[1, n], part_s.at[1 + n], part_r.at[1 + n], (dev, d, r - 1))
            for n, dev in enumerate((s, o))
        ]
        down = [
            remote(part.at[:, 3], part_h.at[0, n], part_s.at[3 + n], part_r.at[3 + n], (dev, d, r + 1))
            for n, dev in enumerate((s, o))
        ]
        return full, up, down

    full, up, down = part_copies()

    @pl.when(has_up)
    def _():
        for c in up:
            c.start()

    @pl.when(has_down)
    def _():
        for c in down:
            c.start()

    full.start()
    send_end(1)

    zero_slab = jnp.zeros((CZ, 256), BF16)

    def build(source, target):
        def one(a, carry):
            for pp in range(2):
                for qq in range(2):
                    for pos in range(16):
                        di, dj, p, q = pos // 8, pos // 4 % 2, pos // 2 % 2, pos % 2
                        b = 2 * di + p - 1 + pp
                        e = 2 * dj + q - 1 + qq
                        if 0 <= b < 3 and 0 <= e < 3:
                            slab = source[a * 9 + b * 3 + e]
                        else:
                            slab = zero_slab
                        wide[pp * 2 + qq, a, pl.ds(pos * 16, 16), target] = slab
            return carry

        lax.fori_loop(0, 3, one, 0)

    build(cw, lanes)
    lat_all[pl.ds(2 * d, 2)] = lat_pk[...]
    for n, ref in enumerate((cb, gain, gbias)):
        par_all[n, :, lanes] = ref[...]

    for k in range(1, n_dec):
        lat_copy(k, lax.rem(d + n_dec - k, n_dec)).wait_recv()
    for st in range(2):
        live = (span[st] > 0).astype(F32)
        x = lat_all[moves[2 * d + st]].astype(F32) * live
        lat_own[:, pl.ds(8 * st, 8), :] = x.reshape(4, 8, 128)
    lat_edge_up = remote(lat_own.at[0], lat_h.at[1], lh_s.at[0], lh_r.at[0], (s, d, r - 1))
    lat_edge_down = remote(lat_own.at[3], lat_h.at[0], lh_s.at[1], lh_r.at[1], (s, d, r + 1))

    @pl.when(has_up)
    def _():
        lat_edge_up.start()

    @pl.when(has_down)
    def _():
        lat_edge_down.start()

    send_end(2)
    send_cross(2)
    cw_copy.wait_recv()
    cw_pass.start()
    pass_on(0)
    send_end(3)

    full.wait_recv()

    @pl.when(has_up)
    def _():
        for c in down:
            c.wait_recv()
        lat_edge_down.wait_recv()

    @pl.when(has_down)
    def _():
        for c in up:
            c.wait_recv()
        lat_edge_up.wait_recv()

    bias = jnp.concatenate([head_bias[...], head_bias[...]], axis=1)

    def place(low, base, step, packed):
        count = packed.shape[0]
        flat = packed.astype(BF16).astype(F32).reshape(count * 16, 128)
        lane = lax.broadcasted_iota(jnp.int32, flat.shape, 1) < 64
        turn = pltpu.roll(flat, 64, 1)
        before = shifted(flat, -1)
        after = shifted(flat, 1)
        turn_before = pltpu.roll(before, 64, 1)
        turn_after = pltpu.roll(after, 64, 1)
        for q, frame, left, right in (
            (0, base, before, turn),
            (0, base + step, turn_before, flat),
            (1, base, flat, turn_after),
            (1, base + step, turn, after),
        ):
            z[q, frame, pl.ds(low, count)] = (
                jnp.where(lane, left, right).astype(BF16).reshape(count, 16, 128)
            )

    up_live = has_up.astype(F32)
    down_live = has_down.astype(F32)

    @pl.when(jnp.logical_not(has_up))
    def _():
        part_h[0] = jnp.zeros((2, 2, 16, 128), F32)
        lat_h[0] = jnp.zeros((16, 128), F32)

    @pl.when(jnp.logical_not(has_down))
    def _():
        part_h[1] = jnp.zeros((2, 2, 16, 128), F32)
        lat_h[1] = jnp.zeros((16, 128), F32)

    for t in range(2):
        own = part[t] + part_x[t] + bias
        nl_v[t] = own.astype(BF16)
        place(1, 2 + t, 2, own)
        place(0, 2 + t, 2, ((part_h[0, 0, t] + part_h[0, 1, t] + bias) * up_live)[None])
        place(5, 2 + t, 2, ((part_h[1, 0, t] + part_h[1, 1, t] + bias) * down_live)[None])
    place(1, 0, 1, lat_own[...])
    place(0, 0, 1, lat_h[0][None])
    place(5, 0, 1, lat_h[1][None])

    out_lat = pltpu.make_async_copy(nl_v, new_lat, local_sem.at[4])
    out_lat.start()
    pass_on(1)
    send_cross(3)

    def input_conv(pp, qq, row, count, part_lanes):
        out = jnp.zeros((64 * count, 256), F32)
        for a in range(3):
            lhs = jnp.concatenate(
                [
                    z[qq, a : a + 4, row + di : row + di + count].reshape(64 * count, 128)
                    for di in range(2)
                ],
                axis=1,
            )
            out = out + jnp.dot(lhs, wide[pp * 2 + qq, a, :, part_lanes], preferred_element_type=F32)
        first = (out + par_all[0, :, part_lanes]).astype(BF16)
        h1[pp * 2 + qq, :, row : row + count, :, part_lanes] = first.reshape(4, count, 16, 256)
        return first

    def stat_copies(n):
        return [
            remote(
                stats.at[n], stats_in.at[n, k - 1], st_s.at[n, k - 1], st_r.at[n, k - 1],
                (s, d, lax.rem(r + k, n_row)),
            )
            for k in range(1, n_row)
        ]

    def input_half(n, part_lanes):
        total = jnp.zeros((16, 256), F32)
        square = jnp.zeros((16, 256), F32)
        for pp in range(2):
            for qq in range(2):
                mine = input_conv(pp, qq, pp, 4, part_lanes).astype(F32).reshape(16, 16, 256)
                total = total + jnp.sum(mine, axis=0)
                square = square + jnp.sum(mine * mine, axis=0)
        stats[n] = jnp.concatenate(
            [
                jnp.sum(total[0:8], axis=0, keepdims=True),
                jnp.sum(total[8:16], axis=0, keepdims=True),
                jnp.sum(square[0:8], axis=0, keepdims=True),
                jnp.sum(square[8:16], axis=0, keepdims=True),
                jnp.zeros((4, 256), F32),
            ],
            axis=0,
        )
        for c in stat_copies(n):
            c.start()
        for pp in range(2):
            for qq in range(2):
                input_conv(pp, qq, 0 if pp == 1 else 4, 1, part_lanes)

    input_half(0, lanes)
    pass_on(2)
    cw_pass.wait_recv()
    build(cw_in, olanes)
    for n, ref in enumerate((cb, gain, gbias)):
        remote(ref, par_all.at[n, :, olanes], w_s.at[n + 1], w_r.at[n + 1], (o, d, r)).wait_recv()
    input_half(1, olanes)

    zero_row = jnp.zeros((2, 32, 512), BF16)

    @pl.when(jnp.logical_not(has_up))
    def _():
        pm[:, 0] = zero_row

    @pl.when(jnp.logical_not(has_down))
    def _():
        pm[:, 9] = zero_row

    def pm_full(c):
        low = 1 + 4 * (c % 2)
        block = pm.at[1 - c // 2, low : low + 4, :, lanes]
        return remote(block, block, pm_s.at[c, 0], pm_r.at[c, 0], (o, d, r))

    def pm_up(c):
        f = 1 - c // 2
        return [
            remote(pm.at[f, 1, :, lanes], pm.at[f, 9, :, lanes], pm_s.at[c, 1 + n], pm_r.at[c, 1 + n], (dev, d, r - 1))
            for n, dev in enumerate((s, o))
        ]

    def pm_down(c):
        f = 1 - c // 2
        return [
            remote(pm.at[f, 8, :, lanes], pm.at[f, 0, :, lanes], pm_s.at[c, 1 + n], pm_r.at[c, 1 + n], (dev, d, r + 1))
            for n, dev in enumerate((s, o))
        ]

    def share(c, pick):
        low = 1 + 4 * (c % 2)
        for st in range(2):
            live = (span[st] > 0).astype(BF16)
            pm[1 - c // 2, low : low + 4, pl.ds(16 * st, 16), lanes] = pick(st) * live
        pm_full(c).start()
        if c % 2 == 0:

            @pl.when(has_up)
            def _():
                for e in pm_up(c):
                    e.start()

        else:

            @pl.when(has_down)
            def _():
                for e in pm_down(c):
                    e.start()

    def share_inner(f):
        if line:

            @pl.when(inner)
            def _():
                own_mid[f].wait()
                cross_copy(f).wait_recv()
                pass_copy(f).wait_recv()
                for st in range(2):
                    sel[f, :, pl.ds(16 * st, 16), :] = gm[f][moves[2 * end + st]]
                pick_copy(f, end).start()
                share(f, lambda st: gm[f][moves[2 * d + st]])

    def share_end(f):
        if line:

            @pl.when(jnp.logical_not(inner))
            def _():
                pick_copy(f, near).wait_recv()
                share(f, lambda st: sel[f, :, pl.ds(16 * st, 16), :])

        else:
            own_mid[f].wait()
            for k in range(1, n_dec):
                mid_copy(k, lax.rem(d + n_dec - k, n_dec), f).wait_recv()
            share(f, lambda st: gm[f][moves[2 * d + st]])

    pass_on(3)
    share_inner(0)

    def activate_half(n, part_lanes):
        for c in stat_copies(n):
            c.wait_recv()
        sums = stats[n]
        for k in range(1, n_row):
            sums = sums + stats_in[n, k - 1]
        lane8 = lax.broadcasted_iota(jnp.int32, (8, 256), 1)
        for k in (1, 2, 4, 8):
            other = jnp.where((lane8 & k) > 0, pltpu.roll(sums, k, 1), pltpu.roll(sums, 256 - k, 1))
            sums = sums + other
        sums = sums / (4 * 8 * 16 * GROUP * n_row)
        gv = sums[2:4] - sums[0:2] * sums[0:2]
        scale = 0.5 * (lax.rsqrt(gv + 1e-5) * par_all[1, :, part_lanes])
        shift = 0.5 * par_all[2, :, part_lanes]

        def spread(v):
            return jnp.concatenate(
                [jnp.broadcast_to(v[0:1], (8, 256)), jnp.broadcast_to(v[1:2], (8, 256))], axis=0
            )

        mean16 = spread(sums[0:2])
        scale16 = spread(scale)

        def activate(t, carry):
            for pp in range(2):
                for qq in range(2):
                    u = (h1[pp * 2 + qq, t, :, :, part_lanes].astype(F32) - mean16) * scale16 + shift
                    v = u * jnp.tanh(u) + u
                    mb[pp, qq, t + 2, :, :, part_lanes] = v.astype(BF16)
                    moved = shifted(v.reshape(80, 256), -1 if qq == 1 else 1)
                    mb[pp, 2 if qq == 1 else 3, t + 2, :, :, part_lanes] = moved.astype(BF16).reshape(
                        5, 16, 256
                    )
            return carry

        lax.fori_loop(0, 4, activate, 0)

    activate_half(0, lanes)
    share_inner(1)
    activate_half(1, olanes)

    @pl.when(jnp.logical_not(has_up))
    def _():
        mb[1, :, 2:6, 0] = jnp.zeros((4, 4, 16, 512), BF16)

    @pl.when(jnp.logical_not(has_down))
    def _():
        mb[0, :, 2:6, 4] = jnp.zeros((4, 4, 16, 512), BF16)

    share_inner(2)
    share_end(0)

    acc[...] = jnp.zeros_like(acc)

    def conv(b, pairs):
        for a, t0, nt in pairs:
            joined = 1 if nt == 4 else 4 if nt == 1 else 2
            for low in range(0, 4, joined):
                pieces = []
                for n in range(low, low + joined):
                    pp, qq = n // 2, n % 2
                    src = (b + 1) % 2 if pp == 0 else b % 2
                    off = b // 2 if pp == 0 else (b + 1) // 2
                    taps = (2, 0, 1) if qq == 0 else (0, 1, 3)
                    pieces.append(
                        jnp.concatenate(
                            [
                                mb[src, var, t0 + a : t0 + a + nt, pl.ds(off, 4)].reshape(nt * 64, 512)
                                for var in taps
                            ],
                            axis=1,
                        )
                    )
                lhs = pieces[0] if joined == 1 else jnp.concatenate(pieces, axis=0)
                got = jnp.dot(lhs, midw_v[a * 3 + b], preferred_element_type=F32)
                acc[low : low + joined, t0 : t0 + nt] += got.reshape(joined, nt, 64, 256)

    load_w.wait()

    def tap_late(b, carry):
        conv(b, ((2, 0, 4),))
        return carry

    lax.fori_loop(0, 1, tap_late, 0)
    share_inner(3)
    share_end(1)
    lax.fori_loop(1, 2, tap_late, 0)
    share_end(2)
    lax.fori_loop(2, 3, tap_late, 0)
    share_end(3)

    def tap_mid(k, carry):
        conv(k, ((1, 1, 3), (0, 2, 2)))
        return carry

    lax.fori_loop(0, 3, tap_mid, 0)

    ro = lax.broadcasted_iota(jnp.int32, (64, 32), 0)
    co = lax.broadcasted_iota(jnp.int32, (64, 32), 1)
    v4 = ro // 16
    j2 = 2 * (ro % 8)
    col = jnp.where(v4 == 0, j2, jnp.where(v4 == 1, j2 + 1, jnp.where(v4 == 2, j2 - 1, j2 + 2)))
    fits = (col >= 0) & (col < 16) & (co == (ro // 8) % 2 * 16 + col)
    deal = jnp.where(fits, 1.0, 0.0).astype(BF16)

    for t in range(2):
        for pp in range(2):
            for qq in range(2):
                nm_v[t, pp, :, pl.ds(16 * qq, 16), :] = mb[pp, qq, t + 4, pp : pp + 4, :, lanes]
    out_mid = pltpu.make_async_copy(nm_v, new_mid, local_sem.at[5])
    out_mid.start()

    def finish(t, carry):
        for pp in range(2):
            for qq in range(2):
                y = (
                    h1[pp * 2 + qq, t, pp : pp + 4, :, lanes].astype(F32)
                    + acc[pp * 2 + qq, t].reshape(4, 16, 256)
                    + midb[...]
                )
                dec_v[t, pp, :, pl.ds(16 * qq, 16), :] = y.astype(BF16)
        return carry

    lax.fori_loop(2, 4, finish, 0)
    out_late = pltpu.make_async_copy(
        dec_v.at[pl.ds(2, 2)], decoded.at[pl.ds(2, 2)], local_sem.at[6]
    )
    out_late.start()

    for f, pairs in ((1, ((1, 0, 1), (0, 1, 1))), (0, ((0, 0, 1),))):
        first = 2 - 2 * f
        pm_full(first).wait_recv()
        pm_full(first + 1).wait_recv()

        @pl.when(has_up)
        def _():
            for c in pm_down(first + 1):
                c.wait_recv()

        @pl.when(has_down)
        def _():
            for c in pm_up(first):
                c.wait_recv()

        for row in range(10):
            y = jnp.dot(deal, pm[f, row], preferred_element_type=F32).astype(BF16)
            for v in range(4):
                mb[(row + 1) % 2, v, f, row // 2] = y[16 * v : 16 * v + 16]

        def tap_early(b, carry):
            conv(b, pairs)
            return carry

        lax.fori_loop(0, 3, tap_early, 0)

    lax.fori_loop(0, 2, finish, 0)
    out_early = pltpu.make_async_copy(
        dec_v.at[pl.ds(0, 2)], decoded.at[pl.ds(0, 2)], local_sem.at[7]
    )
    out_early.start()

    for k in range(1, n_dec):
        lat_copy(k, d).wait_send()
    for c in par_copies + stat_copies(0) + stat_copies(1) + [full, cw_copy, cw_pass] + [pm_full(c) for c in range(4)]:
        c.wait_send()
    if line:

        @pl.when(inner)
        def _():
            for f in range(4):
                cross_copy(f).wait_send()
                pass_copy(f).wait_send()
                pick_copy(f, end).wait_send()

        @pl.when(jnp.logical_not(inner))
        def _():
            for f in range(4):
                end_copy(f).wait_send()
                own_mid[f].wait()

    else:
        for k in range(1, n_dec):
            for f in range(4):
                mid_copy(k, d, f).wait_send()

    @pl.when(has_up)
    def _():
        for c in up + pm_up(0) + pm_up(2) + [lat_edge_up]:
            c.wait_send()

    @pl.when(has_down)
    def _():
        for c in down + pm_down(1) + pm_down(3) + [lat_edge_down]:
            c.wait_send()
    for c in (out_lat, out_mid, out_late, out_early):
        c.wait()


def weave_kernel(
    decoded_in, new_lat_in, new_mid_in, decoded_out, new_lat_out, new_mid_out, decoded, new_lat, new_mid, sem
):
    loads = [
        pltpu.make_async_copy(source, target, sem.at[n])
        for n, (source, target) in enumerate(
            ((new_lat_in, new_lat), (new_mid_in, new_mid), (decoded_in, decoded))
        )
    ]
    for c in loads:
        c.start()
    ro = lax.broadcasted_iota(jnp.int32, (32, 32), 0)
    co = lax.broadcasted_iota(jnp.int32, (32, 32), 1)
    weave = jnp.where(co == (ro % 2) * 16 + (ro // 16) * 8 + (ro % 16) // 2, 1.0, 0.0).astype(BF16)

    def spread(source, target, t):
        for pp in range(2):
            for i in range(4):
                y = jnp.dot(weave, source[t, pp, i], preferred_element_type=F32).astype(BF16)
                target[0, t, 2 * i + pp] = y[0:16]
                target[1, t, 2 * i + pp] = y[16:32]

    loads[0].wait()
    patches = new_lat[...].reshape(128, 128)
    ro = lax.broadcasted_iota(jnp.int32, (256, 128), 0)
    co = lax.broadcasted_iota(jnp.int32, (256, 128), 1)
    grown = [
        jnp.dot(
            jnp.where((co == ro // 16 * 8 + ro % 16 // 2) & (ro % 2 == q), 1.0, 0.0).astype(BF16),
            patches,
            preferred_element_type=F32,
        )
        for q in range(2)
    ]
    grown = jnp.where(co // 16 % 2 == 0, grown[0], grown[1])
    ro = lax.broadcasted_iota(jnp.int32, (128, CZ), 0)
    for p in range(2):
        fold = (ro // 32 == 2 + p) & (ro % CZ == lax.broadcasted_iota(jnp.int32, (128, CZ), 1))
        y = jnp.dot(
            grown.astype(BF16), jnp.where(fold, 1.0, 0.0).astype(BF16), preferred_element_type=F32
        ).astype(BF16)
        for t in range(2):
            for i in range(4):
                for st in range(2):
                    row = ((t * 4 + i) * 2 + st) * 16
                    new_lat_out[st, t, 2 * i + p] = y[row : row + 16]
    loads[1].wait()
    for t in range(2):
        spread(new_mid, new_mid_out, t)
    loads[2].wait()
    for t in range(4):
        spread(decoded, decoded_out, t)


def shards(
    n_dec,
    n_row,
    hidden,
    head_weight,
    head_bias,
    lat_cache,
    mid_cache,
    moves,
    span_index,
    conv_in_weight,
    conv_in_bias,
    gn_gain,
    gn_bias,
    mid_weight,
    mid_bias,
):
    slots = n_dec * 2
    depth = hidden.shape[-1]
    vm = pl.BlockSpec(memory_space=pltpu.VMEM)
    sm = pl.BlockSpec(memory_space=pltpu.SMEM)
    hbm = pl.BlockSpec(memory_space=pl.ANY)
    dma = pltpu.SemaphoreType.DMA
    parts = pl.pallas_call(
        functools.partial(kernel, n_dec, n_row),
        out_shape=(
            jax.ShapeDtypeStruct((4, 2, 4, 32, 256), BF16),
            jax.ShapeDtypeStruct((2, 4, 16, 128), BF16),
            jax.ShapeDtypeStruct((2, 2, 4, 32, 256), BF16),
        ),
        in_specs=[hbm, vm, vm, vm, hbm, sm, sm, vm, vm, vm, vm, hbm, vm],
        out_specs=(hbm, hbm, hbm),
        scratch_shapes=[
            pltpu.VMEM((4, 2, 4, 32, 256), BF16),
            pltpu.VMEM((2, 4, 16, 128), BF16),
            pltpu.VMEM((2, 2, 4, 32, 256), BF16),
            pltpu.VMEM((2, 32, 128), BF16),
            pltpu.VMEM((256, depth), BF16),
            pltpu.VMEM((9, 1536, 256), BF16),
            pltpu.VMEM((2, 4, 16, 128), F32),
            pltpu.VMEM((2, 4, 16, 128), F32),
            pltpu.VMEM((2, 2, 2, 16, 128), F32),
            pltpu.VMEM((slots, 32, 128), BF16),
            pltpu.VMEM((4, 16, 128), F32),
            pltpu.VMEM((2, 16, 128), F32),
            pltpu.VMEM((27, CZ, 256), BF16),
            pltpu.VMEM((3, 1, 512), F32),
            pltpu.VMEM((4, 3, 256, 512), BF16),
            pltpu.VMEM((2, 6, 6, 16, 128), BF16),
            pltpu.VMEM((4, 4, 5, 16, 512), BF16),
            pltpu.VMEM((2, 8, 256), F32),
            pltpu.VMEM((2, n_row - 1, 8, 256), F32),
            pltpu.VMEM((slots, 4, 16, 256), BF16),
            pltpu.VMEM((slots, 4, 16, 256), BF16),
            pltpu.VMEM((slots, 4, 16, 256), BF16),
            pltpu.VMEM((slots, 4, 16, 256), BF16),
            pltpu.VMEM((4, 4, 32, 256), BF16),
            pltpu.VMEM((2, 10, 32, 512), BF16),
            pltpu.VMEM((2, 4, 6, 5, 16, 512), BF16),
            pltpu.VMEM((4, 4, 64, 256), F32),
            dma((12,)),
            dma((n_dec - 1,)),
            dma((n_dec - 1,)),
            dma((n_dec - 1, 4)),
            dma((n_dec - 1, 4)),
            dma((4, 4)),
            dma((4, 4)),
            dma((5,)),
            dma((5,)),
            dma((5,)),
            dma((5,)),
            dma((2,)),
            dma((2,)),
            dma((2, n_row - 1)),
            dma((2, n_row - 1)),
            dma((4, 3)),
            dma((4, 3)),
        ],
        compiler_params=pltpu.CompilerParams(
            collective_id=0, has_side_effects=True, vmem_limit_bytes=56 * 1024 * 1024
        ),
        cost_estimate=pl.CostEstimate(
            flops=9_000_000_000, bytes_accessed=12_000_000, transcendentals=700_000
        ),
    )(
        hidden.reshape(256, depth),
        head_weight.T,
        head_bias.reshape(1, 64),
        lat_cache,
        mid_cache,
        moves,
        span_index,
        conv_in_weight.reshape(27, CZ, 256),
        conv_in_bias.reshape(1, 256),
        gn_gain.reshape(1, 256),
        gn_bias.reshape(1, 256),
        mid_weight.reshape(9, 1536, 256),
        mid_bias.reshape(1, 256),
    )
    return pl.pallas_call(
        weave_kernel,
        out_shape=(
            jax.ShapeDtypeStruct((2, 4, 8, 16, 256), BF16),
            jax.ShapeDtypeStruct((2, 2, 8, 16, CZ), BF16),
            jax.ShapeDtypeStruct((2, 2, 8, 16, 256), BF16),
        ),
        in_specs=[hbm, hbm, hbm],
        out_specs=(vm, vm, vm),
        scratch_shapes=[
            pltpu.VMEM((4, 2, 4, 32, 256), BF16),
            pltpu.VMEM((2, 4, 16, 128), BF16),
            pltpu.VMEM((2, 2, 4, 32, 256), BF16),
            dma((3,)),
        ],
        compiler_params=pltpu.CompilerParams(vmem_limit_bytes=60 * 1024 * 1024),
        cost_estimate=pl.CostEstimate(flops=30_000_000, bytes_accessed=1_600_000, transcendentals=0),
    )(*parts)


def solution(mesh):
    placed = (
        P("dec", None, "row", None, "section"),
        P("section", None),
        P(),
        P("dec", None, "row", None, None),
        P("dec", None, "row", None, "section"),
        P(),
        P("dec"),
        P(None, None, None, None, "section"),
        P("section"),
        P("section"),
        P("section"),
        P(None, None, None, None, "section"),
        P("section"),
    )
    return jax.shard_map(
        functools.partial(shards, mesh.shape["dec"], mesh.shape["row"]),
        mesh=mesh,
        in_specs=placed,
        out_specs=(
            P("dec", None, "row", None, "section"),
            P("dec", None, "row", None, None),
            P("dec", None, "row", None, "section"),
        ),
        check_vma=False,
    )
```

```python
import functools

import jax
import jax.numpy as jnp
from jax import lax
from jax.experimental import pallas as pl
from jax.experimental.pallas import tpu as pltpu
from jax.sharding import PartitionSpec as P

CZ = 16
GROUP = 16
MESH = pl.DeviceIdType.MESH
F32 = jnp.float32
BF16 = jnp.bfloat16


def shifted(flat, step):
    n = flat.shape[0]
    j = lax.broadcasted_iota(jnp.int32, flat.shape, 0) % 8
    if step < 0:
        return jnp.where(j == 0, 0.0, pltpu.roll(flat, 1, 0))
    return jnp.where(j == 7, 0.0, pltpu.roll(flat, n - 1, 0))


def kernel(
    n_dec,
    n_row,
    hidden,
    head_t,
    head_bias,
    lat,
    mid,
    moves,
    span,
    cw,
    cb,
    gain,
    gbias,
    midw,
    midb,
    decoded,
    new_lat,
    new_mid,
    dec_v,
    nl_v,
    nm_v,
    lat_pk,
    hid_v,
    midw_v,
    part,
    part_x,
    part_h,
    lat_all,
    lat_own,
    lat_h,
    cw_in,
    par_all,
    wide,
    z,
    h1,
    stats,
    stats_in,
    gm0,
    gm1,
    gm2,
    gm3,
    sel,
    pm,
    mb,
    acc,
    local_sem,
    lat_s,
    lat_r,
    mid_s,
    mid_r,
    hop_s,
    hop_r,
    w_s,
    w_r,
    part_s,
    part_r,
    lh_s,
    lh_r,
    st_s,
    st_r,
    pm_s,
    pm_r,
):
    s = lax.axis_index("section")
    d = lax.axis_index("dec")
    r = lax.axis_index("row")
    o = 1 - s
    lanes = pl.ds(pl.multiple_of(s * 256, 256), 256)
    olanes = pl.ds(pl.multiple_of(o * 256, 256), 256)
    has_up = r > 0
    has_down = r < n_row - 1

    barrier = pltpu.get_barrier_semaphore()

    def greet(dev):
        pl.semaphore_signal(barrier, inc=1, device_id=dev, device_id_type=MESH)

    greet((o, d, r))
    for k in range(1, n_dec):
        greet((s, lax.rem(d + k, n_dec), r))
    for k in range(1, n_row):
        greet((s, d, lax.rem(r + k, n_row)))
        greet((o, d, lax.rem(r + k, n_row)))

    load_hidden = pltpu.make_async_copy(hidden, hid_v, local_sem.at[0])
    load_hidden.start()
    gm = (gm0, gm1, gm2, gm3)

    def chunk(c):
        return mid.at[:, 1 - c // 2, 4 * (c % 2) : 4 * (c % 2) + 4]

    own_mid = [
        pltpu.make_async_copy(chunk(c), gm[c].at[pl.ds(2 * d, 2)], local_sem.at[8 + c])
        for c in range(4)
    ]
    for c in own_mid:
        c.start()
    load_w = pltpu.make_async_copy(midw, midw_v, local_sem.at[3])

    pl.semaphore_wait(barrier, 1 + (n_dec - 1) + 2 * (n_row - 1))

    def remote(src, dst, ssem, rsem, dev):
        return pltpu.make_async_remote_copy(
            src_ref=src, dst_ref=dst, send_sem=ssem, recv_sem=rsem, device_id=dev, device_id_type=MESH
        )

    def lat_copy(k, origin):
        return remote(
            lat_pk, lat_all.at[pl.ds(2 * origin, 2)], lat_s.at[k - 1], lat_r.at[k - 1],
            (s, lax.rem(d + k, n_dec), r),
        )

    def mid_copy(k, origin, f):
        return remote(
            chunk(f), gm[f].at[pl.ds(2 * origin, 2)], mid_s.at[k - 1, f], mid_r.at[k - 1, f],
            (s, lax.rem(d + k, n_dec), r),
        )

    line = n_dec == 4
    inner = (d == 1) | (d == 2)
    end = 3 * (d - 1)
    near = 1 + d // 3

    def end_copy(f):
        return remote(
            chunk(f), gm[f].at[pl.ds(2 * d, 2)], hop_s.at[0, f], hop_r.at[0, f], (s, near, r)
        )

    def cross_copy(f):
        return remote(
            chunk(f), gm[f].at[pl.ds(2 * d, 2)], hop_s.at[1, f], hop_r.at[1, f], (s, 3 - d, r)
        )

    def pass_copy(f):
        slots = pl.ds(2 * end, 2)
        return remote(
            gm[f].at[slots], gm[f].at[slots], hop_s.at[2, f], hop_r.at[2, f], (s, 3 - d, r)
        )

    def pick_copy(f, target):
        return remote(sel.at[f], sel.at[f], hop_s.at[3, f], hop_r.at[3, f], (s, target, r))

    def pass_on(f):
        if line:

            @pl.when(inner)
            def _():
                end_copy(f).wait_recv()
                pass_copy(f).start()

    half = lax.rem(r, 2)
    half_lanes = pl.ds(pl.multiple_of(half * 128, 128), 128)
    cw_copy = remote(
        cw.at[:, :, half_lanes], cw_in.at[:, :, half_lanes], w_s.at[0], w_r.at[0], (o, d, r)
    )
    cw_copy.start()
    cw_pass = remote(
        cw_in.at[:, :, half_lanes], cw_in.at[:, :, half_lanes], w_s.at[4], w_r.at[4],
        (s, d, r + 1 - 2 * half),
    )
    par_copies = [
        remote(ref, par_all.at[n, :, lanes], w_s.at[n + 1], w_r.at[n + 1], (o, d, r))
        for n, ref in enumerate((cb, gain, gbias))
    ]
    for c in par_copies:
        c.start()
    ri = lax.broadcasted_iota(jnp.int32, (CZ, 128), 0)
    ci = lax.broadcasted_iota(jnp.int32, (CZ, 128), 1)
    tile = jnp.where(ci % CZ == ri, 1.0, 0.0).astype(BF16)
    wide_lat = jnp.dot(lat[...].reshape(512, CZ), tile, preferred_element_type=F32)
    wide_lat = wide_lat.reshape(2, 2, 4, 2, 16, 128)
    lane6 = lax.broadcasted_iota(jnp.int32, (2, 4, 16, 128), 3) // 32
    merged = jnp.where(
        lane6 == 0,
        wide_lat[:, 0, :, 0],
        jnp.where(lane6 == 1, wide_lat[:, 0, :, 1], jnp.where(lane6 == 2, wide_lat[:, 1, :, 0], wide_lat[:, 1, :, 1])),
    )
    merged = merged.reshape(128, 128).astype(BF16)
    ri = lax.broadcasted_iota(jnp.int32, (64, 128), 0)
    ci = lax.broadcasted_iota(jnp.int32, (64, 128), 1)
    halves = [
        jnp.dot(
            jnp.where(ci == ri // 8 * 16 + 2 * (ri % 8) + q, 1.0, 0.0).astype(BF16),
            merged,
            preferred_element_type=F32,
        )
        for q in range(2)
    ]
    lat_pk[...] = (
        jnp.where(ci // 16 % 2 == 0, halves[0], halves[1]).astype(BF16).reshape(2, 32, 128)
    )

    for k in range(1, n_dec):
        lat_copy(k, d).start()

    def send_end(*chunks):
        if line:

            @pl.when(jnp.logical_not(inner))
            def _():
                for c in chunks:
                    end_copy(c).start()

    def send_cross(*chunks):
        if line:

            @pl.when(inner)
            def _():
                for c in chunks:
                    cross_copy(c).start()

    send_end(0)
    send_cross(0, 1)
    if not line:
        for k in range(1, n_dec):
            for f in range(4):
                mid_copy(k, d, f).start()

    load_hidden.wait()
    load_w.start()
    head = lax.dot_general(
        hid_v[...],
        jnp.concatenate([head_t[...], jnp.zeros_like(head_t)], axis=0),
        (((1,), (1,)), ((), ())),
        preferred_element_type=F32,
    )
    head = head.reshape(2, 4, 4, 8, 128)
    lane = lax.broadcasted_iota(jnp.int32, (4, 8, 128), 2)
    for t in range(2):
        for st in range(2):
            high = pltpu.roll(head[st, t + 2].reshape(32, 128), 64, 1).reshape(4, 8, 128)
            part[t, :, pl.ds(8 * st, 8), :] = jnp.where(lane < 64, head[st, t], high)

    def part_copies():
        full = remote(part, part_x, part_s.at[0], part_r.at[0], (o, d, r))
        up = [
            remote(part.at[:, 0], part_h.at[1, n], part_s.at[1 + n], part_r.at[1 + n], (dev, d, r - 1))
            for n, dev in enumerate((s, o))
        ]
        down = [
            remote(part.at[:, 3], part_h.at[0, n], part_s.at[3 + n], part_r.at[3 + n], (dev, d, r + 1))
            for n, dev in enumerate((s, o))
        ]
        return full, up, down

    full, up, down = part_copies()

    @pl.when(has_up)
    def _():
        for c in up:
            c.start()

    @pl.when(has_down)
    def _():
        for c in down:
            c.start()

    full.start()
    send_end(1)

    zero_slab = jnp.zeros((CZ, 256), BF16)

    def build(source, target):
        def one(a, carry):
            for pp in range(2):
                for qq in range(2):
                    for pos in range(16):
                        di, dj, p, q = pos // 8, pos // 4 % 2, pos // 2 % 2, pos % 2
                        b = 2 * di + p - 1 + pp
                        e = 2 * dj + q - 1 + qq
                        if 0 <= b < 3 and 0 <= e < 3:
                            slab = source[a * 9 + b * 3 + e]
                        else:
                            slab = zero_slab
                        wide[pp * 2 + qq, a, pl.ds(pos * 16, 16), target] = slab
            return carry

        lax.fori_loop(0, 3, one, 0)

    build(cw, lanes)
    lat_all[pl.ds(2 * d, 2)] = lat_pk[...]
    for n, ref in enumerate((cb, gain, gbias)):
        par_all[n, :, lanes] = ref[...]

    for k in range(1, n_dec):
        lat_copy(k, lax.rem(d + n_dec - k, n_dec)).wait_recv()
    for st in range(2):
        live = (span[st] > 0).astype(F32)
        x = lat_all[moves[2 * d + st]].astype(F32) * live
        lat_own[:, pl.ds(8 * st, 8), :] = x.reshape(4, 8, 128)
    lat_edge_up = remote(lat_own.at[0], lat_h.at[1], lh_s.at[0], lh_r.at[0], (s, d, r - 1))
    lat_edge_down = remote(lat_own.at[3], lat_h.at[0], lh_s.at[1], lh_r.at[1], (s, d, r + 1))

    @pl.when(has_up)
    def _():
        lat_edge_up.start()

    @pl.when(has_down)
    def _():
        lat_edge_down.start()

    send_end(2)
    send_cross(2)
    cw_copy.wait_recv()
    cw_pass.start()
    pass_on(0)
    send_end(3)

    full.wait_recv()

    @pl.when(has_up)
    def _():
        for c in down:
            c.wait_recv()
        lat_edge_down.wait_recv()

    @pl.when(has_down)
    def _():
        for c in up:
            c.wait_recv()
        lat_edge_up.wait_recv()

    bias = jnp.concatenate([head_bias[...], head_bias[...]], axis=1)

    def place(low, base, step, packed):
        count = packed.shape[0]
        flat = packed.astype(BF16).astype(F32).reshape(count * 16, 128)
        lane = lax.broadcasted_iota(jnp.int32, flat.shape, 1) < 64
        turn = pltpu.roll(flat, 64, 1)
        before = shifted(flat, -1)
        after = shifted(flat, 1)
        turn_before = pltpu.roll(before, 64, 1)
        turn_after = pltpu.roll(after, 64, 1)
        for q, frame, left, right in (
            (0, base, before, turn),
            (0, base + step, turn_before, flat),
            (1, base, flat, turn_after),
            (1, base + step, turn, after),
        ):
            z[q, frame, pl.ds(low, count)] = (
                jnp.where(lane, left, right).astype(BF16).reshape(count, 16, 128)
            )

    up_live = has_up.astype(F32)
    down_live = has_down.astype(F32)

    @pl.when(jnp.logical_not(has_up))
    def _():
        part_h[0] = jnp.zeros((2, 2, 16, 128), F32)
        lat_h[0] = jnp.zeros((16, 128), F32)

    @pl.when(jnp.logical_not(has_down))
    def _():
        part_h[1] = jnp.zeros((2, 2, 16, 128), F32)
        lat_h[1] = jnp.zeros((16, 128), F32)

    for t in range(2):
        own = part[t] + part_x[t] + bias
        nl_v[t] = own.astype(BF16)
        place(1, 2 + t, 2, own)
        place(0, 2 + t, 2, ((part_h[0, 0, t] + part_h[0, 1, t] + bias) * up_live)[None])
        place(5, 2 + t, 2, ((part_h[1, 0, t] + part_h[1, 1, t] + bias) * down_live)[None])
    place(1, 0, 1, lat_own[...])
    place(0, 0, 1, lat_h[0][None])
    place(5, 0, 1, lat_h[1][None])

    out_lat = pltpu.make_async_copy(nl_v, new_lat, local_sem.at[4])
    out_lat.start()
    pass_on(1)
    send_cross(3)

    def input_conv(pp, qq, row, count, part_lanes):
        out = jnp.zeros((64 * count, 256), F32)
        for a in range(3):
            lhs = jnp.concatenate(
                [
                    z[qq, a : a + 4, row + di : row + di + count].reshape(64 * count, 128)
                    for di in range(2)
                ],
                axis=1,
            )
            out = out + jnp.dot(lhs, wide[pp * 2 + qq, a, :, part_lanes], preferred_element_type=F32)
        first = (out + par_all[0, :, part_lanes]).astype(BF16)
        h1[pp * 2 + qq, :, row : row + count, :, part_lanes] = first.reshape(4, count, 16, 256)
        return first

    def stat_copies(n):
        return [
            remote(
                stats.at[n], stats_in.at[n, k - 1], st_s.at[n, k - 1], st_r.at[n, k - 1],
                (s, d, lax.rem(r + k, n_row)),
            )
            for k in range(1, n_row)
        ]

    def input_half(n, part_lanes):
        total = jnp.zeros((16, 256), F32)
        square = jnp.zeros((16, 256), F32)
        for pp in range(2):
            for qq in range(2):
                mine = input_conv(pp, qq, pp, 4, part_lanes).astype(F32).reshape(16, 16, 256)
                total = total + jnp.sum(mine, axis=0)
                square = square + jnp.sum(mine * mine, axis=0)
        stats[n] = jnp.concatenate(
            [
                jnp.sum(total[0:8], axis=0, keepdims=True),
                jnp.sum(total[8:16], axis=0, keepdims=True),
                jnp.sum(square[0:8], axis=0, keepdims=True),
                jnp.sum(square[8:16], axis=0, keepdims=True),
                jnp.zeros((4, 256), F32),
            ],
            axis=0,
        )
        for c in stat_copies(n):
            c.start()
        for pp in range(2):
            for qq in range(2):
                input_conv(pp, qq, 0 if pp == 1 else 4, 1, part_lanes)

    input_half(0, lanes)
    pass_on(2)
    cw_pass.wait_recv()
    build(cw_in, olanes)
    for n, ref in enumerate((cb, gain, gbias)):
        remote(ref, par_all.at[n, :, olanes], w_s.at[n + 1], w_r.at[n + 1], (o, d, r)).wait_recv()
    input_half(1, olanes)

    zero_row = jnp.zeros((2, 32, 512), BF16)

    @pl.when(jnp.logical_not(has_up))
    def _():
        pm[:, 0] = zero_row

    @pl.when(jnp.logical_not(has_down))
    def _():
        pm[:, 9] = zero_row

    def pm_full(c):
        low = 1 + 4 * (c % 2)
        block = pm.at[1 - c // 2, low : low + 4, :, lanes]
        return remote(block, block, pm_s.at[c, 0], pm_r.at[c, 0], (o, d, r))

    def pm_up(c):
        f = 1 - c // 2
        return [
            remote(pm.at[f, 1, :, lanes], pm.at[f, 9, :, lanes], pm_s.at[c, 1 + n], pm_r.at[c, 1 + n], (dev, d, r - 1))
            for n, dev in enumerate((s, o))
        ]

    def pm_down(c):
        f = 1 - c // 2
        return [
            remote(pm.at[f, 8, :, lanes], pm.at[f, 0, :, lanes], pm_s.at[c, 1 + n], pm_r.at[c, 1 + n], (dev, d, r + 1))
            for n, dev in enumerate((s, o))
        ]

    def share(c, pick):
        low = 1 + 4 * (c % 2)
        for st in range(2):
            live = (span[st] > 0).astype(BF16)
            pm[1 - c // 2, low : low + 4, pl.ds(16 * st, 16), lanes] = pick(st) * live
        pm_full(c).start()
        if c % 2 == 0:

            @pl.when(has_up)
            def _():
                for e in pm_up(c):
                    e.start()

        else:

            @pl.when(has_down)
            def _():
                for e in pm_down(c):
                    e.start()

    def share_inner(f):
        if line:

            @pl.when(inner)
            def _():
                own_mid[f].wait()
                cross_copy(f).wait_recv()
                pass_copy(f).wait_recv()
                for st in range(2):
                    sel[f, :, pl.ds(16 * st, 16), :] = gm[f][moves[2 * end + st]]
                pick_copy(f, end).start()
                share(f, lambda st: gm[f][moves[2 * d + st]])

    def share_end(f):
        if line:

            @pl.when(jnp.logical_not(inner))
            def _():
                pick_copy(f, near).wait_recv()
                share(f, lambda st: sel[f, :, pl.ds(16 * st, 16), :])

        else:
            own_mid[f].wait()
            for k in range(1, n_dec):
                mid_copy(k, lax.rem(d + n_dec - k, n_dec), f).wait_recv()
            share(f, lambda st: gm[f][moves[2 * d + st]])

    pass_on(3)
    share_inner(0)

    def activate_half(n, part_lanes):
        for c in stat_copies(n):
            c.wait_recv()
        sums = stats[n]
        for k in range(1, n_row):
            sums = sums + stats_in[n, k - 1]
        lane8 = lax.broadcasted_iota(jnp.int32, (8, 256), 1)
        for k in (1, 2, 4, 8):
            other = jnp.where((lane8 & k) > 0, pltpu.roll(sums, k, 1), pltpu.roll(sums, 256 - k, 1))
            sums = sums + other
        sums = sums / (4 * 8 * 16 * GROUP * n_row)
        gv = sums[2:4] - sums[0:2] * sums[0:2]
        scale = 0.5 * (lax.rsqrt(gv + 1e-5) * par_all[1, :, part_lanes])
        shift = 0.5 * par_all[2, :, part_lanes]

        def spread(v):
            return jnp.concatenate(
                [jnp.broadcast_to(v[0:1], (8, 256)), jnp.broadcast_to(v[1:2], (8, 256))], axis=0
            )

        mean16 = spread(sums[0:2])
        scale16 = spread(scale)

        def activate(t, carry):
            for pp in range(2):
                for qq in range(2):
                    u = (h1[pp * 2 + qq, t, :, :, part_lanes].astype(F32) - mean16) * scale16 + shift
                    v = u * jnp.tanh(u) + u
                    mb[pp, qq, t + 2, :, :, part_lanes] = v.astype(BF16)
                    moved = shifted(v.reshape(80, 256), -1 if qq == 1 else 1)
                    mb[pp, 2 if qq == 1 else 3, t + 2, :, :, part_lanes] = moved.astype(BF16).reshape(
                        5, 16, 256
                    )
            return carry

        lax.fori_loop(0, 4, activate, 0)

    activate_half(0, lanes)
    share_inner(1)
    activate_half(1, olanes)

    @pl.when(jnp.logical_not(has_up))
    def _():
        mb[1, :, 2:6, 0] = jnp.zeros((4, 4, 16, 512), BF16)

    @pl.when(jnp.logical_not(has_down))
    def _():
        mb[0, :, 2:6, 4] = jnp.zeros((4, 4, 16, 512), BF16)

    share_inner(2)
    share_end(0)

    acc[...] = jnp.zeros_like(acc)

    def conv(b, pairs):
        for a, t0, nt in pairs:
            joined = 1 if nt == 4 else 4 if nt == 1 else 2
            for low in range(0, 4, joined):
                pieces = []
                for n in range(low, low + joined):
                    pp, qq = n // 2, n % 2
                    src = (b + 1) % 2 if pp == 0 else b % 2
                    off = b // 2 if pp == 0 else (b + 1) // 2
                    taps = (2, 0, 1) if qq == 0 else (0, 1, 3)
                    pieces.append(
                        jnp.concatenate(
                            [
                                mb[src, var, t0 + a : t0 + a + nt, pl.ds(off, 4)].reshape(nt * 64, 512)
                                for var in taps
                            ],
                            axis=1,
                        )
                    )
                lhs = pieces[0] if joined == 1 else jnp.concatenate(pieces, axis=0)
                got = jnp.dot(lhs, midw_v[a * 3 + b], preferred_element_type=F32)
                acc[low : low + joined, t0 : t0 + nt] += got.reshape(joined, nt, 64, 256)

    load_w.wait()

    def tap_late(b, carry):
        conv(b, ((2, 0, 4),))
        return carry

    lax.fori_loop(0, 1, tap_late, 0)
    share_inner(3)
    share_end(1)
    lax.fori_loop(1, 2, tap_late, 0)
    share_end(2)
    lax.fori_loop(2, 3, tap_late, 0)
    share_end(3)

    def tap_mid(k, carry):
        conv(k, ((1, 1, 3), (0, 2, 2)))
        return carry

    lax.fori_loop(0, 3, tap_mid, 0)

    ro = lax.broadcasted_iota(jnp.int32, (64, 32), 0)
    co = lax.broadcasted_iota(jnp.int32, (64, 32), 1)
    v4 = ro // 16
    j2 = 2 * (ro % 8)
    col = jnp.where(v4 == 0, j2, jnp.where(v4 == 1, j2 + 1, jnp.where(v4 == 2, j2 - 1, j2 + 2)))
    fits = (col >= 0) & (col < 16) & (co == (ro // 8) % 2 * 16 + col)
    deal = jnp.where(fits, 1.0, 0.0).astype(BF16)

    for t in range(2):
        for pp in range(2):
            for qq in range(2):
                nm_v[t, pp, :, pl.ds(16 * qq, 16), :] = mb[pp, qq, t + 4, pp : pp + 4, :, lanes]
    out_mid = pltpu.make_async_copy(nm_v, new_mid, local_sem.at[5])
    out_mid.start()

    def finish(t, carry):
        for pp in range(2):
            for qq in range(2):
                y = (
                    h1[pp * 2 + qq, t, pp : pp + 4, :, lanes].astype(F32)
                    + acc[pp * 2 + qq, t].reshape(4, 16, 256)
                    + midb[...]
                )
                dec_v[t, pp, :, pl.ds(16 * qq, 16), :] = y.astype(BF16)
        return carry

    lax.fori_loop(2, 4, finish, 0)
    out_late = pltpu.make_async_copy(
        dec_v.at[pl.ds(2, 2)], decoded.at[pl.ds(2, 2)], local_sem.at[6]
    )
    out_late.start()

    for f, pairs in ((1, ((1, 0, 1), (0, 1, 1))), (0, ((0, 0, 1),))):
        first = 2 - 2 * f
        pm_full(first).wait_recv()
        pm_full(first + 1).wait_recv()

        @pl.when(has_up)
        def _():
            for c in pm_down(first + 1):
                c.wait_recv()

        @pl.when(has_down)
        def _():
            for c in pm_up(first):
                c.wait_recv()

        for row in range(10):
            y = jnp.dot(deal, pm[f, row], preferred_element_type=F32).astype(BF16)
            for v in range(4):
                mb[(row + 1) % 2, v, f, row // 2] = y[16 * v : 16 * v + 16]

        def tap_early(b, carry):
            conv(b, pairs)
            return carry

        lax.fori_loop(0, 3, tap_early, 0)

    lax.fori_loop(0, 2, finish, 0)
    out_early = pltpu.make_async_copy(
        dec_v.at[pl.ds(0, 2)], decoded.at[pl.ds(0, 2)], local_sem.at[7]
    )
    out_early.start()

    for k in range(1, n_dec):
        lat_copy(k, d).wait_send()
    for c in par_copies + stat_copies(0) + stat_copies(1) + [full, cw_copy, cw_pass] + [pm_full(c) for c in range(4)]:
        c.wait_send()
    if line:

        @pl.when(inner)
        def _():
            for f in range(4):
                cross_copy(f).wait_send()
                pass_copy(f).wait_send()
                pick_copy(f, end).wait_send()

        @pl.when(jnp.logical_not(inner))
        def _():
            for f in range(4):
                end_copy(f).wait_send()
                own_mid[f].wait()

    else:
        for k in range(1, n_dec):
            for f in range(4):
                mid_copy(k, d, f).wait_send()

    @pl.when(has_up)
    def _():
        for c in up + pm_up(0) + pm_up(2) + [lat_edge_up]:
            c.wait_send()

    @pl.when(has_down)
    def _():
        for c in down + pm_down(1) + pm_down(3) + [lat_edge_down]:
            c.wait_send()
    for c in (out_lat, out_mid, out_late, out_early):
        c.wait()


def weave_kernel(
    decoded_in,
    new_lat_in,
    new_mid_in,
    decoded_hbm,
    new_lat_out,
    new_mid_hbm,
    decoded,
    new_lat,
    new_mid,
    decoded_out,
    new_mid_out,
    sem,
):
    loads = [
        pltpu.make_async_copy(source, target, sem.at[n])
        for n, (source, target) in enumerate(
            [(new_mid_in, new_mid)]
            + [(decoded_in.at[t], decoded.at[t]) for t in range(4)]
            + [(new_lat_in, new_lat)]
        )
    ]
    for c in loads:
        c.start()
    ro = lax.broadcasted_iota(jnp.int32, (32, 32), 0)
    co = lax.broadcasted_iota(jnp.int32, (32, 32), 1)
    weave = jnp.where(co == (ro % 2) * 16 + (ro // 16) * 8 + (ro % 16) // 2, 1.0, 0.0).astype(BF16)

    def spread(source, target, t):
        for pp in range(2):
            for i in range(4):
                y = jnp.dot(weave, source[t, pp, i], preferred_element_type=F32).astype(BF16)
                target[0, t, 2 * i + pp] = y[0:16]
                target[1, t, 2 * i + pp] = y[16:32]

    loads[0].wait()
    for t in range(2):
        spread(new_mid, new_mid_out, t)
    stores = [pltpu.make_async_copy(new_mid_out, new_mid_hbm, sem.at[6])]
    stores[0].start()
    for t in range(4):
        loads[1 + t].wait()
        spread(decoded, decoded_out, t)
        stores.append(
            pltpu.make_async_copy(decoded_out.at[:, t], decoded_hbm.at[:, t], sem.at[7 + t])
        )
        stores[-1].start()
    loads[5].wait()

    patches = new_lat[...].reshape(128, 128)
    ro = lax.broadcasted_iota(jnp.int32, (256, 128), 0)
    co = lax.broadcasted_iota(jnp.int32, (256, 128), 1)
    grown = [
        jnp.dot(
            jnp.where((co == ro // 16 * 8 + ro % 16 // 2) & (ro % 2 == q), 1.0, 0.0).astype(BF16),
            patches,
            preferred_element_type=F32,
        )
        for q in range(2)
    ]
    grown = jnp.where(co // 16 % 2 == 0, grown[0], grown[1])
    ro = lax.broadcasted_iota(jnp.int32, (128, CZ), 0)
    for p in range(2):
        fold = (ro // 32 == 2 + p) & (ro % CZ == lax.broadcasted_iota(jnp.int32, (128, CZ), 1))
        y = jnp.dot(
            grown.astype(BF16), jnp.where(fold, 1.0, 0.0).astype(BF16), preferred_element_type=F32
        ).astype(BF16)
        for t in range(2):
            for i in range(4):
                for st in range(2):
                    row = ((t * 4 + i) * 2 + st) * 16
                    new_lat_out[st, t, 2 * i + p] = y[row : row + 16]
    for c in stores:
        c.wait()


def shards(
    n_dec,
    n_row,
    hidden,
    head_weight,
    head_bias,
    lat_cache,
    mid_cache,
    moves,
    span_index,
    conv_in_weight,
    conv_in_bias,
    gn_gain,
    gn_bias,
    mid_weight,
    mid_bias,
):
    slots = n_dec * 2
    depth = hidden.shape[-1]
    vm = pl.BlockSpec(memory_space=pltpu.VMEM)
    sm = pl.BlockSpec(memory_space=pltpu.SMEM)
    hbm = pl.BlockSpec(memory_space=pl.ANY)
    dma = pltpu.SemaphoreType.DMA
    parts = pl.pallas_call(
        functools.partial(kernel, n_dec, n_row),
        out_shape=(
            jax.ShapeDtypeStruct((4, 2, 4, 32, 256), BF16),
            jax.ShapeDtypeStruct((2, 4, 16, 128), BF16),
            jax.ShapeDtypeStruct((2, 2, 4, 32, 256), BF16),
        ),
        in_specs=[hbm, vm, vm, vm, hbm, sm, sm, vm, vm, vm, vm, hbm, vm],
        out_specs=(hbm, hbm, hbm),
        scratch_shapes=[
            pltpu.VMEM((4, 2, 4, 32, 256), BF16),
            pltpu.VMEM((2, 4, 16, 128), BF16),
            pltpu.VMEM((2, 2, 4, 32, 256), BF16),
            pltpu.VMEM((2, 32, 128), BF16),
            pltpu.VMEM((256, depth), BF16),
            pltpu.VMEM((9, 1536, 256), BF16),
            pltpu.VMEM((2, 4, 16, 128), F32),
            pltpu.VMEM((2, 4, 16, 128), F32),
            pltpu.VMEM((2, 2, 2, 16, 128), F32),
            pltpu.VMEM((slots, 32, 128), BF16),
            pltpu.VMEM((4, 16, 128), F32),
            pltpu.VMEM((2, 16, 128), F32),
            pltpu.VMEM((27, CZ, 256), BF16),
            pltpu.VMEM((3, 1, 512), F32),
            pltpu.VMEM((4, 3, 256, 512), BF16),
            pltpu.VMEM((2, 6, 6, 16, 128), BF16),
            pltpu.VMEM((4, 4, 5, 16, 512), BF16),
            pltpu.VMEM((2, 8, 256), F32),
            pltpu.VMEM((2, n_row - 1, 8, 256), F32),
            pltpu.VMEM((slots, 4, 16, 256), BF16),
            pltpu.VMEM((slots, 4, 16, 256), BF16),
            pltpu.VMEM((slots, 4, 16, 256), BF16),
            pltpu.VMEM((slots, 4, 16, 256), BF16),
            pltpu.VMEM((4, 4, 32, 256), BF16),
            pltpu.VMEM((2, 10, 32, 512), BF16),
            pltpu.VMEM((2, 4, 6, 5, 16, 512), BF16),
            pltpu.VMEM((4, 4, 64, 256), F32),
            dma((12,)),
            dma((n_dec - 1,)),
            dma((n_dec - 1,)),
            dma((n_dec - 1, 4)),
            dma((n_dec - 1, 4)),
            dma((4, 4)),
            dma((4, 4)),
            dma((5,)),
            dma((5,)),
            dma((5,)),
            dma((5,)),
            dma((2,)),
            dma((2,)),
            dma((2, n_row - 1)),
            dma((2, n_row - 1)),
            dma((4, 3)),
            dma((4, 3)),
        ],
        compiler_params=pltpu.CompilerParams(
            collective_id=0, has_side_effects=True, vmem_limit_bytes=56 * 1024 * 1024
        ),
        cost_estimate=pl.CostEstimate(
            flops=9_000_000_000, bytes_accessed=12_000_000, transcendentals=700_000
        ),
    )(
        hidden.reshape(256, depth),
        head_weight.T,
        head_bias.reshape(1, 64),
        lat_cache,
        mid_cache,
        moves,
        span_index,
        conv_in_weight.reshape(27, CZ, 256),
        conv_in_bias.reshape(1, 256),
        gn_gain.reshape(1, 256),
        gn_bias.reshape(1, 256),
        mid_weight.reshape(9, 1536, 256),
        mid_bias.reshape(1, 256),
    )
    return pl.pallas_call(
        weave_kernel,
        out_shape=(
            jax.ShapeDtypeStruct((2, 4, 8, 16, 256), BF16),
            jax.ShapeDtypeStruct((2, 2, 8, 16, CZ), BF16),
            jax.ShapeDtypeStruct((2, 2, 8, 16, 256), BF16),
        ),
        in_specs=[hbm, hbm, hbm],
        out_specs=(hbm, vm, hbm),
        scratch_shapes=[
            pltpu.VMEM((4, 2, 4, 32, 256), BF16),
            pltpu.VMEM((2, 4, 16, 128), BF16),
            pltpu.VMEM((2, 2, 4, 32, 256), BF16),
            pltpu.VMEM((2, 4, 8, 16, 256), BF16),
            pltpu.VMEM((2, 2, 8, 16, 256), BF16),
            dma((11,)),
        ],
        compiler_params=pltpu.CompilerParams(vmem_limit_bytes=60 * 1024 * 1024),
        cost_estimate=pl.CostEstimate(flops=30_000_000, bytes_accessed=1_600_000, transcendentals=0),
    )(*parts)


def solution(mesh):
    placed = (
        P("dec", None, "row", None, "section"),
        P("section", None),
        P(),
        P("dec", None, "row", None, None),
        P("dec", None, "row", None, "section"),
        P(),
        P("dec"),
        P(None, None, None, None, "section"),
        P("section"),
        P("section"),
        P("section"),
        P(None, None, None, None, "section"),
        P("section"),
    )
    return jax.shard_map(
        functools.partial(shards, mesh.shape["dec"], mesh.shape["row"]),
        mesh=mesh,
        in_specs=placed,
        out_specs=(
            P("dec", None, "row", None, "section"),
            P("dec", None, "row", None, None),
            P("dec", None, "row", None, "section"),
        ),
        check_vma=False,
    )
```
